512 devices in a mesh: grp: 8 (over y), cent: 64 (over x, z, core).
Axes of the slice: x: 4, y: 8, z: 8, core: 2. Of those that a mesh axis runs over, the one named last changes fastest.
Arguments:
- vectors: bfloat16 [16384, 768], P(('grp', 'cent')), may hold values from -6 to 6
- centroids: bfloat16 [131072, 768], P('cent'), may hold values from -6 to 6
- postings: bfloat16 [256, 128, 768], P('cent'), may hold values from -6 to 6
- fill: int32 [256], P('cent'), may hold values from 32 to 64
- assign: int32 [16384], P(('grp', 'cent')), may hold values from 0 to 255, as said below
- split_posts: int32 [128], P('cent'), may hold values from -1 to 3, as said below
- split_members: int32 [128, 128], P('cent'), may hold values from 0 to 1
- neigh_post: int32 [32768], P(('grp', 'cent')), may hold values from 0 to 3
- neigh_row: int32 [32768], P(('grp', 'cent')), may hold values from 0 to 31
- neigh_split: int32 [32768], P(('grp', 'cent')), may hold values from 0 to 1, as said below
- neigh_dest: int32 [32768], P(('grp', 'cent')), may hold values from 0 to 63, as said below
Outputs:
- best_score: float32 [16384], P(('grp', 'cent'))
- postings_out: bfloat16 [256, 128, 768], P('cent')
- new_fill: int32 [256], P('cent')
- split_centers: float32 [128, 2, 768], P('cent')
- moved_rows: bfloat16 [65536, 768], P(('grp', 'cent'))
- moved_scores: bfloat16 [2, 65536], P(None, ('grp', 'cent'))
The draws below stay inside these ranges and needn't reach their ends.
Inputs may be any that keep to these rules, and one draw needn't show every extreme that they name: `assign`: global posting ids. Among one device's new vectors each centroid shard (id // 4) is named 0 or exactly 2 times; among those of the 8 devices that share a cent index it is named exactly 4 times; among those of the devices that share a grp index it is named exactly 32 times; every posting is named exactly 64 times in all. `split_posts`: each shard's block of 2 slots holds 1 to 2 distinct local postings first and -1 after them; some shard's block is full. `neigh_split`: names a slot of the device's centroid shard that holds a posting. `neigh_dest`: among one device's neighbor vectors each destination shard is named 0 or exactly 2 times.
All inputs are finite; a program needn't handle non-finite values.
Results may differ from the reference program's by a relative error of at most 0.0022.
Values may be sent and summed in bfloat16 or wider, within the bound.
No kernel may reach another device: no remote copies, remote signals or barrier semaphores. Data moves between devices by JAX's collectives and lax.ppermute only.
A program may use at most 64 MiB of HBM per device.

```python
import jax
import jax.numpy as jnp
from jax import lax

D = 768
ROWS = 128
ITERS = 2
SEND_CAP = 2
V_DEV = 32
C_DEV = 2048
P_DEV = 4
VECS = 16384
CENTS = 131072
POSTS = 256
GROUP_CAP = 4
APPENDS = 64
S_MAX = 2
SPLITS = 128
NB_DEV = 64
NEIGHS = 32768
MOVED = 65536
N_GRP = 8
N_CENT = 64


def live_counts(key):
    key = jax.random.fold_in(key, 5)
    counts = jax.random.randint(key, (N_CENT,), 1, S_MAX + 1)
    full_shard = jax.random.randint(jax.random.fold_in(key, 1), (), 0, N_CENT)
    return jnp.where(jnp.arange(N_CENT) == full_shard, S_MAX, counts).astype(jnp.int32)


def permutations(key, count, length):
    return jax.vmap(lambda single: jax.random.permutation(single, length))(jax.random.split(key, count)).astype(jnp.int32)


def draw_assign(key, part):
    key = jax.random.fold_in(key, 11)
    key_shard, key_post, key_shuffle = jax.random.split(key, 3)
    grp_ids = jnp.arange(N_GRP, dtype=jnp.int32)[:, None, None]
    cent_ids = jnp.arange(N_CENT, dtype=jnp.int32)[None, :, None]
    row_ids = jnp.arange(V_DEV, dtype=jnp.int32)[None, None, :]
    turn_ids = row_ids // 2 + V_DEV // 2 * grp_ids
    shard_perm = jax.random.permutation(key_shard, N_CENT).astype(jnp.int32)
    cent_full = jnp.broadcast_to(cent_ids, (N_GRP, N_CENT, V_DEV))
    turn_full = jnp.broadcast_to(turn_ids, (N_GRP, N_CENT, V_DEV))
    row_full = jnp.broadcast_to(row_ids, (N_GRP, N_CENT, V_DEV))
    dest_shard = shard_perm[(cent_full + turn_full) % N_CENT]
    occurrence = 2 * (turn_full // N_CENT) + row_full % 2
    post_perm = permutations(key_post, N_CENT, P_DEV)
    local_post = post_perm[dest_shard, (cent_full * GROUP_CAP + occurrence) % P_DEV]
    posting = dest_shard * P_DEV + local_post
    shuffle = permutations(key_shuffle, N_GRP * N_CENT, V_DEV).reshape(N_GRP, N_CENT, V_DEV)
    posting = jnp.take_along_axis(posting, shuffle, axis=2)
    return posting.reshape(-1).astype(jnp.int32)


def draw_split_posts(key, part):
    counts = live_counts(key)
    key = jax.random.fold_in(key, 13)
    chosen = permutations(key, N_CENT, P_DEV)[:, :S_MAX]
    slot_ids = jnp.arange(S_MAX, dtype=jnp.int32)
    return jnp.where(slot_ids[None, :] < counts[:, None], chosen, -1).reshape(-1).astype(jnp.int32)


def draw_neigh_split(key, part):
    counts = live_counts(key)
    key = jax.random.fold_in(key, 17)
    raw_slot = jax.random.randint(key, (N_GRP, N_CENT, NB_DEV), 0, S_MAX)
    return (raw_slot % counts[None, :, None]).reshape(-1).astype(jnp.int32)


def draw_neigh_dest(key, part):
    key = jax.random.fold_in(key, 19)
    key_dest, key_shuffle = jax.random.split(key)
    dest_perm = permutations(key_dest, N_GRP * N_CENT, N_CENT)
    half_ids = jnp.arange(NB_DEV, dtype=jnp.int32) // 2
    targets = dest_perm[:, half_ids]
    shuffle = permutations(key_shuffle, N_GRP * N_CENT, NB_DEV)
    return jnp.take_along_axis(targets, shuffle, axis=1).reshape(-1).astype(jnp.int32)


def place_ends(array, own_key, smallest, high):
    longest = array.shape.index(max(array.shape))
    spots = []
    for shift in (0, 1):
        where = [jax.random.randint(jax.random.fold_in(own_key, axis), (), 0, length) for axis, length in enumerate(array.shape)]
        where[longest] = (where[longest] + shift) % array.shape[longest]
        spots.append(tuple(where))
    return array.at[spots[0]].set(smallest).at[spots[1]].set(high)


def block_scale(key, shape, cuts, smallest, top_value):
    loudness = 1.0
    for axis_at, shards_of in cuts:
        heights = jax.random.uniform(jax.random.fold_in(jax.random.fold_in(key, 6), axis_at), (shards_of,), jnp.float32, smallest / len(cuts), top_value / len(cuts))
        loudness = loudness * jnp.repeat(jnp.exp(heights), shape[axis_at] // shards_of).reshape((-1,) + (1,) * (len(shape) - 1 - axis_at))
    return loudness


def normal_values(stream_key, dims, scale, reach, shards=(), kind=jnp.bfloat16):
    result = scale * jax.random.normal(stream_key, dims, jnp.float32)
    if shards:
        result = result * block_scale(stream_key, dims, shards, -0.22, 0.18)
    return jnp.clip(result, -reach, reach).astype(kind)


def setup_inputs(seed: int = 0) -> dict:
    seeds = jax.random.split(jax.random.key(seed), 12)
    vectors = normal_values(seeds[0], (VECS, D), 1.0, 6.0, ((0, 512),))
    centroids = normal_values(seeds[1], (CENTS, D), 1.0, 6.0, ((0, 64),))
    postings = normal_values(seeds[2], (POSTS, ROWS, D), 1.0, 6.0, ((0, 64),))
    fill = place_ends(jax.random.randint(seeds[3], (POSTS,), 32, ROWS - APPENDS + 1), jax.random.fold_in(seeds[3], 1), 32, ROWS - APPENDS).astype(jnp.int32)
    assign = draw_assign(jax.random.fold_in(seeds[11], 71), 0)
    split_posts = draw_split_posts(jax.random.fold_in(seeds[11], 71), 0)
    split_members = place_ends(jax.random.randint(seeds[6], (SPLITS, ROWS), 0, 2), jax.random.fold_in(seeds[6], 1), 0, 1).astype(jnp.int32)
    neigh_post = place_ends(jax.random.randint(seeds[7], (NEIGHS,), 0, P_DEV), jax.random.fold_in(seeds[7], 1), 0, P_DEV - 1).astype(jnp.int32)
    neigh_row = place_ends(jax.random.randint(seeds[8], (NEIGHS,), 0, 32), jax.random.fold_in(seeds[8], 1), 0, 31).astype(jnp.int32)
    neigh_split = draw_neigh_split(jax.random.fold_in(seeds[11], 71), 0)
    neigh_dest = draw_neigh_dest(jax.random.fold_in(seeds[11], 71), 0)
    return dict(vectors=vectors, centroids=centroids, postings=postings, fill=fill, assign=assign, split_posts=split_posts, split_members=split_members, neigh_post=neigh_post, neigh_row=neigh_row, neigh_split=neigh_split, neigh_dest=neigh_dest)


def center_update(rows_f, row_mask, weights, prior):
    first = row_mask * weights
    second = row_mask * (1.0 - weights)
    both = jnp.stack([first, second])
    sums = jnp.dot(both, rows_f, precision=lax.Precision.HIGHEST)
    totals = jnp.sum(both, axis=1)
    return (sums + prior[None, :]) / (totals[:, None] + 1.0)


def two_means(rows_f, count, members, prior):
    row_mask = (jnp.arange(rows_f.shape[0], dtype=jnp.int32) < count).astype(rows_f.dtype)
    weights = members.astype(rows_f.dtype)
    centers = center_update(rows_f, row_mask, weights, prior)
    for turn in range(ITERS):
        far_two = jnp.sum(jnp.square(rows_f - centers[1][None, :]), axis=1)
        far_one = jnp.sum(jnp.square(rows_f - centers[0][None, :]), axis=1)
        weights = jax.nn.sigmoid(0.125 * (far_two - far_one))
        centers = center_update(rows_f, row_mask, weights, prior)
    return centers


def reference(vectors, centroids, postings, fill, assign, split_posts, split_members, neigh_post, neigh_row, neigh_split, neigh_dest):
    blocks = centroids.reshape(-1, 256, D)

    def scan_step(running, block):
        scores = lax.dot_general(vectors, block, (((1,), (1,)), ((), ())), preferred_element_type=jnp.float32)
        return jnp.maximum(running, jnp.max(scores, axis=1)), None

    best_score = lax.scan(scan_step, jnp.full((VECS,), -jnp.inf, jnp.float32), blocks)[0]

    order = jnp.argsort(assign, stable=True).astype(jnp.int32)
    sorted_posts = assign[order]
    first_place = jnp.searchsorted(sorted_posts, sorted_posts, side="left").astype(jnp.int32)
    rank_sorted = jnp.arange(VECS, dtype=jnp.int32) - first_place
    vec_rank = jnp.zeros((VECS,), jnp.int32).at[order].set(rank_sorted)
    row_place = fill[assign] + vec_rank
    postings_out = postings.at[assign, row_place].set(vectors)
    new_fill = fill + jax.ops.segment_sum(jnp.ones((VECS,), jnp.int32), assign, POSTS).astype(jnp.int32)

    shard_of = jnp.arange(SPLITS, dtype=jnp.int32) // S_MAX
    local_post = jnp.maximum(split_posts, 0)
    post_index = shard_of * P_DEV + local_post
    cent_index = shard_of * C_DEV + local_post
    live_slot = (split_posts >= 0).astype(jnp.float32)

    def split_one(post_id, cent_id, members, alive):
        rows_f = postings_out[post_id].astype(jnp.float32)
        prior = centroids[cent_id].astype(jnp.float32)
        return two_means(rows_f, new_fill[post_id], members, prior) * alive

    split_centers = jax.vmap(split_one)(post_index, cent_index, split_members, live_slot)

    device_of = jnp.arange(NEIGHS, dtype=jnp.int32) // NB_DEV
    grp_of = device_of // N_CENT
    cent_of = device_of % N_CENT
    flat_rows = postings_out.reshape(POSTS * ROWS, D)
    picked = flat_rows[(cent_of * P_DEV + neigh_post) * ROWS + neigh_row]
    chosen = split_centers[cent_of * S_MAX + neigh_split]
    scores = jnp.einsum("nkd,nd->nk", chosen, picked.astype(jnp.float32), precision=lax.Precision.HIGHEST).astype(jnp.bfloat16)
    dest_grid = neigh_dest.reshape(N_GRP * N_CENT, NB_DEV)
    index_grid = jnp.arange(NB_DEV, dtype=jnp.int32)
    earlier = (dest_grid[:, :, None] == dest_grid[:, None, :]) & (index_grid[None, None, :] < index_grid[None, :, None])
    slot_rank = jnp.sum(earlier.astype(jnp.int32), axis=2).reshape(NEIGHS)
    out_row = ((grp_of * N_CENT + neigh_dest) * N_CENT + cent_of) * SEND_CAP + slot_rank
    moved_rows = jnp.zeros((MOVED, D), jnp.bfloat16).at[out_row].set(picked)
    moved_scores = jnp.zeros((2, MOVED), jnp.bfloat16).at[:, out_row].set(scores.T)
    return best_score, postings_out, new_fill, split_centers, moved_rows, moved_scores
```

```python
import functools

import jax
import jax.numpy as jnp
from jax import lax
from jax.experimental import pallas as pl
from jax.experimental.pallas import tpu as pltpu
from jax.sharding import Mesh, PartitionSpec as P

D = 768
W = 896
ROWS = 128
HEAD = 32
ITERS = 2
NX, NY, NZ, NK = 4, 8, 8, 2
NC = NX * NZ * NK
V = 32
NB = 64
POSTS = 4
CENT = ("x", "z", "core")
LOW = -3.0e38
F32 = jnp.float32
BF = jnp.bfloat16
I32 = jnp.int32
VMEM_BYTES = 40 * 1024 * 1024


def iota(shape, dim):
    return lax.broadcasted_iota(I32, shape, dim)


def as_column(row):
    n = row.shape[1]
    eye = iota((n, n), 0) == iota((n, n), 1)
    return jnp.sum(jnp.where(eye, jnp.broadcast_to(row, (n, n)), 0), axis=1, keepdims=True)


def earlier_equal(row):
    n = row.shape[1]
    same = (as_column(row) == row) & (iota((n, n), 0) < iota((n, n), 1))
    return jnp.sum(same.astype(I32), axis=0, keepdims=True)


def one_hot(mask):
    return jnp.where(mask, 1.0, 0.0).astype(BF)


def dot(a, b):
    return jnp.dot(a, b, preferred_element_type=F32)


def dot_nt(a, b):
    return lax.dot_general(a, b, (((1,), (1,)), ((), ())), preferred_element_type=F32)


def pack_kernel(vec_ref, head_ref, assign_ref, npost_ref, nrow_ref, ndest_ref, out_ref):
    assign = assign_ref[...]
    dest = assign // POSTS
    place = earlier_equal(dest)
    slot = iota((NC * 8, V), 0)
    to, r = slot // 8, slot % 8
    col = iota((NC * 8, V), 1)
    share = (r < 4) & (col == ((to // (NZ * NK)) * NK + to % NK) * 4 + r)
    route = (dest == to) & (place == r - 4) & (r >= 4) & (r < 6)
    ndest = ndest_ref[...]
    nplace = earlier_equal(ndest)
    nslot = iota((NC * 8, NB), 0)
    chosen = one_hot((ndest == nslot // 8) & (nplace == nslot % 8 - 6) & (nslot % 8 >= 6))
    where_row = npost_ref[...] * HEAD + nrow_ref[...]
    picks = one_hot(where_row == iota((POSTS * HEAD, NB), 0))
    table = dot_nt(chosen, picks).astype(BF)
    head = head_ref[...].reshape(POSTS * HEAD, D)
    out_ref[:, :D] = (dot(one_hot(share | route), vec_ref[...]) + dot(table, head)).astype(BF)
    post = as_column(assign) % POSTS + 1
    mark = jnp.where(iota((V, 128), 1) == 0, post, 0).astype(F32).astype(BF)
    out_ref[:, D:] = dot(one_hot(route), mark).astype(BF)


def unpack_kernel(in_ref, share_ref, moved_ref, spread_ref):
    n = NC * 8
    p = iota((NC * 4, n), 1)
    i = iota((NC * 4, n), 0)
    rows = in_ref[:, :D]
    share_ref[...] = dot(one_hot(p == (i // 4) * 8 + i % 4), rows).astype(BF)
    p2, i2 = p[: NC * 2], i[: NC * 2]
    moved_ref[...] = dot(one_hot(p2 == (i2 // 2) * 8 + 6 + i2 % 2), rows).astype(BF)
    mark = dot_nt(one_hot(iota((8, 128), 1) == 0), in_ref[:, D:])
    upper = one_hot(iota((n, n), 0) < iota((n, n), 1))
    rank = dot(one_hot(mark > 0.5), upper)
    hit = (mark[:1] > 0.5) & (rank[:1].astype(I32) == iota((V, n), 0))
    compact = dot(one_hot(hit), in_ref[...]).astype(BF)
    for g in range(NY):
        spread_ref[g] = compact


def append_kernel(
    fill_ref, split_ref, got_ref, post_ref, prior_ref, member_ref, npost_ref, nrow_ref, nsplit_ref,
    ndest_ref, out_ref, count_ref, centers_ref, score_ref,
):
    n = NY * V
    mark = dot_nt(one_hot(iota((8, 128), 1) == 0), got_ref[:, D:]).astype(I32)
    match = mark == iota((8, n), 0) + 1
    upper = one_hot(iota((n, n), 0) < iota((n, n), 1))
    rank = dot(one_hot(match), upper).astype(I32)
    row = iota((ROWS, n), 0)
    line = iota((ROWS, 1), 0)
    got = got_ref[:, :D]
    for q in range(POSTS):
        mine = match[q : q + 1]
        count = jnp.sum(mine.astype(I32))
        first = fill_ref[q]
        table = one_hot(mine & (row == first + rank[q : q + 1]))
        written = dot(table, got)
        hit = (line >= first) & (line < first + count)
        out_ref[q] = jnp.where(hit, written, post_ref[q].astype(F32)).astype(BF)
        count_ref[q] = first + count

    head = post_ref[:, :HEAD, :].reshape(POSTS * HEAD, D).astype(F32)
    members = member_ref[...].astype(F32)
    eye = iota((ROWS, ROWS), 0) == iota((ROWS, ROWS), 1)
    lane = iota((POSTS * HEAD, 128), 1)
    ndest = ndest_ref[...]
    nplace = earlier_equal(ndest)
    nsplit = nsplit_ref[...]
    picks = one_hot(npost_ref[...] * HEAD + nrow_ref[...] == iota((POSTS * HEAD, NB), 0))
    to = iota((NC, NB), 0)
    sent = jnp.zeros((NC, 128), F32)
    for s in range(2):
        j = split_ref[s]
        alive = jnp.where(j >= 0, 1.0, 0.0).astype(F32)
        q = jnp.maximum(j, 0)
        x = out_ref[q].astype(F32)
        own = prior_ref[...].astype(F32)
        prior = jnp.sum(jnp.where(iota(own.shape, 0) == q, own, 0.0), axis=0, keepdims=True)
        mask = jnp.where(line < count_ref[q], 1.0, 0.0).astype(F32)
        weights = jnp.sum(jnp.where(eye, members[s : s + 1], 0.0), axis=1, keepdims=True)

        def update(weights):
            w1, w2 = mask * weights, mask * (1.0 - weights)
            s1 = jnp.sum(w1 * x, axis=0, keepdims=True) + prior
            s2 = jnp.sum(w2 * x, axis=0, keepdims=True) + prior
            t1 = jnp.sum(w1, axis=0, keepdims=True) + 1.0
            t2 = jnp.sum(w2, axis=0, keepdims=True) + 1.0
            return s1 / t1, s2 / t2

        a1, a2 = update(weights)
        for _ in range(ITERS):
            far = jnp.sum(jnp.square(x - a2), axis=1, keepdims=True) - jnp.sum(
                jnp.square(x - a1), axis=1, keepdims=True
            )
            a1, a2 = update(jax.nn.sigmoid(0.125 * far))
        a1, a2 = a1 * alive, a2 * alive
        centers_ref[s, 0:1, :] = a1
        centers_ref[s, 1:2, :] = a2
        c1 = jnp.sum(head * a1, axis=1, keepdims=True)
        c2 = jnp.sum(head * a2, axis=1, keepdims=True)
        for t in range(2):
            where_to = one_hot((ndest == to) & (nplace == t) & (nsplit == s))
            table = dot_nt(where_to, picks).astype(BF)
            values = jnp.where(lane == 32 + 2 * t, c1, jnp.where(lane == 33 + 2 * t, c2, 0.0))
            sent = sent + dot(table, values.astype(BF))
    score_ref[...] = sent


BLOCK = 1024
STEPS = 2048 // BLOCK


def best_kernel(place_ref, own_ref, mate_ref, v0_ref, v1_ref, v2_ref, v3_ref, score_ref, out_ref, acc_ref):
    step = pl.program_id(0)
    parts = (v0_ref, v1_ref, v2_ref, v3_ref)

    @pl.when(step == 0)
    def _():
        acc_ref[...] = jnp.full(acc_ref.shape, LOW, F32)

    def scan(block_ref):
        for a, part in enumerate(parts):
            scores = dot_nt(block_ref[...], part[...])
            top = jnp.max(scores.reshape(BLOCK // 8, 8, NC * 4), axis=0)
            acc_ref[a] = jnp.maximum(acc_ref[a], top)

    @pl.when(step < STEPS)
    def _():
        scan(own_ref)

    @pl.when(step >= STEPS)
    def _():
        scan(mate_ref)

    @pl.when(step == 2 * STEPS - 1)
    def _():
        x, core = place_ref[0], place_ref[1]
        wide = (NC, NC * 4)
        mine = iota(wide, 1) // 4 == iota(wide, 0)
        lane = iota((NC, 128), 1)
        best = jnp.full((NC, 128), LOW, F32)
        for a in range(NX):
            top = jnp.max(acc_ref[a], axis=0, keepdims=True)
            spread = jnp.where(mine, jnp.broadcast_to(top, wide), LOW)
            folded = jnp.maximum(spread[:, :128], spread[:, 128:])
            for shift in (64, 32, 16, 8, 4):
                folded = jnp.maximum(folded, pltpu.roll(folded, shift, 1))
            group = lax.rem(x + NX - a, NX) * NK + core
            best = jnp.where(lane // 4 == group, folded, best)
        out_ref[...] = jnp.where(lane < V, best, score_ref[...])


def final_kernel(in_ref, best_ref, score_ref):
    got = in_ref[...]
    best_ref[...] = jnp.max(got, axis=0, keepdims=True)[:, :V]
    lane = iota((NC, 128), 1)
    src = iota((NC, 128), 0)
    vals = jnp.where((lane >= 32) & (lane < 36), got, 0.0).astype(BF)
    total = jnp.zeros((8, 128), F32)
    pick = iota((8, 128), 0)
    at = iota((8, 128), 1)
    for t in range(2):
        chosen = one_hot(at == 32 + 2 * t + pick)
        rows = dot_nt(chosen, vals).astype(BF)
        total = total + dot(rows, one_hot(lane == src * 2 + t))
    score_ref[...] = total[:2].astype(BF)


def vm():
    return pl.BlockSpec(memory_space=pltpu.VMEM)


def sm():
    return pl.BlockSpec(memory_space=pltpu.SMEM)


def params(**kw):
    return pltpu.CompilerParams(vmem_limit_bytes=VMEM_BYTES, **kw)


def shards(
    vectors,
    centroids,
    postings,
    fill,
    assign,
    split_posts,
    split_members,
    neigh_post,
    neigh_row,
    neigh_split,
    neigh_dest,
):
    place = jnp.stack([lax.axis_index("x"), lax.axis_index("core")]).astype(I32)
    npost, nrow, nsplit, ndest = (
        a.reshape(1, NB) for a in (neigh_post, neigh_row, neigh_split, neigh_dest)
    )
    mate = lax.ppermute(centroids, "core", [(0, 1), (1, 0)])
    one = lambda *shape: pl.BlockSpec(shape, lambda i: (0,) * len(shape))
    packed = pl.pallas_call(
        pack_kernel,
        out_shape=jax.ShapeDtypeStruct((NC * 8, W), BF),
        grid=(1,),
        in_specs=[one(V, D), one(POSTS, HEAD, D), one(1, V), one(1, NB), one(1, NB), one(1, NB)],
        out_specs=one(NC * 8, W),
        compiler_params=params(),
        name="pack_rows",
    )(vectors, postings, assign.reshape(1, V), npost, nrow, ndest)
    got = lax.all_to_all(packed.reshape(NC, 8, W), CENT, 0, 0, tiled=True).reshape(NC * 8, W)
    share, moved_rows, spread = pl.pallas_call(
        unpack_kernel,
        out_shape=(
            jax.ShapeDtypeStruct((NC * 4, D), BF),
            jax.ShapeDtypeStruct((NC * 2, D), BF),
            jax.ShapeDtypeStruct((NY, V, W), BF),
        ),
        in_specs=[vm()],
        out_specs=(vm(), vm(), vm()),
        compiler_params=params(),
        name="unpack_rows",
    )(got)
    parts = [share] + [
        lax.ppermute(share, "x", [(i, (i + a) % NX) for i in range(NX)]) for a in range(1, NX)
    ]
    gathered = lax.all_to_all(spread, "y", 0, 0, tiled=True).reshape(NY * V, W)
    postings_out, new_fill, split_centers, scores = pl.pallas_call(
        append_kernel,
        out_shape=(
            jax.ShapeDtypeStruct((POSTS, ROWS, D), BF),
            jax.ShapeDtypeStruct((POSTS,), I32),
            jax.ShapeDtypeStruct((2, 2, D), F32),
            jax.ShapeDtypeStruct((NC, 128), F32),
        ),
        grid=(1,),
        in_specs=[
            sm(), sm(), one(NY * V, W), one(POSTS, ROWS, D), one(16, D), one(2, ROWS),
            one(1, NB), one(1, NB), one(1, NB), one(1, NB),
        ],
        out_specs=(one(POSTS, ROWS, D), sm(), one(2, 2, D), one(NC, 128)),
        compiler_params=params(),
        name="append_split",
    )(fill, split_posts, gathered, postings, centroids, split_members, npost, nrow, nsplit, ndest)
    whole = one(NC * 4, D)
    sending = pl.pallas_call(
        best_kernel,
        out_shape=jax.ShapeDtypeStruct((NC, 128), F32),
        grid=(2 * STEPS,),
        in_specs=[
            sm(),
            pl.BlockSpec((BLOCK, D), lambda i: (jnp.minimum(i, STEPS - 1), 0)),
            pl.BlockSpec((BLOCK, D), lambda i: (jnp.maximum(i - STEPS, 0), 0)),
            whole, whole, whole, whole,
            one(NC, 128),
        ],
        out_specs=one(NC, 128),
        scratch_shapes=[pltpu.VMEM((NX, 8, NC * 4), F32)],
        compiler_params=params(),
        name="best_scores",
    )(place, centroids, mate, *parts, scores)
    back = lax.all_to_all(sending.reshape(NC, 1, 128), CENT, 0, 0, tiled=True).reshape(NC, 128)
    best_score, moved_scores = pl.pallas_call(
        final_kernel,
        out_shape=(jax.ShapeDtypeStruct((1, V), F32), jax.ShapeDtypeStruct((2, 2 * NC), BF)),
        in_specs=[vm()],
        out_specs=(vm(), vm()),
        compiler_params=params(),
        name="last_step",
    )(back)
    return (
        best_score.reshape(V), postings_out, new_fill, split_centers, moved_rows, moved_scores
    )


def solution(mesh):
    fine = Mesh(mesh.devices.reshape(NY, NX, NZ, NK), ("y", "x", "z", "core"))
    both = ("y",) + CENT
    return jax.shard_map(
        shards,
        mesh=fine,
        in_specs=(
            P(both, None),
            P(CENT, None),
            P(CENT, None, None),
            P(CENT),
            P(both),
            P(CENT),
            P(CENT, None),
            P(both),
            P(both),
            P(both),
            P(both),
        ),
        out_specs=(
            P(both),
            P(CENT, None, None),
            P(CENT),
            P(CENT, None, None),
            P(both, None),
            P(None, both),
        ),
        check_vma=False,
    )
```

```python
import functools

import jax
import jax.numpy as jnp
from jax import lax
from jax.experimental import pallas as pl
from jax.experimental.pallas import tpu as pltpu
from jax.sharding import Mesh, PartitionSpec as P

D = 768
W = 896
ROWS = 128
HEAD = 32
ITERS = 2
NX, NY, NZ, NK = 4, 8, 8, 2
NC = NX * NZ * NK
V = 32
NB = 64
POSTS = 4
CENT = ("x", "z", "core")
LOW = -3.0e38
HALF = D // 2
P8 = HALF + 256
F32 = jnp.float32
BF = jnp.bfloat16
I32 = jnp.int32
MIB = 1024 * 1024


def iota(shape, dim):
    return lax.broadcasted_iota(I32, shape, dim)


def as_column(row):
    n = row.shape[1]
    eye = iota((n, n), 0) == iota((n, n), 1)
    return jnp.sum(jnp.where(eye, jnp.broadcast_to(row, (n, n)), 0), axis=1, keepdims=True)


def earlier_equal(row):
    n = row.shape[1]
    same = (as_column(row) == row) & (iota((n, n), 0) < iota((n, n), 1))
    return jnp.sum(same.astype(I32), axis=0, keepdims=True)


def one_hot(mask):
    return jnp.where(mask, 1.0, 0.0).astype(BF)


def dot(a, b):
    return jnp.dot(a, b, preferred_element_type=F32)


def dot_nt(a, b):
    return lax.dot_general(a, b, (((1,), (1,)), ((), ())), preferred_element_type=F32)


def pack_kernel(vec_ref, head_ref, assign_ref, npost_ref, nrow_ref, ndest_ref, out_ref, table_ref):
    n = NC * 8
    assign = assign_ref[...]
    dest = assign // POSTS
    zdest = (dest // NK) % NZ
    place = earlier_equal(dest)

    ones = jnp.ones((V, 128), BF)

    def routed(count, per):
        p = iota((count, V), 0)
        to, t = p // per, p % 4
        return (dest == to) & (place == t), (zdest != (to // NK) % NZ)

    named, other = routed(n, 8)
    small, _ = routed(NC * 4, 4)
    free = (1.0 - dot(one_hot(small), ones)).astype(BF)
    p, c = iota((n, NC * 4), 0), iota((n, NC * 4), 1)
    pd, cd = p // 8, c // 4
    slot = ((pd // (NZ * NK)) * NK + pd % NK) * 4 + p % 4
    cslot = ((cd // (NZ * NK)) * NK + cd % NK) * 4 + c % 4
    before = one_hot(((pd // NK) % NZ == (cd // NK) % NZ) & (cslot < slot))
    free_rank = dot(before, free)[:, :V]
    upper = one_hot(iota((V, V), 0) < iota((V, V), 1))
    rest_rank = dot(one_hot(other), upper)
    taken = dot(one_hot(named), ones)[:, :V]
    share = named | (other & (taken < 0.5) & (free_rank == rest_rank))
    low_half = iota((n, V), 0) % 8 < 4
    table = one_hot(share & low_half)
    table_ref[:, :V] = table
    out_ref[:, :HALF] = (
        dot(table, vec_ref[:, :HALF]) + dot(one_hot(share & ~low_half), vec_ref[:, HALF:])
    ).astype(BF)

    ndest = ndest_ref[...]
    nplace = earlier_equal(ndest)
    picks = one_hot(npost_ref[...] * HEAD + nrow_ref[...] == iota((POSTS * HEAD, NB), 0))
    head = head_ref[...].reshape(POSTS * HEAD, D)
    p, c = iota((n, 6 * NC), 0), iota((n, 6 * NC), 1)
    spread = one_hot((p // 8 == c % NC) & (p % 8 == c // NC))
    post = as_column(assign) % POSTS + 1
    mark = jnp.where(iota((V, 128), 1) == as_column(place), post, 0).astype(F32).astype(BF)
    sixth = one_hot((iota((n, V), 0) // 8 == dest) & (iota((n, V), 0) % 8 == 6))
    for t in range(2):
        chosen = one_hot((ndest == iota((NC, NB), 0)) & (nplace == t))
        rows = dot(dot_nt(chosen, picks).astype(BF), head).astype(BF)
        stack = jnp.concatenate([rows[:, 128 * k : 128 * k + 128] for k in range(6)], axis=0)
        tile = dot(spread, stack)
        if t == 0:
            tile = tile + dot(sixth, mark)
        out_ref[:, HALF + 128 * t : HALF + 128 * t + 128] = tile.astype(BF)


def share_kernel(in_ref, share_ref):
    n = NC * 8
    p, i = iota((NC * 4, n), 1), iota((NC * 4, n), 0)
    first = (i // 4) * 8 + i % 4
    rows = in_ref[:, :HALF]
    share_ref[:, :HALF] = dot(one_hot(p == first), rows).astype(BF)
    share_ref[:, HALF:] = dot(one_hot(p == first + 4), rows).astype(BF)


def moved_kernel(in_ref, moved_ref):
    n = NC * 8
    tiles = in_ref[:, HALF:]
    p, i = iota((NC * 2, n), 1), iota((NC * 2, n), 0)
    odd = iota((NC * 2, 128), 0) % 2 == 1
    for k in range(6):
        both = dot(one_hot(p == (i // 2) * 8 + k), tiles)
        moved_ref[:, 128 * k : 128 * k + 128] = jnp.where(odd, both[:, 128:], both[:, :128]).astype(BF)


def spread_kernel(in_ref, share_ref, out_ref, buf_ref, sems):
    n = NC * 8
    p, d = iota((NC, n), 1), iota((NC, n), 0)
    marks = dot(one_hot(p == d * 8 + 6), in_ref[:, HALF : HALF + 128]).astype(BF)
    first = dot_nt(one_hot(iota((8, 128), 1) == 0), marks)
    upper = one_hot(iota((NC, NC), 0) < iota((NC, NC), 1))
    valid = one_hot(first > 0.5)
    rank = dot(valid, upper).astype(BF)
    m = NC * 4
    widen = one_hot(iota((NC, m), 0) == iota((NC, m), 1) // 4)
    valid, rank = dot(valid, widen)[:1], dot(rank, widen)[:1].astype(I32)
    t = iota((V, m), 1) % 4
    hit = one_hot((valid > 0.5) & (t < 2) & (2 * rank + t == iota((V, m), 0)))
    tall = one_hot(iota((m, NC), 1) == iota((m, NC), 0) // 4)
    lane = iota((m, 128), 1)
    mine = jnp.where(lane == iota((m, 128), 0) % 4, dot(tall, marks), 0.0)
    post = jnp.sum(mine, axis=1, keepdims=True)
    buf_ref[:, :D] = dot(hit, share_ref[...]).astype(BF)
    buf_ref[:, D:] = dot(hit, jnp.where(lane == 0, post, 0.0).astype(BF)).astype(BF)
    copies = [pltpu.make_async_copy(buf_ref, out_ref.at[g], sems.at[g]) for g in range(NY)]
    for copy in copies:
        copy.start()
    for copy in copies:
        copy.wait()


def append_kernel(
    fill_ref, split_ref, got_ref, post_ref, prior_ref, member_ref, npost_ref, nrow_ref, nsplit_ref,
    ndest_ref, best_ref, out_ref, count_ref, centers_ref, send_ref,
):
    n = NY * V
    mark = dot_nt(one_hot(iota((8, 128), 1) == 0), got_ref[:, D:]).astype(I32)
    match = mark == iota((8, n), 0) + 1
    upper = one_hot(iota((n, n), 0) < iota((n, n), 1))
    rank = dot(one_hot(match), upper).astype(I32)
    row = iota((ROWS, n), 0)
    line = iota((ROWS, 1), 0)
    got = got_ref[:, :D]
    for q in range(POSTS):
        mine = match[q : q + 1]
        count = jnp.sum(mine.astype(I32))
        first = fill_ref[q]
        table = one_hot(mine & (row == first + rank[q : q + 1]))
        written = dot(table, got)
        hit = (line >= first) & (line < first + count)
        out_ref[q] = jnp.where(hit, written, post_ref[q].astype(F32)).astype(BF)
        count_ref[q] = first + count

    head = post_ref[:, :HEAD, :].reshape(POSTS * HEAD, D).astype(F32)
    members = member_ref[...].astype(F32)
    eye = iota((ROWS, ROWS), 0) == iota((ROWS, ROWS), 1)
    lane = iota((POSTS * HEAD, 128), 1)
    ndest = ndest_ref[...]
    nplace = earlier_equal(ndest)
    nsplit = nsplit_ref[...]
    picks = one_hot(npost_ref[...] * HEAD + nrow_ref[...] == iota((POSTS * HEAD, NB), 0))
    to = iota((NC, NB), 0)
    sent = jnp.zeros((NC, 128), F32)
    for s in range(2):
        j = split_ref[s]
        alive = jnp.where(j >= 0, 1.0, 0.0).astype(F32)
        q = jnp.maximum(j, 0)
        x = out_ref[q].astype(F32)
        own = prior_ref[...].astype(F32)
        prior = jnp.sum(jnp.where(iota(own.shape, 0) == q, own, 0.0), axis=0, keepdims=True)
        mask = jnp.where(line < count_ref[q], 1.0, 0.0).astype(F32)
        weights = jnp.sum(jnp.where(eye, members[s : s + 1], 0.0), axis=1, keepdims=True)

        def update(weights):
            w1, w2 = mask * weights, mask * (1.0 - weights)
            s1 = jnp.sum(w1 * x, axis=0, keepdims=True) + prior
            s2 = jnp.sum(w2 * x, axis=0, keepdims=True) + prior
            t1 = jnp.sum(w1, axis=0, keepdims=True) + 1.0
            t2 = jnp.sum(w2, axis=0, keepdims=True) + 1.0
            return s1 / t1, s2 / t2

        a1, a2 = update(weights)
        for _ in range(ITERS):
            far = jnp.sum(jnp.square(x - a2), axis=1, keepdims=True) - jnp.sum(
                jnp.square(x - a1), axis=1, keepdims=True
            )
            a1, a2 = update(jax.nn.sigmoid(0.125 * far))
        a1, a2 = a1 * alive, a2 * alive
        centers_ref[s, 0:1, :] = a1
        centers_ref[s, 1:2, :] = a2
        c1 = jnp.sum(head * a1, axis=1, keepdims=True)
        c2 = jnp.sum(head * a2, axis=1, keepdims=True)
        for t in range(2):
            where_to = one_hot((ndest == to) & (nplace == t) & (nsplit == s))
            table = dot_nt(where_to, picks).astype(BF)
            values = jnp.where(lane == 32 + 2 * t, c1, jnp.where(lane == 33 + 2 * t, c2, 0.0))
            sent = sent + dot(table, values.astype(BF))
    send_ref[...] = jnp.where(iota((NC, 128), 1) < V, best_ref[...], sent)


BLOCK = 1024


def scan_blocks(ref, part, best):
    for i in range(2048 // BLOCK):
        scores = dot_nt(ref[BLOCK * i : BLOCK * i + BLOCK, :], part)
        best = jnp.maximum(best, jnp.max(scores.reshape(BLOCK // 8, 8, NC * 4), axis=0))
    return best


def first_kernel(own_ref, mate_ref, v_ref, acc_ref, buf_ref, sem):
    copy = pltpu.make_async_copy(mate_ref, buf_ref, sem)
    copy.start()
    best = scan_blocks(own_ref, v_ref[...], jnp.full((8, NC * 4), LOW, F32))
    copy.wait()
    acc_ref[0] = scan_blocks(buf_ref, v_ref[...], best)


def best_kernel(
    place_ref, own_ref, mate_ref, v1_ref, v2_ref, v3_ref, acc0_ref, out_ref, acc_ref, part_ref, buf_ref, sems
):
    copies = [
        pltpu.make_async_copy(v, part_ref.at[a], sems.at[a])
        for a, v in enumerate((v1_ref, v2_ref, v3_ref))
    ] + [pltpu.make_async_copy(mate_ref, buf_ref, sems.at[NX - 1])]
    for copy in copies:
        copy.start()
    for a in range(NX - 1):
        copies[a].wait()
        acc_ref[a] = scan_blocks(own_ref, part_ref[a], jnp.full((8, NC * 4), LOW, F32))
    copies[NX - 1].wait()
    for a in range(NX - 1):
        acc_ref[a] = scan_blocks(buf_ref, part_ref[a], acc_ref[a])
    x, core = place_ref[0], place_ref[1]
    wide = (NC, NC * 4)
    mine = iota(wide, 1) // 4 == iota(wide, 0)
    lane = iota((NC, 128), 1)
    best = jnp.full((NC, 128), LOW, F32)
    for a in range(NX):
        acc = acc0_ref[0] if a == 0 else acc_ref[a - 1]
        top = jnp.max(acc, axis=0, keepdims=True)
        spread = jnp.where(mine, jnp.broadcast_to(top, wide), LOW)
        folded = jnp.maximum(spread[:, :128], spread[:, 128:])
        for shift in (64, 32, 16, 8, 4):
            folded = jnp.maximum(folded, pltpu.roll(folded, shift, 1))
        group = lax.rem(x + NX - a, NX) * NK + core
        best = jnp.where(lane // 4 == group, folded, best)
    out_ref[...] = best


def final_kernel(in_ref, table_ref, best_ref, score_ref):
    got = in_ref[...]
    lane = iota((NC, 128), 1)
    src = iota((NC, 128), 0)
    n = NZ * NK
    pair = jnp.maximum(
        jnp.maximum(got[:n], got[n : 2 * n]), jnp.maximum(got[2 * n : 3 * n], got[3 * n :])
    )
    tops = jnp.concatenate(
        [
            jnp.broadcast_to(jnp.max(pair[NK * z : NK * z + NK], axis=0, keepdims=True), (16, 128))
            for z in range(NZ)
        ],
        axis=0,
    )
    p = iota((128, 128), 0)
    best = jnp.full((1, V), LOW, F32)
    for x in range(NX):
        slot = (x * NK + (p // 8) % NK) * 4 + p % 4
        value = jnp.max(jnp.where(iota((128, 128), 1) == slot, tops, LOW), axis=1, keepdims=True)
        table = table_ref[128 * x : 128 * x + 128, :V].astype(F32)
        best = jnp.maximum(best, jnp.max(jnp.where(table > 0.5, value, LOW), axis=0, keepdims=True))
    best_ref[...] = best
    vals = jnp.where((lane >= 32) & (lane < 36), got, 0.0).astype(BF)
    total = jnp.zeros((8, 128), F32)
    pick = iota((8, 128), 0)
    at = iota((8, 128), 1)
    for t in range(2):
        chosen = one_hot(at == 32 + 2 * t + pick)
        rows = dot_nt(chosen, vals).astype(BF)
        total = total + dot(rows, one_hot(lane == src * 2 + t))
    score_ref[...] = total[:2].astype(BF)


def vm():
    return pl.BlockSpec(memory_space=pltpu.VMEM)


def sm():
    return pl.BlockSpec(memory_space=pltpu.SMEM)


def params(mib=28):
    return pltpu.CompilerParams(vmem_limit_bytes=mib * MIB)


def shards(
    vectors,
    centroids,
    postings,
    fill,
    assign,
    split_posts,
    split_members,
    neigh_post,
    neigh_row,
    neigh_split,
    neigh_dest,
):
    place = jnp.stack([lax.axis_index("x"), lax.axis_index("core")]).astype(I32)
    npost, nrow, nsplit, ndest = (
        a.reshape(1, NB) for a in (neigh_post, neigh_row, neigh_split, neigh_dest)
    )
    one = lambda *shape: pl.BlockSpec(shape, lambda i: (0,) * len(shape))
    packed, table = pl.pallas_call(
        pack_kernel,
        out_shape=(
            jax.ShapeDtypeStruct((NC * 8, P8), BF),
            jax.ShapeDtypeStruct((NC * 8, 128), BF),
        ),
        grid=(1,),
        in_specs=[one(V, D), one(POSTS, HEAD, D), one(1, V), one(1, NB), one(1, NB), one(1, NB)],
        out_specs=(one(NC * 8, P8), one(NC * 8, 128)),
        compiler_params=params(60),
        name="pack_rows",
    )(vectors, postings, assign.reshape(1, V), npost, nrow, ndest)
    held, packed = lax.optimization_barrier((centroids, packed))
    mate = lax.ppermute(held, "core", [(0, 1), (1, 0)])
    got = lax.all_to_all(packed.reshape(NC, 8, P8), CENT, 0, 0, tiled=True).reshape(NC * 8, P8)
    share = pl.pallas_call(
        share_kernel,
        out_shape=jax.ShapeDtypeStruct((NC * 4, D), BF),
        in_specs=[vm()],
        out_specs=vm(),
        compiler_params=params(),
        name="share_rows",
    )(got)
    parts = [lax.ppermute(share, "x", [(i, (i + a) % NX) for i in range(NX)]) for a in range(1, NX)]
    spread = pl.pallas_call(
        spread_kernel,
        out_shape=jax.ShapeDtypeStruct((NY, V, W), BF),
        in_specs=[vm(), vm()],
        out_specs=pl.BlockSpec(memory_space=pltpu.HBM),
        scratch_shapes=[pltpu.VMEM((V, W), BF), pltpu.SemaphoreType.DMA((NY,))],
        compiler_params=params(),
        name="spread_rows",
    )(got, share)
    gathered = lax.all_to_all(spread, "y", 0, 0, tiled=True).reshape(NY * V, W)
    moved_rows = pl.pallas_call(
        moved_kernel,
        out_shape=jax.ShapeDtypeStruct((NC * 2, D), BF),
        in_specs=[vm()],
        out_specs=vm(),
        compiler_params=params(),
        name="moved_rows",
    )(got)

    hbm = pl.BlockSpec(memory_space=pl.ANY)

    def cost(count):
        work = 2 * 4096 * 256 * D * count
        return pl.CostEstimate(flops=work, bytes_accessed=2 * 4096 * D, transcendentals=0)

    first = pl.pallas_call(
        first_kernel,
        out_shape=jax.ShapeDtypeStruct((1, 8, NC * 4), F32),
        in_specs=[vm(), hbm, vm()],
        out_specs=vm(),
        scratch_shapes=[pltpu.VMEM((2048, D), BF), pltpu.SemaphoreType.DMA],
        compiler_params=params(),
        cost_estimate=cost(1),
        name="best_of_share",
    )(centroids, mate, share)
    best = pl.pallas_call(
        best_kernel,
        out_shape=jax.ShapeDtypeStruct((NC, 128), F32),
        in_specs=[sm(), vm(), hbm, hbm, hbm, hbm, vm()],
        out_specs=vm(),
        scratch_shapes=[
            pltpu.VMEM((NX - 1, 8, NC * 4), F32),
            pltpu.VMEM((NX - 1, NC * 4, D), BF),
            pltpu.VMEM((2048, D), BF),
            pltpu.SemaphoreType.DMA((NX,)),
        ],
        compiler_params=params(),
        cost_estimate=cost(3),
        name="best_scores",
    )(place, centroids, mate, *parts, first)
    postings_out, new_fill, split_centers, sending = pl.pallas_call(
        append_kernel,
        out_shape=(
            jax.ShapeDtypeStruct((POSTS, ROWS, D), BF),
            jax.ShapeDtypeStruct((POSTS,), I32),
            jax.ShapeDtypeStruct((2, 2, D), F32),
            jax.ShapeDtypeStruct((NC, 128), F32),
        ),
        grid=(1,),
        in_specs=[
            sm(), sm(), one(NY * V, W), one(POSTS, ROWS, D), one(16, D), one(2, ROWS),
            one(1, NB), one(1, NB), one(1, NB), one(1, NB), one(NC, 128),
        ],
        out_specs=(one(POSTS, ROWS, D), sm(), one(2, 2, D), one(NC, 128)),
        compiler_params=params(60),
        name="append_split",
    )(
        fill, split_posts, gathered, postings, centroids, split_members, npost, nrow, nsplit, ndest,
        best,
    )
    back = lax.all_to_all(sending.reshape(NC, 1, 128), CENT, 0, 0, tiled=True).reshape(NC, 128)
    best_score, moved_scores = pl.pallas_call(
        final_kernel,
        out_shape=(jax.ShapeDtypeStruct((1, V), F32), jax.ShapeDtypeStruct((2, 2 * NC), BF)),
        in_specs=[vm(), vm()],
        out_specs=(vm(), vm()),
        compiler_params=params(),
        name="last_step",
    )(back, table)
    return (
        best_score.reshape(V), postings_out, new_fill, split_centers, moved_rows, moved_scores
    )


def solution(mesh):
    fine = Mesh(mesh.devices.reshape(NY, NX, NZ, NK), ("y", "x", "z", "core"))
    both = ("y",) + CENT
    return jax.shard_map(
        shards,
        mesh=fine,
        in_specs=(
            P(both, None),
            P(CENT, None),
            P(CENT, None, None),
            P(CENT),
            P(both),
            P(CENT),
            P(CENT, None),
            P(both),
            P(both),
            P(both),
            P(both),
        ),
        out_specs=(
            P(both),
            P(CENT, None, None),
            P(CENT),
            P(CENT, None, None),
            P(both, None),
            P(None, both),
        ),
        check_vma=False,
    )
```

```python
import functools

import jax
import jax.numpy as jnp
from jax import lax
from jax.experimental import pallas as pl
from jax.experimental.pallas import tpu as pltpu
from jax.sharding import Mesh, PartitionSpec as P

D = 768
W = 896
ROWS = 128
HEAD = 32
ITERS = 2
NX, NY, NZ, NK = 4, 8, 8, 2
NC = NX * NZ * NK
V = 32
NB = 64
POSTS = 4
CENT = ("x", "z", "core")
LOW = -3.0e38
HALF = D // 2
P8 = HALF + 256
F32 = jnp.float32
BF = jnp.bfloat16
I32 = jnp.int32
MIB = 1024 * 1024


def iota(shape, dim):
    return lax.broadcasted_iota(I32, shape, dim)


def as_column(row):
    n = row.shape[1]
    eye = iota((n, n), 0) == iota((n, n), 1)
    return jnp.sum(jnp.where(eye, jnp.broadcast_to(row, (n, n)), 0), axis=1, keepdims=True)


def earlier_equal(row):
    n = row.shape[1]
    same = (as_column(row) == row) & (iota((n, n), 0) < iota((n, n), 1))
    return jnp.sum(same.astype(I32), axis=0, keepdims=True)


def one_hot(mask):
    return jnp.where(mask, 1.0, 0.0).astype(BF)


def dot(a, b):
    return jnp.dot(a, b, preferred_element_type=F32)


def dot_nt(a, b):
    return lax.dot_general(a, b, (((1,), (1,)), ((), ())), preferred_element_type=F32)


def fetch(pairs, sems):
    copies = [pltpu.make_async_copy(src, dst, sems.at[i]) for i, (src, dst) in enumerate(pairs)]
    for copy in copies:
        copy.start()
    for copy in copies:
        copy.wait()


def pack_kernel(vec_ref, head_ref, assign_ref, npost_ref, nrow_ref, ndest_ref, out_ref, table_ref):
    n = NC * 8
    assign = assign_ref[...]
    dest = assign // POSTS
    zdest = (dest // NK) % NZ
    place = earlier_equal(dest)

    ones = jnp.ones((V, 128), BF)

    def routed(count, per):
        p = iota((count, V), 0)
        to, t = p // per, p % 4
        return (dest == to) & (place == t), (zdest != (to // NK) % NZ)

    named, other = routed(n, 8)
    small, _ = routed(NC * 4, 4)
    free = (1.0 - dot(one_hot(small), ones)).astype(BF)
    p, c = iota((n, NC * 4), 0), iota((n, NC * 4), 1)
    pd, cd = p // 8, c // 4
    slot = ((pd // (NZ * NK)) * NK + pd % NK) * 4 + p % 4
    cslot = ((cd // (NZ * NK)) * NK + cd % NK) * 4 + c % 4
    before = one_hot(((pd // NK) % NZ == (cd // NK) % NZ) & (cslot < slot))
    free_rank = dot(before, free)[:, :V]
    upper = one_hot(iota((V, V), 0) < iota((V, V), 1))
    rest_rank = dot(one_hot(other), upper)
    taken = dot(one_hot(named), ones)[:, :V]
    share = named | (other & (taken < 0.5) & (free_rank == rest_rank))
    low_half = iota((n, V), 0) % 8 < 4
    table = one_hot(share & low_half)
    table_ref[:, :V] = table
    out_ref[:, :HALF] = (
        dot(table, vec_ref[:, :HALF]) + dot(one_hot(share & ~low_half), vec_ref[:, HALF:])
    ).astype(BF)

    ndest = ndest_ref[...]
    nplace = earlier_equal(ndest)
    picks = one_hot(npost_ref[...] * HEAD + nrow_ref[...] == iota((POSTS * HEAD, NB), 0))
    head = head_ref[...].reshape(POSTS * HEAD, D)
    p, c = iota((n, 6 * NC), 0), iota((n, 6 * NC), 1)
    spread = one_hot((p // 8 == c % NC) & (p % 8 == c // NC))
    post = as_column(assign) % POSTS + 1
    mark = jnp.where(iota((V, 128), 1) == as_column(place), post, 0).astype(F32).astype(BF)
    sixth = one_hot((iota((n, V), 0) // 8 == dest) & (iota((n, V), 0) % 8 == 6))
    for t in range(2):
        chosen = one_hot((ndest == iota((NC, NB), 0)) & (nplace == t))
        rows = dot(dot_nt(chosen, picks).astype(BF), head).astype(BF)
        stack = jnp.concatenate([rows[:, 128 * k : 128 * k + 128] for k in range(6)], axis=0)
        tile = dot(spread, stack)
        if t == 0:
            tile = tile + dot(sixth, mark)
        out_ref[:, HALF + 128 * t : HALF + 128 * t + 128] = tile.astype(BF)


def share_kernel(in_ref, share_ref):
    n = NC * 8
    p, i = iota((NC * 4, n), 1), iota((NC * 4, n), 0)
    first = (i // 4) * 8 + i % 4
    rows = in_ref[:, :HALF]
    share_ref[:, :HALF] = dot(one_hot(p == first), rows).astype(BF)
    share_ref[:, HALF:] = dot(one_hot(p == first + 4), rows).astype(BF)


def moved_kernel(in_ref, moved_ref):
    n = NC * 8
    tiles = in_ref[:, HALF:]
    p, i = iota((NC * 2, n), 1), iota((NC * 2, n), 0)
    odd = iota((NC * 2, 128), 0) % 2 == 1
    for k in range(6):
        both = dot(one_hot(p == (i // 2) * 8 + k), tiles)
        moved_ref[:, 128 * k : 128 * k + 128] = jnp.where(odd, both[:, 128:], both[:, :128]).astype(BF)


def spread_kernel(in_ref, share_ref, out_ref, buf_ref, sems):
    n = NC * 8
    p, d = iota((NC, n), 1), iota((NC, n), 0)
    marks = dot(one_hot(p == d * 8 + 6), in_ref[:, HALF : HALF + 128]).astype(BF)
    first = dot_nt(one_hot(iota((8, 128), 1) == 0), marks)
    upper = one_hot(iota((NC, NC), 0) < iota((NC, NC), 1))
    valid = one_hot(first > 0.5)
    rank = dot(valid, upper).astype(BF)
    m = NC * 4
    widen = one_hot(iota((NC, m), 0) == iota((NC, m), 1) // 4)
    valid, rank = dot(valid, widen)[:1], dot(rank, widen)[:1].astype(I32)
    t = iota((V, m), 1) % 4
    hit = one_hot((valid > 0.5) & (t < 2) & (2 * rank + t == iota((V, m), 0)))
    tall = one_hot(iota((m, NC), 1) == iota((m, NC), 0) // 4)
    lane = iota((m, 128), 1)
    mine = jnp.where(lane == iota((m, 128), 0) % 4, dot(tall, marks), 0.0)
    post = jnp.sum(mine, axis=1, keepdims=True)
    buf_ref[:, :D] = dot(hit, share_ref[...]).astype(BF)
    buf_ref[:, D:] = dot(hit, jnp.where(lane == 0, post, 0.0).astype(BF)).astype(BF)
    copies = [pltpu.make_async_copy(buf_ref, out_ref.at[g], sems.at[g]) for g in range(NY)]
    for copy in copies:
        copy.start()
    for copy in copies:
        copy.wait()


def ranks(got, posts):
    n = NY * V
    mark = dot_nt(one_hot(iota((8, 128), 1) == 0), got).astype(I32)
    row = iota((8, n), 0)
    wanted = jnp.zeros((8, n), I32)
    for i, q in enumerate(posts):
        wanted = jnp.where(row == i, q + 1, wanted)
    match = mark == wanted
    upper = one_hot(iota((n, n), 0) < iota((n, n), 1))
    return match, dot(one_hot(match), upper).astype(I32)


def appended(match, rank, i, first, got, before):
    mine = match[i : i + 1]
    count = jnp.sum(mine.astype(I32))
    table = one_hot(mine & (iota((ROWS, NY * V), 0) == first + rank[i : i + 1]))
    line = iota((ROWS, 1), 0)
    hit = (line >= first) & (line < first + count)
    return jnp.where(hit, dot(table, got), before), first + count


def append_kernel(fill_in, got_in, post_ref, out_ref, count_ref, got_ref, fill_ref, sems):
    fetch([(fill_in, fill_ref), (got_in, got_ref)], sems)
    match, rank = ranks(got_ref[:, D:], range(POSTS))
    for q in range(POSTS):
        rows, count = appended(
            match, rank, q, fill_ref[q], got_ref[:, :D], post_ref[q].astype(F32)
        )
        out_ref[q] = rows.astype(BF)
        count_ref[q] = count


def split_kernel(
    fill_in, split_in, got_in, member_in, npost_in, nrow_in, nsplit_in, ndest_in, post_ref, own_ref, best_ref,
    centers_ref, send_ref,
    fill_ref, split_ref, got_ref, member_ref, npost_ref, nrow_ref, nsplit_ref, ndest_ref, sems,
):
    fetch(
        [
            (fill_in, fill_ref), (split_in, split_ref), (got_in, got_ref), (member_in, member_ref),
            (npost_in, npost_ref), (nrow_in, nrow_ref), (nsplit_in, nsplit_ref), (ndest_in, ndest_ref),
        ],
        sems,
    )
    line = iota((ROWS, 1), 0)
    head = post_ref[:, :HEAD, :].reshape(POSTS * HEAD, D).astype(F32)
    members = member_ref[...].astype(F32)
    eye = iota((ROWS, ROWS), 0) == iota((ROWS, ROWS), 1)
    lane = iota((POSTS * HEAD, 128), 1)
    ndest = ndest_ref[...]
    nplace = earlier_equal(ndest)
    nsplit = nsplit_ref[...]
    picks = one_hot(npost_ref[...] * HEAD + nrow_ref[...] == iota((POSTS * HEAD, NB), 0))
    to = iota((NC, NB), 0)
    own = own_ref[:16, :].astype(F32)
    posts = [jnp.maximum(split_ref[s], 0) for s in range(2)]
    match, rank = ranks(got_ref[:, D:], posts)
    sent = jnp.zeros((NC, 128), F32)
    for s in range(2):
        q = posts[s]
        alive = jnp.where(split_ref[s] >= 0, 1.0, 0.0).astype(F32)
        x, filled = appended(match, rank, s, fill_ref[q], got_ref[:, :D], post_ref[q].astype(F32))
        prior = jnp.sum(jnp.where(iota(own.shape, 0) == q, own, 0.0), axis=0, keepdims=True)
        mask = jnp.where(line < filled, 1.0, 0.0).astype(F32)
        weights = jnp.sum(jnp.where(eye, members[s : s + 1], 0.0), axis=1, keepdims=True)

        def update(weights):
            w1, w2 = mask * weights, mask * (1.0 - weights)
            s1 = jnp.sum(w1 * x, axis=0, keepdims=True) + prior
            s2 = jnp.sum(w2 * x, axis=0, keepdims=True) + prior
            t1 = jnp.sum(w1, axis=0, keepdims=True) + 1.0
            t2 = jnp.sum(w2, axis=0, keepdims=True) + 1.0
            return s1 / t1, s2 / t2

        a1, a2 = update(weights)
        for _ in range(ITERS):
            far = jnp.sum(jnp.square(x - a2), axis=1, keepdims=True) - jnp.sum(
                jnp.square(x - a1), axis=1, keepdims=True
            )
            a1, a2 = update(jax.nn.sigmoid(0.125 * far))
        a1, a2 = a1 * alive, a2 * alive
        centers_ref[s, 0:1, :] = a1
        centers_ref[s, 1:2, :] = a2
        c1 = jnp.sum(head * a1, axis=1, keepdims=True)
        c2 = jnp.sum(head * a2, axis=1, keepdims=True)
        for t in range(2):
            where_to = one_hot((ndest == to) & (nplace == t) & (nsplit == s))
            table = dot_nt(where_to, picks).astype(BF)
            values = jnp.where(lane == 32 + 2 * t, c1, jnp.where(lane == 33 + 2 * t, c2, 0.0))
            sent = sent + dot(table, values.astype(BF))
    send_ref[...] = jnp.where(iota((NC, 128), 1) < V, best_ref[...], sent)


BLOCK = 1024


def scan_blocks(ref, part, best):
    for i in range(2048 // BLOCK):
        scores = dot_nt(ref[BLOCK * i : BLOCK * i + BLOCK, :], part)
        best = jnp.maximum(best, jnp.max(scores.reshape(BLOCK // 8, 8, NC * 4), axis=0))
    return best


def first_kernel(own_ref, mate_in, v_ref, v1_in, v2_in, acc_ref, mate_ref, part_ref, sems):
    pairs = ((v1_in, part_ref.at[0]), (v2_in, part_ref.at[1]), (mate_in, mate_ref))
    copies = [pltpu.make_async_copy(src, dst, sems.at[i]) for i, (src, dst) in enumerate(pairs)]
    for copy in copies:
        copy.start()
    blank = jnp.full((8, NC * 4), LOW, F32)
    acc_ref[0] = scan_blocks(own_ref, v_ref[...], blank)
    copies[0].wait()
    acc_ref[1] = scan_blocks(own_ref, part_ref[0], blank)
    copies[1].wait()
    acc_ref[2] = scan_blocks(own_ref, part_ref[1], blank)
    copies[2].wait()
    acc_ref[0] = scan_blocks(mate_ref, v_ref[...], acc_ref[0])
    acc_ref[1] = scan_blocks(mate_ref, part_ref[0], acc_ref[1])
    acc_ref[2] = scan_blocks(mate_ref, part_ref[1], acc_ref[2])


def best_kernel(
    place_ref, own_ref, mate_ref, v_in, post_in, acc_ref, out_ref, post_ref, part_ref, sems
):
    later = pltpu.make_async_copy(post_in, post_ref, sems.at[1])
    fetch([(v_in, part_ref)], sems)
    later.start()
    best = scan_blocks(own_ref, part_ref[...], jnp.full((8, NC * 4), LOW, F32))
    accs = [acc_ref[0], acc_ref[1], scan_blocks(mate_ref, part_ref[...], best), acc_ref[2]]
    x, core = place_ref[0], place_ref[1]
    wide = (NC, NC * 4)
    mine = iota(wide, 1) // 4 == iota(wide, 0)
    lane = iota((NC, 128), 1)
    best = jnp.full((NC, 128), LOW, F32)
    for a in range(NX):
        top = jnp.max(accs[a], axis=0, keepdims=True)
        spread = jnp.where(mine, jnp.broadcast_to(top, wide), LOW)
        folded = jnp.maximum(spread[:, :128], spread[:, 128:])
        for shift in (64, 32, 16, 8, 4):
            folded = jnp.maximum(folded, pltpu.roll(folded, shift, 1))
        group = lax.rem(x + NX - a, NX) * NK + core
        best = jnp.where(lane // 4 == group, folded, best)
    out_ref[...] = best
    later.wait()


def final_kernel(in_ref, table_ref, best_ref, score_ref):
    got = in_ref[...]
    lane = iota((NC, 128), 1)
    src = iota((NC, 128), 0)
    n = NZ * NK
    pair = jnp.maximum(
        jnp.maximum(got[:n], got[n : 2 * n]), jnp.maximum(got[2 * n : 3 * n], got[3 * n :])
    )
    tops = jnp.concatenate(
        [
            jnp.broadcast_to(jnp.max(pair[NK * z : NK * z + NK], axis=0, keepdims=True), (16, 128))
            for z in range(NZ)
        ],
        axis=0,
    )
    p = iota((128, 128), 0)
    best = jnp.full((1, V), LOW, F32)
    for x in range(NX):
        slot = (x * NK + (p // 8) % NK) * 4 + p % 4
        value = jnp.max(jnp.where(iota((128, 128), 1) == slot, tops, LOW), axis=1, keepdims=True)
        table = table_ref[128 * x : 128 * x + 128, :V].astype(F32)
        best = jnp.maximum(best, jnp.max(jnp.where(table > 0.5, value, LOW), axis=0, keepdims=True))
    best_ref[...] = best
    vals = jnp.where((lane >= 32) & (lane < 36), got, 0.0).astype(BF)
    total = jnp.zeros((8, 128), F32)
    pick = iota((8, 128), 0)
    at = iota((8, 128), 1)
    for t in range(2):
        chosen = one_hot(at == 32 + 2 * t + pick)
        rows = dot_nt(chosen, vals).astype(BF)
        total = total + dot(rows, one_hot(lane == src * 2 + t))
    score_ref[...] = total[:2].astype(BF)


def vm():
    return pl.BlockSpec(memory_space=pltpu.VMEM)


def sm():
    return pl.BlockSpec(memory_space=pltpu.SMEM)


def params(mib=28):
    return pltpu.CompilerParams(vmem_limit_bytes=mib * MIB)


def shards(
    vectors,
    centroids,
    postings,
    fill,
    assign,
    split_posts,
    split_members,
    neigh_post,
    neigh_row,
    neigh_split,
    neigh_dest,
):
    place = jnp.stack([lax.axis_index("x"), lax.axis_index("core")]).astype(I32)
    npost, nrow, nsplit, ndest = (
        a.reshape(1, NB) for a in (neigh_post, neigh_row, neigh_split, neigh_dest)
    )
    one = lambda *shape: pl.BlockSpec(shape, lambda i: (0,) * len(shape))
    hbm = pl.BlockSpec(memory_space=pl.ANY)
    packed, table = pl.pallas_call(
        pack_kernel,
        out_shape=(
            jax.ShapeDtypeStruct((NC * 8, P8), BF),
            jax.ShapeDtypeStruct((NC * 8, 128), BF),
        ),
        grid=(1,),
        in_specs=[one(V, D), one(POSTS, HEAD, D), one(1, V), one(1, NB), one(1, NB), one(1, NB)],
        out_specs=(one(NC * 8, P8), one(NC * 8, 128)),
        compiler_params=params(60),
        name="pack_rows",
    )(vectors, postings, assign.reshape(1, V), npost, nrow, ndest)
    got = lax.all_to_all(packed.reshape(NC, 8, P8), CENT, 0, 0, tiled=True).reshape(NC * 8, P8)
    share = pl.pallas_call(
        share_kernel,
        out_shape=jax.ShapeDtypeStruct((NC * 4, D), BF),
        in_specs=[vm()],
        out_specs=vm(),
        compiler_params=params(),
        name="share_rows",
    )(got)
    held, _ = lax.optimization_barrier((centroids, share))
    mate = lax.ppermute(held, "core", [(0, 1), (1, 0)])
    parts = {a: lax.ppermute(share, "x", [(i, (i + a) % NX) for i in range(NX)]) for a in (2, 1, 3)}
    spread = pl.pallas_call(
        spread_kernel,
        out_shape=jax.ShapeDtypeStruct((NY, V, W), BF),
        in_specs=[vm(), vm()],
        out_specs=pl.BlockSpec(memory_space=pltpu.HBM),
        scratch_shapes=[pltpu.VMEM((V, W), BF), pltpu.SemaphoreType.DMA((NY,))],
        compiler_params=params(),
        name="spread_rows",
    )(got, share)
    gathered = lax.all_to_all(spread, "y", 0, 0, tiled=True).reshape(NY * V, W)
    moved_rows = pl.pallas_call(
        moved_kernel,
        out_shape=jax.ShapeDtypeStruct((NC * 2, D), BF),
        in_specs=[vm()],
        out_specs=vm(),
        compiler_params=params(),
        name="moved_rows",
    )(got)

    def cost(count):
        work = 2 * 4096 * 256 * D * count
        return pl.CostEstimate(flops=work, bytes_accessed=2 * 4096 * D, transcendentals=0)

    first, mate = pl.pallas_call(
        first_kernel,
        out_shape=(
            jax.ShapeDtypeStruct((NX - 1, 8, NC * 4), F32),
            jax.ShapeDtypeStruct((2048, D), BF),
        ),
        in_specs=[vm(), hbm, vm(), hbm, hbm],
        out_specs=(vm(), vm()),
        scratch_shapes=[pltpu.VMEM((2, NC * 4, D), BF), pltpu.SemaphoreType.DMA((3,))],
        compiler_params=params(),
        cost_estimate=cost(3),
        name="best_of_three",
    )(centroids, mate, share, parts[1], parts[3])
    best, post_copy = pl.pallas_call(
        best_kernel,
        out_shape=(
            jax.ShapeDtypeStruct((NC, 128), F32),
            jax.ShapeDtypeStruct((POSTS, ROWS, D), BF),
        ),
        in_specs=[sm(), vm(), vm(), hbm, hbm, vm()],
        out_specs=(vm(), vm()),
        scratch_shapes=[pltpu.VMEM((NC * 4, D), BF), pltpu.SemaphoreType.DMA((2,))],
        compiler_params=params(),
        cost_estimate=cost(3),
        name="best_scores",
    )(place, centroids, mate, parts[2], postings, first)
    row = pltpu.VMEM((1, NB), I32)
    split_centers, sending = pl.pallas_call(
        split_kernel,
        out_shape=(
            jax.ShapeDtypeStruct((2, 2, D), F32),
            jax.ShapeDtypeStruct((NC, 128), F32),
        ),
        in_specs=[hbm] * 8 + [vm()] * 3,
        out_specs=(vm(), vm()),
        scratch_shapes=[
            pltpu.SMEM((POSTS,), I32), pltpu.SMEM((2,), I32), pltpu.VMEM((NY * V, W), BF),
            pltpu.VMEM((2, ROWS), I32), row, row, row, row, pltpu.SemaphoreType.DMA((8,)),
        ],
        compiler_params=params(),
        name="split_scores",
    )(
        fill, split_posts, gathered, split_members, npost, nrow, nsplit, ndest, post_copy, centroids, best
    )
    postings_out, new_fill = pl.pallas_call(
        append_kernel,
        out_shape=(
            jax.ShapeDtypeStruct((POSTS, ROWS, D), BF),
            jax.ShapeDtypeStruct((POSTS,), I32),
        ),
        in_specs=[hbm, hbm, vm()],
        out_specs=(vm(), sm()),
        scratch_shapes=[
            pltpu.VMEM((NY * V, W), BF), pltpu.SMEM((POSTS,), I32), pltpu.SemaphoreType.DMA((2,)),
        ],
        compiler_params=params(),
        name="append_rows",
    )(fill, gathered, post_copy)
    back = lax.all_to_all(sending.reshape(NC, 1, 128), CENT, 0, 0, tiled=True).reshape(NC, 128)
    best_score, moved_scores = pl.pallas_call(
        final_kernel,
        out_shape=(jax.ShapeDtypeStruct((1, V), F32), jax.ShapeDtypeStruct((2, 2 * NC), BF)),
        in_specs=[vm(), vm()],
        out_specs=(vm(), vm()),
        compiler_params=params(),
        name="last_step",
    )(back, table)
    return (
        best_score.reshape(V), postings_out, new_fill, split_centers, moved_rows, moved_scores
    )


def solution(mesh):
    fine = Mesh(mesh.devices.reshape(NY, NX, NZ, NK), ("y", "x", "z", "core"))
    both = ("y",) + CENT
    return jax.shard_map(
        shards,
        mesh=fine,
        in_specs=(
            P(both, None),
            P(CENT, None),
            P(CENT, None, None),
            P(CENT),
            P(both),
            P(CENT),
            P(CENT, None),
            P(both),
            P(both),
            P(both),
            P(both),
        ),
        out_specs=(
            P(both),
            P(CENT, None, None),
            P(CENT),
            P(CENT, None, None),
            P(both, None),
            P(None, both),
        ),
        check_vma=False,
    )
```

```python
import functools

import jax
import jax.numpy as jnp
from jax import lax
from jax.experimental import pallas as pl
from jax.experimental.pallas import tpu as pltpu
from jax.sharding import Mesh, PartitionSpec as P

D = 768
W = 896
ROWS = 128
HEAD = 32
ITERS = 2
NX, NY, NZ, NK = 4, 8, 8, 2
NC = NX * NZ * NK
V = 32
NB = 64
POSTS = 4
CENT = ("x", "z", "core")
LOW = -3.0e38
HALF = D // 2
P8 = HALF + 256
F32 = jnp.float32
BF = jnp.bfloat16
I32 = jnp.int32
MIB = 1024 * 1024


def iota(shape, dim):
    return lax.broadcasted_iota(I32, shape, dim)


def as_column(row):
    n = row.shape[1]
    eye = iota((n, n), 0) == iota((n, n), 1)
    return jnp.sum(jnp.where(eye, jnp.broadcast_to(row, (n, n)), 0), axis=1, keepdims=True)


def earlier_equal(row):
    n = row.shape[1]
    same = (as_column(row) == row) & (iota((n, n), 0) < iota((n, n), 1))
    return jnp.sum(same.astype(I32), axis=0, keepdims=True)


def one_hot(mask):
    return jnp.where(mask, 1.0, 0.0).astype(BF)


def dot(a, b):
    return jnp.dot(a, b, preferred_element_type=F32)


def dot_nt(a, b):
    return lax.dot_general(a, b, (((1,), (1,)), ((), ())), preferred_element_type=F32)


def fetch(pairs, sems):
    copies = [pltpu.make_async_copy(src, dst, sems.at[i]) for i, (src, dst) in enumerate(pairs)]
    for copy in copies:
        copy.start()
    for copy in copies:
        copy.wait()


def pack_kernel(vec_ref, head_ref, assign_ref, npost_ref, nrow_ref, ndest_ref, out_ref, table_ref):
    n = NC * 8
    assign = assign_ref[...]
    dest = assign // POSTS
    zdest = (dest // NK) % NZ
    place = earlier_equal(dest)

    ones = jnp.ones((V, 128), BF)

    def routed(count, per):
        p = iota((count, V), 0)
        to, t = p // per, p % 4
        return (dest == to) & (place == t), (zdest != (to // NK) % NZ)

    named, other = routed(n, 8)
    small, _ = routed(NC * 4, 4)
    free = (1.0 - dot(one_hot(small), ones)).astype(BF)
    p, c = iota((n, NC * 4), 0), iota((n, NC * 4), 1)
    pd, cd = p // 8, c // 4
    slot = ((pd // (NZ * NK)) * NK + pd % NK) * 4 + p % 4
    cslot = ((cd // (NZ * NK)) * NK + cd % NK) * 4 + c % 4
    before = one_hot(((pd // NK) % NZ == (cd // NK) % NZ) & (cslot < slot))
    free_rank = dot(before, free)[:, :V]
    upper = one_hot(iota((V, V), 0) < iota((V, V), 1))
    rest_rank = dot(one_hot(other), upper)
    taken = dot(one_hot(named), ones)[:, :V]
    share = named | (other & (taken < 0.5) & (free_rank == rest_rank))
    low_half = iota((n, V), 0) % 8 < 4
    table = one_hot(share & low_half)
    table_ref[:, :V] = table
    out_ref[:, :HALF] = (
        dot(table, vec_ref[:, :HALF]) + dot(one_hot(share & ~low_half), vec_ref[:, HALF:])
    ).astype(BF)

    ndest = ndest_ref[...]
    nplace = earlier_equal(ndest)
    picks = one_hot(npost_ref[...] * HEAD + nrow_ref[...] == iota((POSTS * HEAD, NB), 0))
    head = head_ref[...].reshape(POSTS * HEAD, D)
    p, c = iota((n, 6 * NC), 0), iota((n, 6 * NC), 1)
    spread = one_hot((p // 8 == c % NC) & (p % 8 == c // NC))
    post = as_column(assign) % POSTS + 1
    mark = jnp.where(iota((V, 128), 1) == as_column(place), post, 0).astype(F32).astype(BF)
    sixth = one_hot((iota((n, V), 0) // 8 == dest) & (iota((n, V), 0) % 8 == 6))
    for t in range(2):
        chosen = one_hot((ndest == iota((NC, NB), 0)) & (nplace == t))
        rows = dot(dot_nt(chosen, picks).astype(BF), head).astype(BF)
        stack = jnp.concatenate([rows[:, 128 * k : 128 * k + 128] for k in range(6)], axis=0)
        tile = dot(spread, stack)
        if t == 0:
            tile = tile + dot(sixth, mark)
        out_ref[:, HALF + 128 * t : HALF + 128 * t + 128] = tile.astype(BF)


def share_kernel(in_ref, share_ref):
    n = NC * 8
    p, i = iota((NC * 4, n), 1), iota((NC * 4, n), 0)
    first = (i // 4) * 8 + i % 4
    rows = in_ref[:, :HALF]
    share_ref[:, :HALF] = dot(one_hot(p == first), rows).astype(BF)
    share_ref[:, HALF:] = dot(one_hot(p == first + 4), rows).astype(BF)


def moved_kernel(in_ref, moved_ref):
    n = NC * 8
    tiles = in_ref[:, HALF:]
    p, i = iota((NC * 2, n), 1), iota((NC * 2, n), 0)
    odd = iota((NC * 2, 128), 0) % 2 == 1
    for k in range(6):
        both = dot(one_hot(p == (i // 2) * 8 + k), tiles)
        moved_ref[:, 128 * k : 128 * k + 128] = jnp.where(odd, both[:, 128:], both[:, :128]).astype(BF)


def spread_kernel(in_ref, share_ref, out_ref, buf_ref, sems):
    n = NC * 8
    p, d = iota((NC, n), 1), iota((NC, n), 0)
    marks = dot(one_hot(p == d * 8 + 6), in_ref[:, HALF : HALF + 128]).astype(BF)
    first = dot_nt(one_hot(iota((8, 128), 1) == 0), marks)
    upper = one_hot(iota((NC, NC), 0) < iota((NC, NC), 1))
    valid = one_hot(first > 0.5)
    rank = dot(valid, upper).astype(BF)
    m = NC * 4
    widen = one_hot(iota((NC, m), 0) == iota((NC, m), 1) // 4)
    valid, rank = dot(valid, widen)[:1], dot(rank, widen)[:1].astype(I32)
    t = iota((V, m), 1) % 4
    hit = one_hot((valid > 0.5) & (t < 2) & (2 * rank + t == iota((V, m), 0)))
    tall = one_hot(iota((m, NC), 1) == iota((m, NC), 0) // 4)
    lane = iota((m, 128), 1)
    mine = jnp.where(lane == iota((m, 128), 0) % 4, dot(tall, marks), 0.0)
    post = jnp.sum(mine, axis=1, keepdims=True)
    buf_ref[:, :D] = dot(hit, share_ref[...]).astype(BF)
    buf_ref[:, D:] = dot(hit, jnp.where(lane == 0, post, 0.0).astype(BF)).astype(BF)
    copies = [pltpu.make_async_copy(buf_ref, out_ref.at[g], sems.at[g]) for g in range(NY)]
    for copy in copies:
        copy.start()
    for copy in copies:
        copy.wait()


def ranks(got, posts):
    n = NY * V
    mark = dot_nt(one_hot(iota((8, 128), 1) == 0), got).astype(I32)
    row = iota((8, n), 0)
    wanted = jnp.zeros((8, n), I32)
    for i, q in enumerate(posts):
        wanted = jnp.where(row == i, q + 1, wanted)
    match = mark == wanted
    upper = one_hot(iota((n, n), 0) < iota((n, n), 1))
    return match, dot(one_hot(match), upper).astype(I32)


def appended(match, rank, i, first, got, before):
    mine = match[i : i + 1]
    count = jnp.sum(mine.astype(I32))
    table = one_hot(mine & (iota((ROWS, NY * V), 0) == first + rank[i : i + 1]))
    line = iota((ROWS, 1), 0)
    hit = (line >= first) & (line < first + count)
    return jnp.where(hit, dot(table, got), before), first + count


def append_kernel(fill_ref, got_ref, post_ref, out_ref, count_ref):
    match, rank = ranks(got_ref[:, D:], range(POSTS))
    for q in range(POSTS):
        rows, count = appended(
            match, rank, q, fill_ref[q], got_ref[:, :D], post_ref[q].astype(F32)
        )
        out_ref[q] = rows.astype(BF)
        count_ref[q] = count


def split_kernel(
    fill_ref, split_ref, got_ref, member_ref, npost_ref, nrow_ref, nsplit_ref, ndest_ref, post_ref, own_ref,
    best_ref, centers_ref, send_ref,
):
    line = iota((ROWS, 1), 0)
    head = post_ref[:, :HEAD, :].reshape(POSTS * HEAD, D).astype(F32)
    members = member_ref[...].astype(F32)
    eye = iota((ROWS, ROWS), 0) == iota((ROWS, ROWS), 1)
    lane = iota((POSTS * HEAD, 128), 1)
    ndest = ndest_ref[...]
    nplace = earlier_equal(ndest)
    nsplit = nsplit_ref[...]
    picks = one_hot(npost_ref[...] * HEAD + nrow_ref[...] == iota((POSTS * HEAD, NB), 0))
    to = iota((NC, NB), 0)
    own = own_ref[:16, :].astype(F32)
    posts = [jnp.maximum(split_ref[s], 0) for s in range(2)]
    match, rank = ranks(got_ref[:, D:], posts)
    sent = jnp.zeros((NC, 128), F32)
    for s in range(2):
        q = posts[s]
        alive = jnp.where(split_ref[s] >= 0, 1.0, 0.0).astype(F32)
        x, filled = appended(match, rank, s, fill_ref[q], got_ref[:, :D], post_ref[q].astype(F32))
        prior = jnp.sum(jnp.where(iota(own.shape, 0) == q, own, 0.0), axis=0, keepdims=True)
        mask = jnp.where(line < filled, 1.0, 0.0).astype(F32)
        weights = jnp.sum(jnp.where(eye, members[s : s + 1], 0.0), axis=1, keepdims=True)

        def update(weights):
            w1, w2 = mask * weights, mask * (1.0 - weights)
            s1 = jnp.sum(w1 * x, axis=0, keepdims=True) + prior
            s2 = jnp.sum(w2 * x, axis=0, keepdims=True) + prior
            t1 = jnp.sum(w1, axis=0, keepdims=True) + 1.0
            t2 = jnp.sum(w2, axis=0, keepdims=True) + 1.0
            return s1 / t1, s2 / t2

        a1, a2 = update(weights)
        for _ in range(ITERS):
            far = jnp.sum(jnp.square(x - a2), axis=1, keepdims=True) - jnp.sum(
                jnp.square(x - a1), axis=1, keepdims=True
            )
            a1, a2 = update(jax.nn.sigmoid(0.125 * far))
        a1, a2 = a1 * alive, a2 * alive
        centers_ref[s, 0:1, :] = a1
        centers_ref[s, 1:2, :] = a2
        c1 = jnp.sum(head * a1, axis=1, keepdims=True)
        c2 = jnp.sum(head * a2, axis=1, keepdims=True)
        for t in range(2):
            where_to = one_hot((ndest == to) & (nplace == t) & (nsplit == s))
            table = dot_nt(where_to, picks).astype(BF)
            values = jnp.where(lane == 32 + 2 * t, c1, jnp.where(lane == 33 + 2 * t, c2, 0.0))
            sent = sent + dot(table, values.astype(BF))
    send_ref[...] = jnp.where(iota((NC, 128), 1) < V, best_ref[...], sent)


BLOCK = 1024


def scan_blocks(ref, part, best):
    for i in range(2048 // BLOCK):
        scores = dot_nt(ref[BLOCK * i : BLOCK * i + BLOCK, :], part)
        best = jnp.maximum(best, jnp.max(scores.reshape(BLOCK // 8, 8, NC * 4), axis=0))
    return best


def first_kernel(own_ref, mate_in, v_ref, v1_in, v2_in, acc_ref, near_ref, mate_ref, part_ref, sems):
    pairs = ((v1_in, part_ref.at[0]), (v2_in, part_ref.at[1]), (mate_in, mate_ref), (own_ref, near_ref))
    copies = [pltpu.make_async_copy(src, dst, sems.at[i]) for i, (src, dst) in enumerate(pairs)]
    for copy in copies:
        copy.start()
    blank = jnp.full((8, NC * 4), LOW, F32)
    acc_ref[0] = scan_blocks(own_ref, v_ref[...], blank)
    copies[0].wait()
    acc_ref[1] = scan_blocks(own_ref, part_ref[0], blank)
    copies[1].wait()
    acc_ref[2] = scan_blocks(own_ref, part_ref[1], blank)
    copies[2].wait()
    acc_ref[0] = scan_blocks(mate_ref, v_ref[...], acc_ref[0])
    acc_ref[1] = scan_blocks(mate_ref, part_ref[0], acc_ref[1])
    acc_ref[2] = scan_blocks(mate_ref, part_ref[1], acc_ref[2])
    copies[3].wait()


def best_kernel(
    place_ref, own_ref, mate_ref, v_in, acc_ref, post_ref, out_ref, prior_ref, part_ref, sems
):
    fetch([(v_in, part_ref)], sems)
    prior_ref[...] = own_ref[:16, :]
    best = scan_blocks(own_ref, part_ref[...], jnp.full((8, NC * 4), LOW, F32))
    accs = [acc_ref[0], acc_ref[1], scan_blocks(mate_ref, part_ref[...], best), acc_ref[2]]
    x, core = place_ref[0], place_ref[1]
    wide = (NC, NC * 4)
    mine = iota(wide, 1) // 4 == iota(wide, 0)
    lane = iota((NC, 128), 1)
    best = jnp.full((NC, 128), LOW, F32)
    for a in range(NX):
        top = jnp.max(accs[a], axis=0, keepdims=True)
        spread = jnp.where(mine, jnp.broadcast_to(top, wide), LOW)
        folded = jnp.maximum(spread[:, :128], spread[:, 128:])
        for shift in (64, 32, 16, 8, 4):
            folded = jnp.maximum(folded, pltpu.roll(folded, shift, 1))
        group = lax.rem(x + NX - a, NX) * NK + core
        best = jnp.where(lane // 4 == group, folded, best)
    out_ref[...] = best


def final_kernel(in_ref, table_ref, best_ref, score_ref):
    got = in_ref[...]
    lane = iota((NC, 128), 1)
    src = iota((NC, 128), 0)
    n = NZ * NK
    pair = jnp.maximum(
        jnp.maximum(got[:n], got[n : 2 * n]), jnp.maximum(got[2 * n : 3 * n], got[3 * n :])
    )
    tops = jnp.concatenate(
        [
            jnp.broadcast_to(jnp.max(pair[NK * z : NK * z + NK], axis=0, keepdims=True), (16, 128))
            for z in range(NZ)
        ],
        axis=0,
    )
    p = iota((128, 128), 0)
    best = jnp.full((1, V), LOW, F32)
    for x in range(NX):
        slot = (x * NK + (p // 8) % NK) * 4 + p % 4
        value = jnp.max(jnp.where(iota((128, 128), 1) == slot, tops, LOW), axis=1, keepdims=True)
        table = table_ref[128 * x : 128 * x + 128, :V].astype(F32)
        best = jnp.maximum(best, jnp.max(jnp.where(table > 0.5, value, LOW), axis=0, keepdims=True))
    best_ref[...] = best
    vals = jnp.where((lane >= 32) & (lane < 36), got, 0.0).astype(BF)
    total = jnp.zeros((8, 128), F32)
    pick = iota((8, 128), 0)
    at = iota((8, 128), 1)
    for t in range(2):
        chosen = one_hot(at == 32 + 2 * t + pick)
        rows = dot_nt(chosen, vals).astype(BF)
        total = total + dot(rows, one_hot(lane == src * 2 + t))
    score_ref[...] = total[:2].astype(BF)


def vm():
    return pl.BlockSpec(memory_space=pltpu.VMEM)


def sm():
    return pl.BlockSpec(memory_space=pltpu.SMEM)


def params(mib=28):
    return pltpu.CompilerParams(vmem_limit_bytes=mib * MIB)


def shards(
    vectors,
    centroids,
    postings,
    fill,
    assign,
    split_posts,
    split_members,
    neigh_post,
    neigh_row,
    neigh_split,
    neigh_dest,
):
    place = jnp.stack([lax.axis_index("x"), lax.axis_index("core")]).astype(I32)
    npost, nrow, nsplit, ndest = (
        a.reshape(1, NB) for a in (neigh_post, neigh_row, neigh_split, neigh_dest)
    )
    one = lambda *shape: pl.BlockSpec(shape, lambda i: (0,) * len(shape))
    hbm = pl.BlockSpec(memory_space=pl.ANY)
    packed, table = pl.pallas_call(
        pack_kernel,
        out_shape=(
            jax.ShapeDtypeStruct((NC * 8, P8), BF),
            jax.ShapeDtypeStruct((NC * 8, 128), BF),
        ),
        grid=(1,),
        in_specs=[one(V, D), one(POSTS, HEAD, D), one(1, V), one(1, NB), one(1, NB), one(1, NB)],
        out_specs=(one(NC * 8, P8), one(NC * 8, 128)),
        compiler_params=params(60),
        name="pack_rows",
    )(vectors, postings, assign.reshape(1, V), npost, nrow, ndest)
    got = lax.all_to_all(packed.reshape(NC, 8, P8), CENT, 0, 0, tiled=True).reshape(NC * 8, P8)
    share = pl.pallas_call(
        share_kernel,
        out_shape=jax.ShapeDtypeStruct((NC * 4, D), BF),
        in_specs=[vm()],
        out_specs=vm(),
        compiler_params=params(),
        name="share_rows",
    )(got)
    held, _ = lax.optimization_barrier((centroids, share))
    mate = lax.ppermute(held, "core", [(0, 1), (1, 0)])
    parts = {a: lax.ppermute(share, "x", [(i, (i + a) % NX) for i in range(NX)]) for a in (2, 1, 3)}
    spread = pl.pallas_call(
        spread_kernel,
        out_shape=jax.ShapeDtypeStruct((NY, V, W), BF),
        in_specs=[vm(), vm()],
        out_specs=pl.BlockSpec(memory_space=pltpu.HBM),
        scratch_shapes=[pltpu.VMEM((V, W), BF), pltpu.SemaphoreType.DMA((NY,))],
        compiler_params=params(),
        name="spread_rows",
    )(got, share)
    gathered = lax.all_to_all(spread, "y", 0, 0, tiled=True).reshape(NY * V, W)
    moved_rows = pl.pallas_call(
        moved_kernel,
        out_shape=jax.ShapeDtypeStruct((NC * 2, D), BF),
        in_specs=[vm()],
        out_specs=vm(),
        compiler_params=params(),
        name="moved_rows",
    )(got)

    def cost(count):
        work = 2 * 4096 * 256 * D * count
        return pl.CostEstimate(flops=work, bytes_accessed=2 * 4096 * D, transcendentals=0)

    first, near, mate = pl.pallas_call(
        first_kernel,
        out_shape=(
            jax.ShapeDtypeStruct((NX - 1, 8, NC * 4), F32),
            jax.ShapeDtypeStruct((2048, D), BF),
            jax.ShapeDtypeStruct((2048, D), BF),
        ),
        in_specs=[vm(), hbm, vm(), hbm, hbm],
        out_specs=(vm(), vm(), vm()),
        scratch_shapes=[pltpu.VMEM((2, NC * 4, D), BF), pltpu.SemaphoreType.DMA((4,))],
        compiler_params=params(),
        cost_estimate=cost(3),
        name="best_of_three",
    )(centroids, mate, share, parts[1], parts[3])
    best, priors = pl.pallas_call(
        best_kernel,
        out_shape=(jax.ShapeDtypeStruct((NC, 128), F32), jax.ShapeDtypeStruct((16, D), BF)),
        in_specs=[sm(), vm(), vm(), hbm, vm(), vm()],
        out_specs=(vm(), vm()),
        scratch_shapes=[pltpu.VMEM((NC * 4, D), BF), pltpu.SemaphoreType.DMA((1,))],
        compiler_params=params(),
        cost_estimate=cost(1),
        name="best_scores",
    )(place, near, mate, parts[2], first, postings)
    split_centers, sending = pl.pallas_call(
        split_kernel,
        out_shape=(
            jax.ShapeDtypeStruct((2, 2, D), F32),
            jax.ShapeDtypeStruct((NC, 128), F32),
        ),
        in_specs=[sm(), sm()] + [vm()] * 9,
        out_specs=(vm(), vm()),
        compiler_params=params(),
        name="split_scores",
    )(
        fill, split_posts, gathered, split_members, npost, nrow, nsplit, ndest, postings, priors, best
    )
    postings_out, new_fill = pl.pallas_call(
        append_kernel,
        out_shape=(
            jax.ShapeDtypeStruct((POSTS, ROWS, D), BF),
            jax.ShapeDtypeStruct((POSTS,), I32),
        ),
        in_specs=[sm(), vm(), vm()],
        out_specs=(vm(), sm()),
        compiler_params=params(),
        name="append_rows",
    )(fill, gathered, postings)
    back = lax.all_to_all(sending.reshape(NC, 1, 128), CENT, 0, 0, tiled=True).reshape(NC, 128)
    best_score, moved_scores = pl.pallas_call(
        final_kernel,
        out_shape=(jax.ShapeDtypeStruct((1, V), F32), jax.ShapeDtypeStruct((2, 2 * NC), BF)),
        in_specs=[vm(), vm()],
        out_specs=(vm(), vm()),
        compiler_params=params(),
        name="last_step",
    )(back, table)
    return (
        best_score.reshape(V), postings_out, new_fill, split_centers, moved_rows, moved_scores
    )


def solution(mesh):
    fine = Mesh(mesh.devices.reshape(NY, NX, NZ, NK), ("y", "x", "z", "core"))
    both = ("y",) + CENT
    return jax.shard_map(
        shards,
        mesh=fine,
        in_specs=(
            P(both, None),
            P(CENT, None),
            P(CENT, None, None),
            P(CENT),
            P(both),
            P(CENT),
            P(CENT, None),
            P(both),
            P(both),
            P(both),
            P(both),
        ),
        out_specs=(
            P(both),
            P(CENT, None, None),
            P(CENT),
            P(CENT, None, None),
            P(both, None),
            P(None, both),
        ),
        check_vma=False,
    )
```

```python
import functools

import jax
import jax.numpy as jnp
from jax import lax
from jax.experimental import pallas as pl
from jax.experimental.pallas import tpu as pltpu
from jax.sharding import Mesh, PartitionSpec as P

D = 768
W = 896
ROWS = 128
HEAD = 32
ITERS = 2
NX, NY, NZ, NK = 4, 8, 8, 2
NC = NX * NZ * NK
V = 32
NB = 64
POSTS = 4
CENT = ("x", "z", "core")
LOW = -3.0e38
HALF = D // 2
P8 = HALF + 256
F32 = jnp.float32
BF = jnp.bfloat16
I32 = jnp.int32
MIB = 1024 * 1024


def iota(shape, dim):
    return lax.broadcasted_iota(I32, shape, dim)


def as_column(row):
    n = row.shape[1]
    eye = iota((n, n), 0) == iota((n, n), 1)
    return jnp.sum(jnp.where(eye, jnp.broadcast_to(row, (n, n)), 0), axis=1, keepdims=True)


def earlier_equal(row):
    n = row.shape[1]
    same = (as_column(row) == row) & (iota((n, n), 0) < iota((n, n), 1))
    return jnp.sum(same.astype(I32), axis=0, keepdims=True)


def one_hot(mask):
    return jnp.where(mask, 1.0, 0.0).astype(BF)


def dot(a, b):
    return jnp.dot(a, b, preferred_element_type=F32)


def dot_nt(a, b):
    return lax.dot_general(a, b, (((1,), (1,)), ((), ())), preferred_element_type=F32)


def fetch(pairs, sems):
    copies = [pltpu.make_async_copy(src, dst, sems.at[i]) for i, (src, dst) in enumerate(pairs)]
    for copy in copies:
        copy.start()
    for copy in copies:
        copy.wait()


def pack_kernel(vec_ref, head_ref, assign_ref, npost_ref, nrow_ref, ndest_ref, out_ref, table_ref):
    n = NC * 8
    assign = assign_ref[...]
    dest = assign // POSTS
    zdest = (dest // NK) % NZ
    place = earlier_equal(dest)

    ones = jnp.ones((V, 128), BF)

    def routed(count, per):
        p = iota((count, V), 0)
        to, t = p // per, p % 4
        return (dest == to) & (place == t), (zdest != (to // NK) % NZ)

    named, other = routed(n, 8)
    small, _ = routed(NC * 4, 4)
    free = (1.0 - dot(one_hot(small), ones)).astype(BF)
    p, c = iota((n, NC * 4), 0), iota((n, NC * 4), 1)
    pd, cd = p // 8, c // 4
    slot = ((pd // (NZ * NK)) * NK + pd % NK) * 4 + p % 4
    cslot = ((cd // (NZ * NK)) * NK + cd % NK) * 4 + c % 4
    before = one_hot(((pd // NK) % NZ == (cd // NK) % NZ) & (cslot < slot))
    free_rank = dot(before, free)[:, :V]
    upper = one_hot(iota((V, V), 0) < iota((V, V), 1))
    rest_rank = dot(one_hot(other), upper)
    taken = dot(one_hot(named), ones)[:, :V]
    share = named | (other & (taken < 0.5) & (free_rank == rest_rank))
    low_half = iota((n, V), 0) % 8 < 4
    table = one_hot(share & low_half)
    table_ref[:, :V] = table
    out_ref[:, :HALF] = (
        dot(table, vec_ref[:, :HALF]) + dot(one_hot(share & ~low_half), vec_ref[:, HALF:])
    ).astype(BF)

    ndest = ndest_ref[...]
    nplace = earlier_equal(ndest)
    picks = one_hot(npost_ref[...] * HEAD + nrow_ref[...] == iota((POSTS * HEAD, NB), 0))
    head = head_ref[...].reshape(POSTS * HEAD, D)
    p, c = iota((n, 6 * NC), 0), iota((n, 6 * NC), 1)
    spread = one_hot((p // 8 == c % NC) & (p % 8 == c // NC))
    post = as_column(assign) % POSTS + 1
    mark = jnp.where(iota((V, 128), 1) == as_column(place), post, 0).astype(F32).astype(BF)
    sixth = one_hot((iota((n, V), 0) // 8 == dest) & (iota((n, V), 0) % 8 == 6))
    for t in range(2):
        chosen = one_hot((ndest == iota((NC, NB), 0)) & (nplace == t))
        rows = dot(dot_nt(chosen, picks).astype(BF), head).astype(BF)
        stack = jnp.concatenate([rows[:, 128 * k : 128 * k + 128] for k in range(6)], axis=0)
        tile = dot(spread, stack)
        if t == 0:
            tile = tile + dot(sixth, mark)
        out_ref[:, HALF + 128 * t : HALF + 128 * t + 128] = tile.astype(BF)


def share_kernel(in_ref, share_ref):
    n = NC * 8
    p, i = iota((NC * 4, n), 1), iota((NC * 4, n), 0)
    first = (i // 4) * 8 + i % 4
    rows = in_ref[:, :HALF]
    share_ref[:, :HALF] = dot(one_hot(p == first), rows).astype(BF)
    share_ref[:, HALF:] = dot(one_hot(p == first + 4), rows).astype(BF)


def moved_kernel(in_ref, moved_ref):
    n = NC * 8
    tiles = in_ref[:, HALF:]
    p, i = iota((NC * 2, n), 1), iota((NC * 2, n), 0)
    odd = iota((NC * 2, 128), 0) % 2 == 1
    for k in range(6):
        both = dot(one_hot(p == (i // 2) * 8 + k), tiles)
        moved_ref[:, 128 * k : 128 * k + 128] = jnp.where(odd, both[:, 128:], both[:, :128]).astype(BF)


def spread_kernel(in_ref, share_ref, out_ref, buf_ref, sems):
    n = NC * 8
    p, d = iota((NC, n), 1), iota((NC, n), 0)
    marks = dot(one_hot(p == d * 8 + 6), in_ref[:, HALF : HALF + 128]).astype(BF)
    first = dot_nt(one_hot(iota((8, 128), 1) == 0), marks)
    upper = one_hot(iota((NC, NC), 0) < iota((NC, NC), 1))
    valid = one_hot(first > 0.5)
    rank = dot(valid, upper).astype(BF)
    m = NC * 4
    widen = one_hot(iota((NC, m), 0) == iota((NC, m), 1) // 4)
    valid, rank = dot(valid, widen)[:1], dot(rank, widen)[:1].astype(I32)
    t = iota((V, m), 1) % 4
    hit = one_hot((valid > 0.5) & (t < 2) & (2 * rank + t == iota((V, m), 0)))
    tall = one_hot(iota((m, NC), 1) == iota((m, NC), 0) // 4)
    lane = iota((m, 128), 1)
    mine = jnp.where(lane == iota((m, 128), 0) % 4, dot(tall, marks), 0.0)
    post = jnp.sum(mine, axis=1, keepdims=True)
    buf_ref[:, :D] = dot(hit, share_ref[...]).astype(BF)
    buf_ref[:, D:] = dot(hit, jnp.where(lane == 0, post, 0.0).astype(BF)).astype(BF)
    copies = [pltpu.make_async_copy(buf_ref, out_ref.at[g], sems.at[g]) for g in range(NY)]
    for copy in copies:
        copy.start()
    for copy in copies:
        copy.wait()


def ranks(got, posts):
    n = NY * V
    mark = dot_nt(one_hot(iota((8, 128), 1) == 0), got).astype(I32)
    row = iota((8, n), 0)
    wanted = jnp.zeros((8, n), I32)
    for i, q in enumerate(posts):
        wanted = jnp.where(row == i, q + 1, wanted)
    match = mark == wanted
    upper = one_hot(iota((n, n), 0) < iota((n, n), 1))
    return match, dot(one_hot(match), upper).astype(I32)


def appended(match, rank, i, first, got, before):
    mine = match[i : i + 1]
    count = jnp.sum(mine.astype(I32))
    table = one_hot(mine & (iota((ROWS, NY * V), 0) == first + rank[i : i + 1]))
    line = iota((ROWS, 1), 0)
    hit = (line >= first) & (line < first + count)
    return jnp.where(hit, dot(table, got), before), first + count


def append_kernel(fill_ref, got_ref, post_ref, out_ref, count_ref):
    match, rank = ranks(got_ref[:, D:], range(POSTS))
    for q in range(POSTS):
        rows, count = appended(
            match, rank, q, fill_ref[q], got_ref[:, :D], post_ref[q].astype(F32)
        )
        out_ref[q] = rows.astype(BF)
        count_ref[q] = count


def split_kernel(
    fill_ref, split_ref, got_ref, member_ref, npost_ref, nrow_ref, nsplit_ref, ndest_ref, post_ref, own_ref,
    best_ref, centers_ref, send_ref,
):
    line = iota((ROWS, 1), 0)
    head = post_ref[:, :HEAD, :].reshape(POSTS * HEAD, D).astype(F32)
    members = member_ref[...].astype(F32)
    eye = iota((ROWS, ROWS), 0) == iota((ROWS, ROWS), 1)
    lane = iota((POSTS * HEAD, 128), 1)
    ndest = ndest_ref[...]
    nplace = earlier_equal(ndest)
    nsplit = nsplit_ref[...]
    picks = one_hot(npost_ref[...] * HEAD + nrow_ref[...] == iota((POSTS * HEAD, NB), 0))
    to = iota((NC, NB), 0)
    own = own_ref[:16, :].astype(F32)
    posts = [jnp.maximum(split_ref[s], 0) for s in range(2)]
    match, rank = ranks(got_ref[:, D:], posts)
    sent = jnp.zeros((NC, 128), F32)
    for s in range(2):
        q = posts[s]
        alive = jnp.where(split_ref[s] >= 0, 1.0, 0.0).astype(F32)
        x, filled = appended(match, rank, s, fill_ref[q], got_ref[:, :D], post_ref[q].astype(F32))
        prior = jnp.sum(jnp.where(iota(own.shape, 0) == q, own, 0.0), axis=0, keepdims=True)
        mask = jnp.where(line < filled, 1.0, 0.0).astype(F32)
        weights = jnp.sum(jnp.where(eye, members[s : s + 1], 0.0), axis=1, keepdims=True)

        def update(weights):
            w1, w2 = mask * weights, mask * (1.0 - weights)
            s1 = jnp.sum(w1 * x, axis=0, keepdims=True) + prior
            s2 = jnp.sum(w2 * x, axis=0, keepdims=True) + prior
            t1 = jnp.sum(w1, axis=0, keepdims=True) + 1.0
            t2 = jnp.sum(w2, axis=0, keepdims=True) + 1.0
            return s1 / t1, s2 / t2

        a1, a2 = update(weights)
        for _ in range(ITERS):
            far = jnp.sum(jnp.square(x - a2), axis=1, keepdims=True) - jnp.sum(
                jnp.square(x - a1), axis=1, keepdims=True
            )
            a1, a2 = update(jax.nn.sigmoid(0.125 * far))
        a1, a2 = a1 * alive, a2 * alive
        centers_ref[s, 0:1, :] = a1
        centers_ref[s, 1:2, :] = a2
        c1 = jnp.sum(head * a1, axis=1, keepdims=True)
        c2 = jnp.sum(head * a2, axis=1, keepdims=True)
        for t in range(2):
            where_to = one_hot((ndest == to) & (nplace == t) & (nsplit == s))
            table = dot_nt(where_to, picks).astype(BF)
            values = jnp.where(lane == 32 + 2 * t, c1, jnp.where(lane == 33 + 2 * t, c2, 0.0))
            sent = sent + dot(table, values.astype(BF))
    send_ref[...] = jnp.where(iota((NC, 128), 1) < V, best_ref[...], sent)


BLOCK = 1024
CUTS = 4


def scan_blocks(ref, part, best):
    for i in range(2048 // BLOCK):
        scores = dot_nt(ref[BLOCK * i : BLOCK * i + BLOCK, :], part)
        best = jnp.maximum(best, jnp.max(scores.reshape(BLOCK // 8, 8, NC * 4), axis=0))
    return best


def first_kernel(own_in, mate_in, v_ref, v1_in, v2_in, acc_ref, own_ref, mate_ref, part_ref, sems):
    rows = 2048 // CUTS
    pieces = [
        (src.at[pl.ds(rows * i, rows), :], dst.at[pl.ds(rows * i, rows), :])
        for src, dst in ((own_in, own_ref), (mate_in, mate_ref))
        for i in range(CUTS)
    ]
    pairs = pieces[:1] + [(v1_in, part_ref.at[0]), (v2_in, part_ref.at[1])] + pieces[1:]
    copies = [pltpu.make_async_copy(src, dst, sems.at[i]) for i, (src, dst) in enumerate(pairs)]
    for copy in copies:
        copy.start()
    for copy in copies[:3]:
        copy.wait()
    best = [jnp.full((8, NC * 4), LOW, F32)] * 3
    for c in range(2 * CUTS):
        if c > 0:
            copies[2 + c].wait()
        ref = own_ref if c < CUTS else mate_ref
        block = ref[rows * (c % CUTS) : rows * (c % CUTS) + rows, :]
        for a, part in enumerate((v_ref[...], part_ref[0], part_ref[1])):
            scores = dot_nt(block, part)
            best[a] = jnp.maximum(best[a], jnp.max(scores.reshape(rows // 8, 8, NC * 4), axis=0))
    for a in range(3):
        acc_ref[a] = best[a]


def best_kernel(
    place_ref, own_ref, mate_ref, v_in, acc_ref, post_ref, out_ref, prior_ref, part_ref, sems
):
    fetch([(v_in, part_ref)], sems)
    prior_ref[...] = own_ref[:16, :]
    best = scan_blocks(own_ref, part_ref[...], jnp.full((8, NC * 4), LOW, F32))
    accs = [acc_ref[0], acc_ref[1], scan_blocks(mate_ref, part_ref[...], best), acc_ref[2]]
    x, core = place_ref[0], place_ref[1]
    wide = (NC, NC * 4)
    mine = iota(wide, 1) // 4 == iota(wide, 0)
    lane = iota((NC, 128), 1)
    best = jnp.full((NC, 128), LOW, F32)
    for a in range(NX):
        top = jnp.max(accs[a], axis=0, keepdims=True)
        spread = jnp.where(mine, jnp.broadcast_to(top, wide), LOW)
        folded = jnp.maximum(spread[:, :128], spread[:, 128:])
        for shift in (64, 32, 16, 8, 4):
            folded = jnp.maximum(folded, pltpu.roll(folded, shift, 1))
        group = lax.rem(x + NX - a, NX) * NK + core
        best = jnp.where(lane // 4 == group, folded, best)
    out_ref[...] = best


def final_kernel(in_ref, table_ref, best_ref, score_ref):
    got = in_ref[...]
    lane = iota((NC, 128), 1)
    src = iota((NC, 128), 0)
    n = NZ * NK
    pair = jnp.maximum(
        jnp.maximum(got[:n], got[n : 2 * n]), jnp.maximum(got[2 * n : 3 * n], got[3 * n :])
    )
    tops = jnp.concatenate(
        [
            jnp.broadcast_to(jnp.max(pair[NK * z : NK * z + NK], axis=0, keepdims=True), (16, 128))
            for z in range(NZ)
        ],
        axis=0,
    )
    p = iota((128, 128), 0)
    best = jnp.full((1, V), LOW, F32)
    for x in range(NX):
        slot = (x * NK + (p // 8) % NK) * 4 + p % 4
        value = jnp.max(jnp.where(iota((128, 128), 1) == slot, tops, LOW), axis=1, keepdims=True)
        table = table_ref[128 * x : 128 * x + 128, :V].astype(F32)
        best = jnp.maximum(best, jnp.max(jnp.where(table > 0.5, value, LOW), axis=0, keepdims=True))
    best_ref[...] = best
    vals = jnp.where((lane >= 32) & (lane < 36), got, 0.0).astype(BF)
    total = jnp.zeros((8, 128), F32)
    pick = iota((8, 128), 0)
    at = iota((8, 128), 1)
    for t in range(2):
        chosen = one_hot(at == 32 + 2 * t + pick)
        rows = dot_nt(chosen, vals).astype(BF)
        total = total + dot(rows, one_hot(lane == src * 2 + t))
    score_ref[...] = total[:2].astype(BF)


def vm():
    return pl.BlockSpec(memory_space=pltpu.VMEM)


def sm():
    return pl.BlockSpec(memory_space=pltpu.SMEM)


def params(mib=28):
    return pltpu.CompilerParams(vmem_limit_bytes=mib * MIB)


def shards(
    vectors,
    centroids,
    postings,
    fill,
    assign,
    split_posts,
    split_members,
    neigh_post,
    neigh_row,
    neigh_split,
    neigh_dest,
):
    place = jnp.stack([lax.axis_index("x"), lax.axis_index("core")]).astype(I32)
    npost, nrow, nsplit, ndest = (
        a.reshape(1, NB) for a in (neigh_post, neigh_row, neigh_split, neigh_dest)
    )
    one = lambda *shape: pl.BlockSpec(shape, lambda i: (0,) * len(shape))
    hbm = pl.BlockSpec(memory_space=pl.ANY)
    packed, table = pl.pallas_call(
        pack_kernel,
        out_shape=(
            jax.ShapeDtypeStruct((NC * 8, P8), BF),
            jax.ShapeDtypeStruct((NC * 8, 128), BF),
        ),
        grid=(1,),
        in_specs=[one(V, D), one(POSTS, HEAD, D), one(1, V), one(1, NB), one(1, NB), one(1, NB)],
        out_specs=(one(NC * 8, P8), one(NC * 8, 128)),
        compiler_params=params(60),
        name="pack_rows",
    )(vectors, postings, assign.reshape(1, V), npost, nrow, ndest)
    held, packed = lax.optimization_barrier((centroids, packed))
    mate = lax.ppermute(held, "core", [(0, 1), (1, 0)])
    got = lax.all_to_all(packed.reshape(NC, 8, P8), CENT, 0, 0, tiled=True).reshape(NC * 8, P8)
    share = pl.pallas_call(
        share_kernel,
        out_shape=jax.ShapeDtypeStruct((NC * 4, D), BF),
        in_specs=[vm()],
        out_specs=vm(),
        compiler_params=params(),
        cost_estimate=pl.CostEstimate(flops=2 * 10**10, bytes_accessed=0, transcendentals=0),
        name="share_rows",
    )(got)
    parts = {a: lax.ppermute(share, "x", [(i, (i + a) % NX) for i in range(NX)]) for a in (1, 3)}
    spread = pl.pallas_call(
        spread_kernel,
        out_shape=jax.ShapeDtypeStruct((NY, V, W), BF),
        in_specs=[vm(), vm()],
        out_specs=pl.BlockSpec(memory_space=pltpu.HBM),
        scratch_shapes=[pltpu.VMEM((V, W), BF), pltpu.SemaphoreType.DMA((NY,))],
        compiler_params=params(),
        cost_estimate=pl.CostEstimate(flops=2 * 10**10, bytes_accessed=0, transcendentals=0),
        name="spread_rows",
    )(got, share)
    later, spread = lax.optimization_barrier((share, spread))
    parts[2] = lax.ppermute(later, "x", [(i, (i + 2) % NX) for i in range(NX)])
    gathered = lax.all_to_all(spread, "y", 0, 0, tiled=True).reshape(NY * V, W)
    moved_rows = pl.pallas_call(
        moved_kernel,
        out_shape=jax.ShapeDtypeStruct((NC * 2, D), BF),
        in_specs=[vm()],
        out_specs=vm(),
        compiler_params=params(),
        name="moved_rows",
    )(got)

    def cost(count):
        work = int(2 * 4096 * 256 * D * count)
        return pl.CostEstimate(flops=work, bytes_accessed=2 * 4096 * D, transcendentals=0)

    first, near, mate = pl.pallas_call(
        first_kernel,
        out_shape=(
            jax.ShapeDtypeStruct((NX - 1, 8, NC * 4), F32),
            jax.ShapeDtypeStruct((2048, D), BF),
            jax.ShapeDtypeStruct((2048, D), BF),
        ),
        in_specs=[hbm, hbm, vm(), hbm, hbm],
        out_specs=(vm(), vm(), vm()),
        scratch_shapes=[pltpu.VMEM((2, NC * 4, D), BF), pltpu.SemaphoreType.DMA((2 + 2 * CUTS,))],
        compiler_params=params(44),
        cost_estimate=cost(3),
        name="best_of_three",
    )(centroids, mate, share, parts[1], parts[3])
    best, priors = pl.pallas_call(
        best_kernel,
        out_shape=(jax.ShapeDtypeStruct((NC, 128), F32), jax.ShapeDtypeStruct((16, D), BF)),
        in_specs=[sm(), vm(), vm(), hbm, vm(), vm()],
        out_specs=(vm(), vm()),
        scratch_shapes=[pltpu.VMEM((NC * 4, D), BF), pltpu.SemaphoreType.DMA((1,))],
        compiler_params=params(),
        cost_estimate=cost(2.6),
        name="best_scores",
    )(place, near, mate, parts[2], first, postings)
    split_centers, sending = pl.pallas_call(
        split_kernel,
        out_shape=(
            jax.ShapeDtypeStruct((2, 2, D), F32),
            jax.ShapeDtypeStruct((NC, 128), F32),
        ),
        in_specs=[sm(), sm()] + [vm()] * 9,
        out_specs=(vm(), vm()),
        compiler_params=params(),
        name="split_scores",
    )(
        fill, split_posts, gathered, split_members, npost, nrow, nsplit, ndest, postings, priors, best
    )
    postings_out, new_fill = pl.pallas_call(
        append_kernel,
        out_shape=(
            jax.ShapeDtypeStruct((POSTS, ROWS, D), BF),
            jax.ShapeDtypeStruct((POSTS,), I32),
        ),
        in_specs=[sm(), vm(), vm()],
        out_specs=(vm(), sm()),
        compiler_params=params(),
        name="append_rows",
    )(fill, gathered, postings)
    back = lax.all_to_all(sending.reshape(NC, 1, 128), CENT, 0, 0, tiled=True).reshape(NC, 128)
    best_score, moved_scores = pl.pallas_call(
        final_kernel,
        out_shape=(jax.ShapeDtypeStruct((1, V), F32), jax.ShapeDtypeStruct((2, 2 * NC), BF)),
        in_specs=[vm(), vm()],
        out_specs=(vm(), vm()),
        compiler_params=params(),
        name="last_step",
    )(back, table)
    return (
        best_score.reshape(V), postings_out, new_fill, split_centers, moved_rows, moved_scores
    )


def solution(mesh):
    fine = Mesh(mesh.devices.reshape(NY, NX, NZ, NK), ("y", "x", "z", "core"))
    both = ("y",) + CENT
    return jax.shard_map(
        shards,
        mesh=fine,
        in_specs=(
            P(both, None),
            P(CENT, None),
            P(CENT, None, None),
            P(CENT),
            P(both),
            P(CENT),
            P(CENT, None),
            P(both),
            P(both),
            P(both),
            P(both),
        ),
        out_specs=(
            P(both),
            P(CENT, None, None),
            P(CENT),
            P(CENT, None, None),
            P(both, None),
            P(None, both),
        ),
        check_vma=False,
    )
```

```python
import functools

import jax
import jax.numpy as jnp
from jax import lax
from jax.experimental import pallas as pl
from jax.experimental.pallas import tpu as pltpu
from jax.sharding import Mesh, PartitionSpec as P

D = 768
W = 896
ROWS = 128
HEAD = 32
ITERS = 2
NX, NY, NZ, NK = 4, 8, 8, 2
NC = NX * NZ * NK
V = 32
NB = 64
POSTS = 4
CENT = ("x", "z", "core")
LOW = -3.0e38
HALF = D // 2
P8 = HALF + 256
F32 = jnp.float32
BF = jnp.bfloat16
I32 = jnp.int32
MIB = 1024 * 1024


def iota(shape, dim):
    return lax.broadcasted_iota(I32, shape, dim)


def as_column(row):
    n = row.shape[1]
    eye = iota((n, n), 0) == iota((n, n), 1)
    return jnp.sum(jnp.where(eye, jnp.broadcast_to(row, (n, n)), 0), axis=1, keepdims=True)


def earlier_equal(row):
    n = row.shape[1]
    same = (as_column(row) == row) & (iota((n, n), 0) < iota((n, n), 1))
    return jnp.sum(same.astype(I32), axis=0, keepdims=True)


def one_hot(mask):
    return jnp.where(mask, 1.0, 0.0).astype(BF)


def dot(a, b):
    return jnp.dot(a, b, preferred_element_type=F32)


def dot_nt(a, b):
    return lax.dot_general(a, b, (((1,), (1,)), ((), ())), preferred_element_type=F32)


def fetch(pairs, sems):
    copies = [pltpu.make_async_copy(src, dst, sems.at[i]) for i, (src, dst) in enumerate(pairs)]
    for copy in copies:
        copy.start()
    for copy in copies:
        copy.wait()


def pack_kernel(vec_ref, head_ref, assign_ref, npost_ref, nrow_ref, ndest_ref, out_ref, table_ref):
    n = NC * 8
    assign = assign_ref[...]
    dest = assign // POSTS
    zdest = (dest // NK) % NZ
    place = earlier_equal(dest)

    ones = jnp.ones((V, 128), BF)

    def routed(count, per):
        p = iota((count, V), 0)
        to, t = p // per, p % 4
        return (dest == to) & (place == t), (zdest != (to // NK) % NZ)

    named, other = routed(n, 8)
    small, _ = routed(NC * 4, 4)
    free = (1.0 - dot(one_hot(small), ones)).astype(BF)
    p, c = iota((n, NC * 4), 0), iota((n, NC * 4), 1)
    pd, cd = p // 8, c // 4
    slot = ((pd // (NZ * NK)) * NK + pd % NK) * 4 + p % 4
    cslot = ((cd // (NZ * NK)) * NK + cd % NK) * 4 + c % 4
    before = one_hot(((pd // NK) % NZ == (cd // NK) % NZ) & (cslot < slot))
    free_rank = dot(before, free)[:, :V]
    upper = one_hot(iota((V, V), 0) < iota((V, V), 1))
    rest_rank = dot(one_hot(other), upper)
    taken = dot(one_hot(named), ones)[:, :V]
    share = named | (other & (taken < 0.5) & (free_rank == rest_rank))
    low_half = iota((n, V), 0) % 8 < 4
    table = one_hot(share & low_half)
    table_ref[:, :V] = table
    out_ref[:, :HALF] = (
        dot(table, vec_ref[:, :HALF]) + dot(one_hot(share & ~low_half), vec_ref[:, HALF:])
    ).astype(BF)

    ndest = ndest_ref[...]
    nplace = earlier_equal(ndest)
    picks = one_hot(npost_ref[...] * HEAD + nrow_ref[...] == iota((POSTS * HEAD, NB), 0))
    head = head_ref[...].reshape(POSTS * HEAD, D)
    p, c = iota((n, 6 * NC), 0), iota((n, 6 * NC), 1)
    spread = one_hot((p // 8 == c % NC) & (p % 8 == c // NC))
    post = as_column(assign) % POSTS + 1
    mark = jnp.where(iota((V, 128), 1) == as_column(place), post, 0).astype(F32).astype(BF)
    sixth = one_hot((iota((n, V), 0) // 8 == dest) & (iota((n, V), 0) % 8 == 6))
    for t in range(2):
        chosen = one_hot((ndest == iota((NC, NB), 0)) & (nplace == t))
        rows = dot(dot_nt(chosen, picks).astype(BF), head).astype(BF)
        stack = jnp.concatenate([rows[:, 128 * k : 128 * k + 128] for k in range(6)], axis=0)
        tile = dot(spread, stack)
        if t == 0:
            tile = tile + dot(sixth, mark)
        out_ref[:, HALF + 128 * t : HALF + 128 * t + 128] = tile.astype(BF)


def share_kernel(in_ref, share_ref):
    n = NC * 8
    p, i = iota((NC * 4, n), 1), iota((NC * 4, n), 0)
    first = (i // 4) * 8 + i % 4
    rows = in_ref[:, :HALF]
    share_ref[:, :HALF] = dot(one_hot(p == first), rows).astype(BF)
    share_ref[:, HALF:] = dot(one_hot(p == first + 4), rows).astype(BF)


def moved_kernel(in_ref, moved_ref):
    n = NC * 8
    tiles = in_ref[:, HALF:]
    p, i = iota((NC * 2, n), 1), iota((NC * 2, n), 0)
    odd = iota((NC * 2, 128), 0) % 2 == 1
    for k in range(6):
        both = dot(one_hot(p == (i // 2) * 8 + k), tiles)
        moved_ref[:, 128 * k : 128 * k + 128] = jnp.where(odd, both[:, 128:], both[:, :128]).astype(BF)


def spread_kernel(in_ref, share_ref, out_ref, buf_ref, sems):
    n = NC * 8
    p, d = iota((NC, n), 1), iota((NC, n), 0)
    marks = dot(one_hot(p == d * 8 + 6), in_ref[:, HALF : HALF + 128]).astype(BF)
    first = dot_nt(one_hot(iota((8, 128), 1) == 0), marks)
    upper = one_hot(iota((NC, NC), 0) < iota((NC, NC), 1))
    valid = one_hot(first > 0.5)
    rank = dot(valid, upper).astype(BF)
    m = NC * 4
    widen = one_hot(iota((NC, m), 0) == iota((NC, m), 1) // 4)
    valid, rank = dot(valid, widen)[:1], dot(rank, widen)[:1].astype(I32)
    t = iota((V, m), 1) % 4
    hit = one_hot((valid > 0.5) & (t < 2) & (2 * rank + t == iota((V, m), 0)))
    tall = one_hot(iota((m, NC), 1) == iota((m, NC), 0) // 4)
    lane = iota((m, 128), 1)
    mine = jnp.where(lane == iota((m, 128), 0) % 4, dot(tall, marks), 0.0)
    post = jnp.sum(mine, axis=1, keepdims=True)
    buf_ref[:, :D] = dot(hit, share_ref[...]).astype(BF)
    buf_ref[:, D:] = dot(hit, jnp.where(lane == 0, post, 0.0).astype(BF)).astype(BF)
    copies = [pltpu.make_async_copy(buf_ref, out_ref.at[g], sems.at[g]) for g in range(NY)]
    for copy in copies:
        copy.start()
    for copy in copies:
        copy.wait()


def ranks(got, posts):
    n = NY * V
    mark = dot_nt(one_hot(iota((8, 128), 1) == 0), got).astype(I32)
    row = iota((8, n), 0)
    wanted = jnp.zeros((8, n), I32)
    for i, q in enumerate(posts):
        wanted = jnp.where(row == i, q + 1, wanted)
    match = mark == wanted
    upper = one_hot(iota((n, n), 0) < iota((n, n), 1))
    return match, dot(one_hot(match), upper).astype(I32)


def appended(match, rank, i, first, got, before):
    mine = match[i : i + 1]
    count = jnp.sum(mine.astype(I32))
    table = one_hot(mine & (iota((ROWS, NY * V), 0) == first + rank[i : i + 1]))
    line = iota((ROWS, 1), 0)
    hit = (line >= first) & (line < first + count)
    return jnp.where(hit, dot(table, got), before), first + count


def append_kernel(fill_ref, got_ref, post_ref, out_ref, count_ref):
    match, rank = ranks(got_ref[:, D:], range(POSTS))
    for q in range(POSTS):
        rows, count = appended(
            match, rank, q, fill_ref[q], got_ref[:, :D], post_ref[q].astype(F32)
        )
        out_ref[q] = rows.astype(BF)
        count_ref[q] = count


def split_kernel(
    fill_ref, split_ref, got_ref, member_ref, npost_ref, nrow_ref, nsplit_ref, ndest_ref, post_ref, own_ref,
    best_ref, centers_ref, send_ref,
):
    line = iota((ROWS, 1), 0)
    head = post_ref[:, :HEAD, :].reshape(POSTS * HEAD, D).astype(F32)
    members = member_ref[...].astype(F32)
    eye = iota((ROWS, ROWS), 0) == iota((ROWS, ROWS), 1)
    lane = iota((POSTS * HEAD, 128), 1)
    ndest = ndest_ref[...]
    nplace = earlier_equal(ndest)
    nsplit = nsplit_ref[...]
    picks = one_hot(npost_ref[...] * HEAD + nrow_ref[...] == iota((POSTS * HEAD, NB), 0))
    to = iota((NC, NB), 0)
    own = own_ref[:16, :].astype(F32)
    posts = [jnp.maximum(split_ref[s], 0) for s in range(2)]
    match, rank = ranks(got_ref[:, D:], posts)
    sent = jnp.zeros((NC, 128), F32)
    for s in range(2):
        q = posts[s]
        alive = jnp.where(split_ref[s] >= 0, 1.0, 0.0).astype(F32)
        x, filled = appended(match, rank, s, fill_ref[q], got_ref[:, :D], post_ref[q].astype(F32))
        prior = jnp.sum(jnp.where(iota(own.shape, 0) == q, own, 0.0), axis=0, keepdims=True)
        mask = jnp.where(line < filled, 1.0, 0.0).astype(F32)
        weights = jnp.sum(jnp.where(eye, members[s : s + 1], 0.0), axis=1, keepdims=True)

        def update(weights):
            w1, w2 = mask * weights, mask * (1.0 - weights)
            s1 = jnp.sum(w1 * x, axis=0, keepdims=True) + prior
            s2 = jnp.sum(w2 * x, axis=0, keepdims=True) + prior
            t1 = jnp.sum(w1, axis=0, keepdims=True) + 1.0
            t2 = jnp.sum(w2, axis=0, keepdims=True) + 1.0
            return s1 / t1, s2 / t2

        a1, a2 = update(weights)
        for _ in range(ITERS):
            far = jnp.sum(jnp.square(x - a2), axis=1, keepdims=True) - jnp.sum(
                jnp.square(x - a1), axis=1, keepdims=True
            )
            a1, a2 = update(jax.nn.sigmoid(0.125 * far))
        a1, a2 = a1 * alive, a2 * alive
        centers_ref[s, 0:1, :] = a1
        centers_ref[s, 1:2, :] = a2
        c1 = jnp.sum(head * a1, axis=1, keepdims=True)
        c2 = jnp.sum(head * a2, axis=1, keepdims=True)
        for t in range(2):
            where_to = one_hot((ndest == to) & (nplace == t) & (nsplit == s))
            table = dot_nt(where_to, picks).astype(BF)
            values = jnp.where(lane == 32 + 2 * t, c1, jnp.where(lane == 33 + 2 * t, c2, 0.0))
            sent = sent + dot(table, values.astype(BF))
    send_ref[...] = jnp.where(iota((NC, 128), 1) < V, best_ref[...], sent)


BLOCK = 1024


def scan_blocks(ref, part, best):
    for i in range(2048 // BLOCK):
        scores = dot_nt(ref[BLOCK * i : BLOCK * i + BLOCK, :], part)
        best = jnp.maximum(best, jnp.max(scores.reshape(BLOCK // 8, 8, NC * 4), axis=0))
    return best


def first_kernel(own_ref, mate_in, v_ref, v1_in, v2_in, acc_ref, near_ref, mate_ref, part_ref, sems):
    pairs = ((v1_in, part_ref.at[0]), (v2_in, part_ref.at[1]), (mate_in, mate_ref), (own_ref, near_ref))
    copies = [pltpu.make_async_copy(src, dst, sems.at[i]) for i, (src, dst) in enumerate(pairs)]
    for copy in copies:
        copy.start()
    blank = jnp.full((8, NC * 4), LOW, F32)
    acc_ref[0] = scan_blocks(own_ref, v_ref[...], blank)
    copies[0].wait()
    acc_ref[1] = scan_blocks(own_ref, part_ref[0], blank)
    copies[1].wait()
    acc_ref[2] = scan_blocks(own_ref, part_ref[1], blank)
    copies[2].wait()
    acc_ref[0] = scan_blocks(mate_ref, v_ref[...], acc_ref[0])
    acc_ref[1] = scan_blocks(mate_ref, part_ref[0], acc_ref[1])
    acc_ref[2] = scan_blocks(mate_ref, part_ref[1], acc_ref[2])
    copies[3].wait()


def best_kernel(
    place_ref, own_ref, mate_ref, v_in, acc_ref, post_ref, out_ref, prior_ref, part_ref, sems
):
    fetch([(v_in, part_ref)], sems)
    prior_ref[...] = own_ref[:16, :]
    best = scan_blocks(own_ref, part_ref[...], jnp.full((8, NC * 4), LOW, F32))
    accs = [acc_ref[0], acc_ref[1], scan_blocks(mate_ref, part_ref[...], best), acc_ref[2]]
    x, core = place_ref[0], place_ref[1]
    wide = (NC, NC * 4)
    mine = iota(wide, 1) // 4 == iota(wide, 0)
    lane = iota((NC, 128), 1)
    best = jnp.full((NC, 128), LOW, F32)
    for a in range(NX):
        top = jnp.max(accs[a], axis=0, keepdims=True)
        spread = jnp.where(mine, jnp.broadcast_to(top, wide), LOW)
        folded = jnp.maximum(spread[:, :128], spread[:, 128:])
        for shift in (64, 32, 16, 8, 4):
            folded = jnp.maximum(folded, pltpu.roll(folded, shift, 1))
        group = lax.rem(x + NX - a, NX) * NK + core
        best = jnp.where(lane // 4 == group, folded, best)
    out_ref[...] = best


def final_kernel(in_ref, table_ref, best_ref, score_ref):
    got = in_ref[...]
    lane = iota((NC, 128), 1)
    src = iota((NC, 128), 0)
    n = NZ * NK
    pair = jnp.maximum(
        jnp.maximum(got[:n], got[n : 2 * n]), jnp.maximum(got[2 * n : 3 * n], got[3 * n :])
    )
    tops = jnp.concatenate(
        [
            jnp.broadcast_to(jnp.max(pair[NK * z : NK * z + NK], axis=0, keepdims=True), (16, 128))
            for z in range(NZ)
        ],
        axis=0,
    )
    p = iota((128, 128), 0)
    best = jnp.full((1, V), LOW, F32)
    for x in range(NX):
        slot = (x * NK + (p // 8) % NK) * 4 + p % 4
        value = jnp.max(jnp.where(iota((128, 128), 1) == slot, tops, LOW), axis=1, keepdims=True)
        table = table_ref[128 * x : 128 * x + 128, :V].astype(F32)
        best = jnp.maximum(best, jnp.max(jnp.where(table > 0.5, value, LOW), axis=0, keepdims=True))
    best_ref[...] = best
    vals = jnp.where((lane >= 32) & (lane < 36), got, 0.0).astype(BF)
    total = jnp.zeros((8, 128), F32)
    pick = iota((8, 128), 0)
    at = iota((8, 128), 1)
    for t in range(2):
        chosen = one_hot(at == 32 + 2 * t + pick)
        rows = dot_nt(chosen, vals).astype(BF)
        total = total + dot(rows, one_hot(lane == src * 2 + t))
    score_ref[...] = total[:2].astype(BF)


def vm():
    return pl.BlockSpec(memory_space=pltpu.VMEM)


def sm():
    return pl.BlockSpec(memory_space=pltpu.SMEM)


def params(mib=28):
    return pltpu.CompilerParams(vmem_limit_bytes=mib * MIB)


def shards(
    vectors,
    centroids,
    postings,
    fill,
    assign,
    split_posts,
    split_members,
    neigh_post,
    neigh_row,
    neigh_split,
    neigh_dest,
):
    place = jnp.stack([lax.axis_index("x"), lax.axis_index("core")]).astype(I32)
    npost, nrow, nsplit, ndest = (
        a.reshape(1, NB) for a in (neigh_post, neigh_row, neigh_split, neigh_dest)
    )
    one = lambda *shape: pl.BlockSpec(shape, lambda i: (0,) * len(shape))
    hbm = pl.BlockSpec(memory_space=pl.ANY)
    packed, table = pl.pallas_call(
        pack_kernel,
        out_shape=(
            jax.ShapeDtypeStruct((NC * 8, P8), BF),
            jax.ShapeDtypeStruct((NC * 8, 128), BF),
        ),
        grid=(1,),
        in_specs=[one(V, D), one(POSTS, HEAD, D), one(1, V), one(1, NB), one(1, NB), one(1, NB)],
        out_specs=(one(NC * 8, P8), one(NC * 8, 128)),
        compiler_params=params(60),
        name="pack_rows",
    )(vectors, postings, assign.reshape(1, V), npost, nrow, ndest)
    held, packed = lax.optimization_barrier((centroids, packed))
    mate = lax.ppermute(held, "core", [(0, 1), (1, 0)])
    got = lax.all_to_all(packed.reshape(NC, 8, P8), CENT, 0, 0, tiled=True).reshape(NC * 8, P8)
    share = pl.pallas_call(
        share_kernel,
        out_shape=jax.ShapeDtypeStruct((NC * 4, D), BF),
        in_specs=[vm()],
        out_specs=vm(),
        compiler_params=params(),
        cost_estimate=pl.CostEstimate(flops=2 * 10**10, bytes_accessed=0, transcendentals=0),
        name="share_rows",
    )(got)
    parts = {a: lax.ppermute(share, "x", [(i, (i + a) % NX) for i in range(NX)]) for a in (2, 1, 3)}
    spread = pl.pallas_call(
        spread_kernel,
        out_shape=jax.ShapeDtypeStruct((NY, V, W), BF),
        in_specs=[vm(), vm()],
        out_specs=pl.BlockSpec(memory_space=pltpu.HBM),
        scratch_shapes=[pltpu.VMEM((V, W), BF), pltpu.SemaphoreType.DMA((NY,))],
        compiler_params=params(),
        cost_estimate=pl.CostEstimate(flops=2 * 10**10, bytes_accessed=0, transcendentals=0),
        name="spread_rows",
    )(got, share)
    gathered = lax.all_to_all(spread, "y", 0, 0, tiled=True).reshape(NY * V, W)
    moved_rows = pl.pallas_call(
        moved_kernel,
        out_shape=jax.ShapeDtypeStruct((NC * 2, D), BF),
        in_specs=[vm()],
        out_specs=vm(),
        compiler_params=params(),
        name="moved_rows",
    )(got)

    def cost(count):
        work = 2 * 4096 * 256 * D * count
        return pl.CostEstimate(flops=work, bytes_accessed=2 * 4096 * D, transcendentals=0)

    first, near, mate = pl.pallas_call(
        first_kernel,
        out_shape=(
            jax.ShapeDtypeStruct((NX - 1, 8, NC * 4), F32),
            jax.ShapeDtypeStruct((2048, D), BF),
            jax.ShapeDtypeStruct((2048, D), BF),
        ),
        in_specs=[vm(), hbm, vm(), hbm, hbm],
        out_specs=(vm(), vm(), vm()),
        scratch_shapes=[pltpu.VMEM((2, NC * 4, D), BF), pltpu.SemaphoreType.DMA((4,))],
        compiler_params=params(),
        cost_estimate=cost(3),
        name="best_of_three",
    )(centroids, mate, share, parts[1], parts[3])
    best, priors = pl.pallas_call(
        best_kernel,
        out_shape=(jax.ShapeDtypeStruct((NC, 128), F32), jax.ShapeDtypeStruct((16, D), BF)),
        in_specs=[sm(), vm(), vm(), hbm, vm(), vm()],
        out_specs=(vm(), vm()),
        scratch_shapes=[pltpu.VMEM((NC * 4, D), BF), pltpu.SemaphoreType.DMA((1,))],
        compiler_params=params(),
        cost_estimate=cost(1),
        name="best_scores",
    )(place, near, mate, parts[2], first, postings)
    split_centers, sending = pl.pallas_call(
        split_kernel,
        out_shape=(
            jax.ShapeDtypeStruct((2, 2, D), F32),
            jax.ShapeDtypeStruct((NC, 128), F32),
        ),
        in_specs=[sm(), sm()] + [vm()] * 9,
        out_specs=(vm(), vm()),
        compiler_params=params(),
        name="split_scores",
    )(
        fill, split_posts, gathered, split_members, npost, nrow, nsplit, ndest, postings, priors, best
    )
    postings_out, new_fill = pl.pallas_call(
        append_kernel,
        out_shape=(
            jax.ShapeDtypeStruct((POSTS, ROWS, D), BF),
            jax.ShapeDtypeStruct((POSTS,), I32),
        ),
        in_specs=[sm(), vm(), vm()],
        out_specs=(vm(), sm()),
        compiler_params=params(),
        name="append_rows",
    )(fill, gathered, postings)
    back = lax.all_to_all(sending.reshape(NC, 1, 128), CENT, 0, 0, tiled=True).reshape(NC, 128)
    best_score, moved_scores = pl.pallas_call(
        final_kernel,
        out_shape=(jax.ShapeDtypeStruct((1, V), F32), jax.ShapeDtypeStruct((2, 2 * NC), BF)),
        in_specs=[vm(), vm()],
        out_specs=(vm(), vm()),
        compiler_params=params(),
        name="last_step",
    )(back, table)
    return (
        best_score.reshape(V), postings_out, new_fill, split_centers, moved_rows, moved_scores
    )


def solution(mesh):
    fine = Mesh(mesh.devices.reshape(NY, NX, NZ, NK), ("y", "x", "z", "core"))
    both = ("y",) + CENT
    return jax.shard_map(
        shards,
        mesh=fine,
        in_specs=(
            P(both, None),
            P(CENT, None),
            P(CENT, None, None),
            P(CENT),
            P(both),
            P(CENT),
            P(CENT, None),
            P(both),
            P(both),
            P(both),
            P(both),
        ),
        out_specs=(
            P(both),
            P(CENT, None, None),
            P(CENT),
            P(CENT, None, None),
            P(both, None),
            P(None, both),
        ),
        check_vma=False,
    )
```

```python
import functools

import jax
import jax.numpy as jnp
from jax import lax
from jax.experimental import pallas as pl
from jax.experimental.pallas import tpu as pltpu
from jax.sharding import Mesh, PartitionSpec as P

D = 768
W = 896
ROWS = 128
HEAD = 32
ITERS = 2
NX, NY, NZ, NK = 4, 8, 8, 2
NC = NX * NZ * NK
V = 32
NB = 64
POSTS = 4
CENT = ("x", "z", "core")
LOW = -3.0e38
HALF = D // 2
P8 = HALF + 256
F32 = jnp.float32
BF = jnp.bfloat16
I32 = jnp.int32
MIB = 1024 * 1024


def iota(shape, dim):
    return lax.broadcasted_iota(I32, shape, dim)


def as_column(row):
    n = row.shape[1]
    eye = iota((n, n), 0) == iota((n, n), 1)
    return jnp.sum(jnp.where(eye, jnp.broadcast_to(row, (n, n)), 0), axis=1, keepdims=True)


def earlier_equal(row):
    n = row.shape[1]
    same = (as_column(row) == row) & (iota((n, n), 0) < iota((n, n), 1))
    return jnp.sum(same.astype(I32), axis=0, keepdims=True)


def one_hot(mask):
    return jnp.where(mask, 1.0, 0.0).astype(BF)


def dot(a, b):
    return jnp.dot(a, b, preferred_element_type=F32)


def dot_nt(a, b):
    return lax.dot_general(a, b, (((1,), (1,)), ((), ())), preferred_element_type=F32)


def fetch(pairs, sems):
    copies = [pltpu.make_async_copy(src, dst, sems.at[i]) for i, (src, dst) in enumerate(pairs)]
    for copy in copies:
        copy.start()
    for copy in copies:
        copy.wait()


def pack_kernel(
    vec_in, post_in, assign_in, npost_in, nrow_in, ndest_in, out_hbm, table_ref,
    vec_ref, head_ref, assign_ref, npost_ref, nrow_ref, ndest_ref, out_ref, sems,
):
    pairs = (
        (assign_in, assign_ref), (vec_in, vec_ref), (ndest_in, ndest_ref), (npost_in, npost_ref),
        (nrow_in, nrow_ref), (post_in.at[:, :HEAD, :], head_ref),
        (out_ref.at[:, :HALF], out_hbm.at[:, :HALF]), (out_ref.at[:, HALF:], out_hbm.at[:, HALF:]),
    )
    copies = [pltpu.make_async_copy(src, dst, sems.at[i]) for i, (src, dst) in enumerate(pairs)]
    for copy in copies[:6]:
        copy.start()
    copies[0].wait()
    n = NC * 8
    assign = assign_ref[...]
    dest = assign // POSTS
    zdest = (dest // NK) % NZ
    place = earlier_equal(dest)

    ones = jnp.ones((V, 128), BF)

    def routed(count, per):
        p = iota((count, V), 0)
        to, t = p // per, p % 4
        return (dest == to) & (place == t), (zdest != (to // NK) % NZ)

    named, other = routed(n, 8)
    small, _ = routed(NC * 4, 4)
    free = (1.0 - dot(one_hot(small), ones)).astype(BF)
    p, c = iota((n, NC * 4), 0), iota((n, NC * 4), 1)
    pd, cd = p // 8, c // 4
    slot = ((pd // (NZ * NK)) * NK + pd % NK) * 4 + p % 4
    cslot = ((cd // (NZ * NK)) * NK + cd % NK) * 4 + c % 4
    before = one_hot(((pd // NK) % NZ == (cd // NK) % NZ) & (cslot < slot))
    free_rank = dot(before, free)[:, :V]
    upper = one_hot(iota((V, V), 0) < iota((V, V), 1))
    rest_rank = dot(one_hot(other), upper)
    taken = dot(one_hot(named), ones)[:, :V]
    share = named | (other & (taken < 0.5) & (free_rank == rest_rank))
    low_half = iota((n, V), 0) % 8 < 4
    table = one_hot(share & low_half)
    table_ref[:, :V] = table
    copies[1].wait()
    out_ref[:, :HALF] = (
        dot(table, vec_ref[:, :HALF]) + dot(one_hot(share & ~low_half), vec_ref[:, HALF:])
    ).astype(BF)
    copies[6].start()
    for copy in copies[2:6]:
        copy.wait()
    ndest = ndest_ref[...]
    nplace = earlier_equal(ndest)
    picks = one_hot(npost_ref[...] * HEAD + nrow_ref[...] == iota((POSTS * HEAD, NB), 0))
    head = head_ref[...].reshape(POSTS * HEAD, D)
    p, c = iota((n, 6 * NC), 0), iota((n, 6 * NC), 1)
    spread = one_hot((p // 8 == c % NC) & (p % 8 == c // NC))
    post = as_column(assign) % POSTS + 1
    mark = jnp.where(iota((V, 128), 1) == as_column(place), post, 0).astype(F32).astype(BF)
    sixth = one_hot((iota((n, V), 0) // 8 == dest) & (iota((n, V), 0) % 8 == 6))
    for t in range(2):
        chosen = one_hot((ndest == iota((NC, NB), 0)) & (nplace == t))
        rows = dot(dot_nt(chosen, picks).astype(BF), head).astype(BF)
        stack = jnp.concatenate([rows[:, 128 * k : 128 * k + 128] for k in range(6)], axis=0)
        tile = dot(spread, stack)
        if t == 0:
            tile = tile + dot(sixth, mark)
        out_ref[:, HALF + 128 * t : HALF + 128 * t + 128] = tile.astype(BF)
    copies[7].start()
    copies[6].wait()
    copies[7].wait()


def share_kernel(in_ref, share_ref):
    n = NC * 8
    p, i = iota((NC * 4, n), 1), iota((NC * 4, n), 0)
    first = (i // 4) * 8 + i % 4
    rows = in_ref[:, :HALF]
    share_ref[:, :HALF] = dot(one_hot(p == first), rows).astype(BF)
    share_ref[:, HALF:] = dot(one_hot(p == first + 4), rows).astype(BF)


def moved_kernel(in_ref, moved_ref):
    n = NC * 8
    tiles = in_ref[:, HALF:]
    p, i = iota((NC * 2, n), 1), iota((NC * 2, n), 0)
    odd = iota((NC * 2, 128), 0) % 2 == 1
    for k in range(6):
        both = dot(one_hot(p == (i // 2) * 8 + k), tiles)
        moved_ref[:, 128 * k : 128 * k + 128] = jnp.where(odd, both[:, 128:], both[:, :128]).astype(BF)


def spread_kernel(in_ref, share_ref, out_ref, buf_ref, sems):
    n = NC * 8
    p, d = iota((NC, n), 1), iota((NC, n), 0)
    marks = dot(one_hot(p == d * 8 + 6), in_ref[:, HALF : HALF + 128]).astype(BF)
    first = dot_nt(one_hot(iota((8, 128), 1) == 0), marks)
    upper = one_hot(iota((NC, NC), 0) < iota((NC, NC), 1))
    valid = one_hot(first > 0.5)
    rank = dot(valid, upper).astype(BF)
    m = NC * 4
    widen = one_hot(iota((NC, m), 0) == iota((NC, m), 1) // 4)
    valid, rank = dot(valid, widen)[:1], dot(rank, widen)[:1].astype(I32)
    t = iota((V, m), 1) % 4
    hit = one_hot((valid > 0.5) & (t < 2) & (2 * rank + t == iota((V, m), 0)))
    tall = one_hot(iota((m, NC), 1) == iota((m, NC), 0) // 4)
    lane = iota((m, 128), 1)
    mine = jnp.where(lane == iota((m, 128), 0) % 4, dot(tall, marks), 0.0)
    post = jnp.sum(mine, axis=1, keepdims=True)
    buf_ref[:, :D] = dot(hit, share_ref[...]).astype(BF)
    buf_ref[:, D:] = dot(hit, jnp.where(lane == 0, post, 0.0).astype(BF)).astype(BF)
    copies = [pltpu.make_async_copy(buf_ref, out_ref.at[g], sems.at[g]) for g in range(NY)]
    for copy in copies:
        copy.start()
    for copy in copies:
        copy.wait()


def ranks(got, posts):
    n = NY * V
    mark = dot_nt(one_hot(iota((8, 128), 1) == 0), got).astype(I32)
    row = iota((8, n), 0)
    wanted = jnp.zeros((8, n), I32)
    for i, q in enumerate(posts):
        wanted = jnp.where(row == i, q + 1, wanted)
    match = mark == wanted
    upper = one_hot(iota((n, n), 0) < iota((n, n), 1))
    return match, dot(one_hot(match), upper).astype(I32)


def appended(match, rank, i, first, got, before):
    mine = match[i : i + 1]
    count = jnp.sum(mine.astype(I32))
    table = one_hot(mine & (iota((ROWS, NY * V), 0) == first + rank[i : i + 1]))
    line = iota((ROWS, 1), 0)
    hit = (line >= first) & (line < first + count)
    return jnp.where(hit, dot(table, got), before), first + count


def append_kernel(fill_ref, got_ref, post_ref, out_ref, count_ref):
    match, rank = ranks(got_ref[:, D:], range(POSTS))
    for q in range(POSTS):
        rows, count = appended(
            match, rank, q, fill_ref[q], got_ref[:, :D], post_ref[q].astype(F32)
        )
        out_ref[q] = rows.astype(BF)
        count_ref[q] = count


def split_kernel(
    fill_ref, split_ref, got_ref, member_ref, npost_ref, nrow_ref, nsplit_ref, ndest_ref, post_ref, own_ref,
    best_ref, centers_ref, send_ref,
):
    line = iota((ROWS, 1), 0)
    head = post_ref[:, :HEAD, :].reshape(POSTS * HEAD, D).astype(F32)
    members = member_ref[...].astype(F32)
    eye = iota((ROWS, ROWS), 0) == iota((ROWS, ROWS), 1)
    lane = iota((POSTS * HEAD, 128), 1)
    ndest = ndest_ref[...]
    nplace = earlier_equal(ndest)
    nsplit = nsplit_ref[...]
    picks = one_hot(npost_ref[...] * HEAD + nrow_ref[...] == iota((POSTS * HEAD, NB), 0))
    to = iota((NC, NB), 0)
    own = own_ref[:16, :].astype(F32)
    posts = [jnp.maximum(split_ref[s], 0) for s in range(2)]
    match, rank = ranks(got_ref[:, D:], posts)
    sent = jnp.zeros((NC, 128), F32)
    for s in range(2):
        q = posts[s]
        alive = jnp.where(split_ref[s] >= 0, 1.0, 0.0).astype(F32)
        x, filled = appended(match, rank, s, fill_ref[q], got_ref[:, :D], post_ref[q].astype(F32))
        prior = jnp.sum(jnp.where(iota(own.shape, 0) == q, own, 0.0), axis=0, keepdims=True)
        mask = jnp.where(line < filled, 1.0, 0.0).astype(F32)
        weights = jnp.sum(jnp.where(eye, members[s : s + 1], 0.0), axis=1, keepdims=True)

        def update(weights):
            w1, w2 = mask * weights, mask * (1.0 - weights)
            s1 = jnp.sum(w1 * x, axis=0, keepdims=True) + prior
            s2 = jnp.sum(w2 * x, axis=0, keepdims=True) + prior
            t1 = jnp.sum(w1, axis=0, keepdims=True) + 1.0
            t2 = jnp.sum(w2, axis=0, keepdims=True) + 1.0
            return s1 / t1, s2 / t2

        a1, a2 = update(weights)
        for _ in range(ITERS):
            far = jnp.sum(jnp.square(x - a2), axis=1, keepdims=True) - jnp.sum(
                jnp.square(x - a1), axis=1, keepdims=True
            )
            a1, a2 = update(jax.nn.sigmoid(0.125 * far))
        a1, a2 = a1 * alive, a2 * alive
        centers_ref[s, 0:1, :] = a1
        centers_ref[s, 1:2, :] = a2
        c1 = jnp.sum(head * a1, axis=1, keepdims=True)
        c2 = jnp.sum(head * a2, axis=1, keepdims=True)
        for t in range(2):
            where_to = one_hot((ndest == to) & (nplace == t) & (nsplit == s))
            table = dot_nt(where_to, picks).astype(BF)
            values = jnp.where(lane == 32 + 2 * t, c1, jnp.where(lane == 33 + 2 * t, c2, 0.0))
            sent = sent + dot(table, values.astype(BF))
    send_ref[...] = jnp.where(iota((NC, 128), 1) < V, best_ref[...], sent)


BLOCK = 1024


def scan_blocks(ref, part, best):
    for i in range(2048 // BLOCK):
        scores = dot_nt(ref[BLOCK * i : BLOCK * i + BLOCK, :], part)
        best = jnp.maximum(best, jnp.max(scores.reshape(BLOCK // 8, 8, NC * 4), axis=0))
    return best


def returned(place_ref, accs, best):
    x, core = place_ref[0], place_ref[1]
    wide = (NC, NC * 4)
    mine = iota(wide, 1) // 4 == iota(wide, 0)
    lane = iota((NC, 128), 1)
    for a, acc in accs:
        top = jnp.max(acc, axis=0, keepdims=True)
        spread = jnp.where(mine, jnp.broadcast_to(top, wide), LOW)
        folded = jnp.maximum(spread[:, :128], spread[:, 128:])
        for shift in (64, 32, 16, 8, 4):
            folded = jnp.maximum(folded, pltpu.roll(folded, shift, 1))
        group = lax.rem(x + NX - a, NX) * NK + core
        best = jnp.where(lane // 4 == group, folded, best)
    return best


def first_kernel(
    place_ref, own_ref, mate_in, v_ref, v1_in, v2_in, best_ref, near_ref, mate_ref, acc_ref, part_ref, sems
):
    pairs = ((v1_in, part_ref.at[0]), (v2_in, part_ref.at[1]), (mate_in, mate_ref), (own_ref, near_ref))
    copies = [pltpu.make_async_copy(src, dst, sems.at[i]) for i, (src, dst) in enumerate(pairs)]
    for copy in copies:
        copy.start()
    blank = jnp.full((8, NC * 4), LOW, F32)
    acc_ref[0] = scan_blocks(own_ref, v_ref[...], blank)
    copies[0].wait()
    acc_ref[1] = scan_blocks(own_ref, part_ref[0], blank)
    copies[1].wait()
    acc_ref[2] = scan_blocks(own_ref, part_ref[1], blank)
    copies[2].wait()
    acc_ref[0] = scan_blocks(mate_ref, v_ref[...], acc_ref[0])
    acc_ref[1] = scan_blocks(mate_ref, part_ref[0], acc_ref[1])
    acc_ref[2] = scan_blocks(mate_ref, part_ref[1], acc_ref[2])
    blank = jnp.full((NC, 128), LOW, F32)
    best_ref[...] = returned(place_ref, ((0, acc_ref[0]), (1, acc_ref[1]), (3, acc_ref[2])), blank)
    copies[3].wait()


def best_kernel(
    place_ref, own_ref, mate_ref, v_in, some_ref, post_ref, out_ref, prior_ref, part_ref, sems
):
    fetch([(v_in, part_ref)], sems)
    prior_ref[...] = own_ref[:16, :]
    best = scan_blocks(own_ref, part_ref[...], jnp.full((8, NC * 4), LOW, F32))
    best = scan_blocks(mate_ref, part_ref[...], best)
    out_ref[...] = returned(place_ref, ((2, best),), some_ref[...])


def final_kernel(in_ref, table_ref, best_ref, score_ref):
    got = in_ref[...]
    lane = iota((NC, 128), 1)
    src = iota((NC, 128), 0)
    n = NZ * NK
    pair = jnp.maximum(
        jnp.maximum(got[:n], got[n : 2 * n]), jnp.maximum(got[2 * n : 3 * n], got[3 * n :])
    )
    tops = jnp.concatenate(
        [
            jnp.broadcast_to(jnp.max(pair[NK * z : NK * z + NK], axis=0, keepdims=True), (16, 128))
            for z in range(NZ)
        ],
        axis=0,
    )
    p = iota((128, 128), 0)
    best = jnp.full((1, V), LOW, F32)
    for x in range(NX):
        slot = (x * NK + (p // 8) % NK) * 4 + p % 4
        value = jnp.max(jnp.where(iota((128, 128), 1) == slot, tops, LOW), axis=1, keepdims=True)
        table = table_ref[128 * x : 128 * x + 128, :V].astype(F32)
        best = jnp.maximum(best, jnp.max(jnp.where(table > 0.5, value, LOW), axis=0, keepdims=True))
    best_ref[...] = best
    vals = jnp.where((lane >= 32) & (lane < 36), got, 0.0).astype(BF)
    total = jnp.zeros((8, 128), F32)
    pick = iota((8, 128), 0)
    at = iota((8, 128), 1)
    for t in range(2):
        chosen = one_hot(at == 32 + 2 * t + pick)
        rows = dot_nt(chosen, vals).astype(BF)
        total = total + dot(rows, one_hot(lane == src * 2 + t))
    score_ref[...] = total[:2].astype(BF)


def vm():
    return pl.BlockSpec(memory_space=pltpu.VMEM)


def sm():
    return pl.BlockSpec(memory_space=pltpu.SMEM)


def params(mib=28):
    return pltpu.CompilerParams(vmem_limit_bytes=mib * MIB)


def shards(
    vectors,
    centroids,
    postings,
    fill,
    assign,
    split_posts,
    split_members,
    neigh_post,
    neigh_row,
    neigh_split,
    neigh_dest,
):
    place = jnp.stack([lax.axis_index("x"), lax.axis_index("core")]).astype(I32)
    npost, nrow, nsplit, ndest = (
        a.reshape(1, NB) for a in (neigh_post, neigh_row, neigh_split, neigh_dest)
    )
    one = lambda *shape: pl.BlockSpec(shape, lambda i: (0,) * len(shape))
    hbm = pl.BlockSpec(memory_space=pl.ANY)
    packed, table = pl.pallas_call(
        pack_kernel,
        out_shape=(
            jax.ShapeDtypeStruct((NC * 8, P8), BF),
            jax.ShapeDtypeStruct((NC * 8, 128), BF),
        ),
        in_specs=[hbm] * 6,
        out_specs=(hbm, vm()),
        scratch_shapes=[
            pltpu.VMEM((V, D), BF), pltpu.VMEM((POSTS, HEAD, D), BF), pltpu.VMEM((1, V), I32),
            pltpu.VMEM((1, NB), I32), pltpu.VMEM((1, NB), I32), pltpu.VMEM((1, NB), I32),
            pltpu.VMEM((NC * 8, P8), BF), pltpu.SemaphoreType.DMA((8,)),
        ],
        compiler_params=params(60),
        name="pack_rows",
    )(vectors, postings, assign.reshape(1, V), npost, nrow, ndest)
    held, packed = lax.optimization_barrier((centroids, packed))
    mate = lax.ppermute(held, "core", [(0, 1), (1, 0)])
    got = lax.all_to_all(packed.reshape(NC, 8, P8), CENT, 0, 0, tiled=True).reshape(NC * 8, P8)
    share = pl.pallas_call(
        share_kernel,
        out_shape=jax.ShapeDtypeStruct((NC * 4, D), BF),
        in_specs=[vm()],
        out_specs=vm(),
        compiler_params=params(),
        cost_estimate=pl.CostEstimate(flops=2 * 10**10, bytes_accessed=0, transcendentals=0),
        name="share_rows",
    )(got)
    parts = {a: lax.ppermute(share, "x", [(i, (i + a) % NX) for i in range(NX)]) for a in (2, 1, 3)}
    spread = pl.pallas_call(
        spread_kernel,
        out_shape=jax.ShapeDtypeStruct((NY, V, W), BF),
        in_specs=[vm(), vm()],
        out_specs=pl.BlockSpec(memory_space=pltpu.HBM),
        scratch_shapes=[pltpu.VMEM((V, W), BF), pltpu.SemaphoreType.DMA((NY,))],
        compiler_params=params(),
        cost_estimate=pl.CostEstimate(flops=2 * 10**10, bytes_accessed=0, transcendentals=0),
        name="spread_rows",
    )(got, share)
    gathered = lax.all_to_all(spread, "y", 0, 0, tiled=True).reshape(NY * V, W)
    moved_rows = pl.pallas_call(
        moved_kernel,
        out_shape=jax.ShapeDtypeStruct((NC * 2, D), BF),
        in_specs=[vm()],
        out_specs=vm(),
        compiler_params=params(),
        name="moved_rows",
    )(got)

    def cost(count):
        work = 2 * 4096 * 256 * D * count
        return pl.CostEstimate(flops=work, bytes_accessed=2 * 4096 * D, transcendentals=0)

    first, near, mate = pl.pallas_call(
        first_kernel,
        out_shape=(
            jax.ShapeDtypeStruct((NC, 128), F32),
            jax.ShapeDtypeStruct((2048, D), BF),
            jax.ShapeDtypeStruct((2048, D), BF),
        ),
        in_specs=[sm(), vm(), hbm, vm(), hbm, hbm],
        out_specs=(vm(), vm(), vm()),
        scratch_shapes=[
            pltpu.VMEM((NX - 1, 8, NC * 4), F32),
            pltpu.VMEM((2, NC * 4, D), BF),
            pltpu.SemaphoreType.DMA((4,)),
        ],
        compiler_params=params(),
        cost_estimate=cost(3),
        name="best_of_three",
    )(place, centroids, mate, share, parts[1], parts[3])
    best, priors = pl.pallas_call(
        best_kernel,
        out_shape=(jax.ShapeDtypeStruct((NC, 128), F32), jax.ShapeDtypeStruct((16, D), BF)),
        in_specs=[sm(), vm(), vm(), hbm, vm(), vm()],
        out_specs=(vm(), vm()),
        scratch_shapes=[pltpu.VMEM((NC * 4, D), BF), pltpu.SemaphoreType.DMA((1,))],
        compiler_params=params(),
        cost_estimate=cost(1),
        name="best_scores",
    )(place, near, mate, parts[2], first, postings)
    split_centers, sending = pl.pallas_call(
        split_kernel,
        out_shape=(
            jax.ShapeDtypeStruct((2, 2, D), F32),
            jax.ShapeDtypeStruct((NC, 128), F32),
        ),
        in_specs=[sm(), sm()] + [vm()] * 9,
        out_specs=(vm(), vm()),
        compiler_params=params(),
        name="split_scores",
    )(
        fill, split_posts, gathered, split_members, npost, nrow, nsplit, ndest, postings, priors, best
    )
    postings_out, new_fill = pl.pallas_call(
        append_kernel,
        out_shape=(
            jax.ShapeDtypeStruct((POSTS, ROWS, D), BF),
            jax.ShapeDtypeStruct((POSTS,), I32),
        ),
        in_specs=[sm(), vm(), vm()],
        out_specs=(vm(), sm()),
        compiler_params=params(),
        name="append_rows",
    )(fill, gathered, postings)
    back = lax.all_to_all(sending.reshape(NC, 1, 128), CENT, 0, 0, tiled=True).reshape(NC, 128)
    best_score, moved_scores = pl.pallas_call(
        final_kernel,
        out_shape=(jax.ShapeDtypeStruct((1, V), F32), jax.ShapeDtypeStruct((2, 2 * NC), BF)),
        in_specs=[vm(), vm()],
        out_specs=(vm(), vm()),
        compiler_params=params(),
        name="last_step",
    )(back, table)
    return (
        best_score.reshape(V), postings_out, new_fill, split_centers, moved_rows, moved_scores
    )


def solution(mesh):
    fine = Mesh(mesh.devices.reshape(NY, NX, NZ, NK), ("y", "x", "z", "core"))
    both = ("y",) + CENT
    return jax.shard_map(
        shards,
        mesh=fine,
        in_specs=(
            P(both, None),
            P(CENT, None),
            P(CENT, None, None),
            P(CENT),
            P(both),
            P(CENT),
            P(CENT, None),
            P(both),
            P(both),
            P(both),
            P(both),
        ),
        out_specs=(
            P(both),
            P(CENT, None, None),
            P(CENT),
            P(CENT, None, None),
            P(both, None),
            P(None, both),
        ),
        check_vma=False,
    )
```

```python
import functools

import jax
import jax.numpy as jnp
from jax import lax
from jax.experimental import pallas as pl
from jax.experimental.pallas import tpu as pltpu
from jax.sharding import Mesh, PartitionSpec as P

D = 768
W = 896
ROWS = 128
HEAD = 32
ITERS = 2
NX, NY, NZ, NK = 4, 8, 8, 2
NC = NX * NZ * NK
V = 32
NB = 64
POSTS = 4
CENT = ("x", "z", "core")
LOW = -3.0e38
HALF = D // 2
P8 = HALF + 256
F32 = jnp.float32
BF = jnp.bfloat16
I32 = jnp.int32
MIB = 1024 * 1024


def iota(shape, dim):
    return lax.broadcasted_iota(I32, shape, dim)


def as_column(row):
    n = row.shape[1]
    eye = iota((n, n), 0) == iota((n, n), 1)
    return jnp.sum(jnp.where(eye, jnp.broadcast_to(row, (n, n)), 0), axis=1, keepdims=True)


def earlier_equal(row):
    n = row.shape[1]
    same = (as_column(row) == row) & (iota((n, n), 0) < iota((n, n), 1))
    return jnp.sum(same.astype(I32), axis=0, keepdims=True)


def one_hot(mask):
    return jnp.where(mask, 1.0, 0.0).astype(BF)


def dot(a, b):
    return jnp.dot(a, b, preferred_element_type=F32)


def dot_nt(a, b):
    return lax.dot_general(a, b, (((1,), (1,)), ((), ())), preferred_element_type=F32)


def fetch(pairs, sems):
    copies = [pltpu.make_async_copy(src, dst, sems.at[i]) for i, (src, dst) in enumerate(pairs)]
    for copy in copies:
        copy.start()
    for copy in copies:
        copy.wait()


def pack_kernel(vec_ref, head_ref, assign_ref, npost_ref, nrow_ref, ndest_ref, out_ref, table_ref):
    n = NC * 8
    assign = assign_ref[...]
    dest = assign >> 2
    zdest = (dest >> 1) & 7
    place = earlier_equal(dest)

    ones = jnp.ones((V, 128), BF)

    def routed(count, per):
        p = iota((count, V), 0)
        to, t = p >> (3 if per == 8 else 2), p & 3
        return (dest == to) & (place == t), (zdest != ((to >> 1) & 7))

    named, other = routed(n, 8)
    small, _ = routed(NC * 4, 4)
    free = (1.0 - dot(one_hot(small), ones)).astype(BF)
    p, c = iota((n, NC * 4), 0), iota((n, NC * 4), 1)
    pd, cd = p >> 3, c >> 2
    slot = ((pd >> 4) * NK + (pd & 1)) * 4 + (p & 3)
    cslot = ((cd >> 4) * NK + (cd & 1)) * 4 + (c & 3)
    before = one_hot((((pd >> 1) & 7) == ((cd >> 1) & 7)) & (cslot < slot))
    free_rank = dot(before, free)[:, :V]
    upper = one_hot(iota((V, V), 0) < iota((V, V), 1))
    rest_rank = dot(one_hot(other), upper)
    taken = dot(one_hot(named), ones)[:, :V]
    share = named | (other & (taken < 0.5) & (free_rank == rest_rank))
    low_half = (iota((n, V), 0) & 7) < 4
    table = one_hot(share & low_half)
    table_ref[:, :V] = table
    out_ref[:, :HALF] = (
        dot(table, vec_ref[:, :HALF]) + dot(one_hot(share & ~low_half), vec_ref[:, HALF:])
    ).astype(BF)

    ndest = ndest_ref[...]
    nplace = earlier_equal(ndest)
    picks = one_hot(npost_ref[...] * HEAD + nrow_ref[...] == iota((POSTS * HEAD, NB), 0))
    head = head_ref[...].reshape(POSTS * HEAD, D)
    p, c = iota((n, 6 * NC), 0), iota((n, 6 * NC), 1)
    spread = one_hot(((p >> 3) == (c & 63)) & ((p & 7) == (c >> 6)))
    post = (as_column(assign) & 3) + 1
    mark = jnp.where(iota((V, 128), 1) == as_column(place), post, 0).astype(F32).astype(BF)
    sixth = one_hot(((iota((n, V), 0) >> 3) == dest) & ((iota((n, V), 0) & 7) == 6))
    for t in range(2):
        chosen = one_hot((ndest == iota((NC, NB), 0)) & (nplace == t))
        rows = dot(dot_nt(chosen, picks).astype(BF), head).astype(BF)
        stack = jnp.concatenate([rows[:, 128 * k : 128 * k + 128] for k in range(6)], axis=0)
        tile = dot(spread, stack)
        if t == 0:
            tile = tile + dot(sixth, mark)
        out_ref[:, HALF + 128 * t : HALF + 128 * t + 128] = tile.astype(BF)


def share_kernel(in_ref, share_ref):
    n = NC * 8
    p, i = iota((NC * 4, n), 1), iota((NC * 4, n), 0)
    first = (i >> 2) * 8 + (i & 3)
    rows = in_ref[:, :HALF]
    share_ref[:, :HALF] = dot(one_hot(p == first), rows).astype(BF)
    share_ref[:, HALF:] = dot(one_hot(p == first + 4), rows).astype(BF)


def moved_kernel(in_ref, moved_ref):
    n = NC * 8
    tiles = in_ref[:, HALF:]
    p, i = iota((NC * 2, n), 1), iota((NC * 2, n), 0)
    odd = (iota((NC * 2, 128), 0) & 1) == 1
    for k in range(6):
        both = dot(one_hot(p == (i >> 1) * 8 + k), tiles)
        moved_ref[:, 128 * k : 128 * k + 128] = jnp.where(odd, both[:, 128:], both[:, :128]).astype(BF)


def spread_kernel(in_ref, share_ref, out_ref, buf_ref, sems):
    n = NC * 8
    p, d = iota((NC, n), 1), iota((NC, n), 0)
    marks = dot(one_hot(p == d * 8 + 6), in_ref[:, HALF : HALF + 128]).astype(BF)
    first = dot_nt(one_hot(iota((8, 128), 1) == 0), marks)
    upper = one_hot(iota((NC, NC), 0) < iota((NC, NC), 1))
    valid = one_hot(first > 0.5)
    rank = dot(valid, upper).astype(BF)
    m = NC * 4
    widen = one_hot(iota((NC, m), 0) == iota((NC, m), 1) >> 2)
    valid, rank = dot(valid, widen)[:1], dot(rank, widen)[:1].astype(I32)
    t = iota((V, m), 1) & 3
    hit = one_hot((valid > 0.5) & (t < 2) & (2 * rank + t == iota((V, m), 0)))
    tall = one_hot(iota((m, NC), 1) == iota((m, NC), 0) >> 2)
    lane = iota((m, 128), 1)
    mine = jnp.where(lane == (iota((m, 128), 0) & 3), dot(tall, marks), 0.0)
    post = jnp.sum(mine, axis=1, keepdims=True)
    buf_ref[:, :D] = dot(hit, share_ref[...]).astype(BF)
    buf_ref[:, D:] = dot(hit, jnp.where(lane == 0, post, 0.0).astype(BF)).astype(BF)
    copies = [pltpu.make_async_copy(buf_ref, out_ref.at[g], sems.at[g]) for g in range(NY)]
    for copy in copies:
        copy.start()
    for copy in copies:
        copy.wait()


def ranks(got, posts):
    n = NY * V
    mark = dot_nt(one_hot(iota((8, 128), 1) == 0), got).astype(I32)
    row = iota((8, n), 0)
    wanted = jnp.zeros((8, n), I32)
    for i, q in enumerate(posts):
        wanted = jnp.where(row == i, q + 1, wanted)
    match = mark == wanted
    upper = one_hot(iota((n, n), 0) < iota((n, n), 1))
    return match, dot(one_hot(match), upper).astype(I32)


def appended(match, rank, i, first, got, before):
    mine = match[i : i + 1]
    count = jnp.sum(mine.astype(I32))
    table = one_hot(mine & (iota((ROWS, NY * V), 0) == first + rank[i : i + 1]))
    line = iota((ROWS, 1), 0)
    hit = (line >= first) & (line < first + count)
    return jnp.where(hit, dot(table, got), before), first + count


def append_kernel(fill_ref, got_ref, post_ref, out_ref, count_ref):
    match, rank = ranks(got_ref[:, D:], range(POSTS))
    for q in range(POSTS):
        rows, count = appended(
            match, rank, q, fill_ref[q], got_ref[:, :D], post_ref[q].astype(F32)
        )
        out_ref[q] = rows.astype(BF)
        count_ref[q] = count


def split_kernel(
    fill_ref, split_ref, got_ref, member_ref, npost_ref, nrow_ref, nsplit_ref, ndest_ref, post_ref, own_ref,
    best_ref, centers_ref, send_ref,
):
    line = iota((ROWS, 1), 0)
    head = post_ref[:, :HEAD, :].reshape(POSTS * HEAD, D).astype(F32)
    members = member_ref[...].astype(F32)
    eye = iota((ROWS, ROWS), 0) == iota((ROWS, ROWS), 1)
    lane = iota((POSTS * HEAD, 128), 1)
    ndest = ndest_ref[...]
    nplace = earlier_equal(ndest)
    nsplit = nsplit_ref[...]
    picks = one_hot(npost_ref[...] * HEAD + nrow_ref[...] == iota((POSTS * HEAD, NB), 0))
    to = iota((NC, NB), 0)
    own = own_ref[:16, :].astype(F32)
    posts = [jnp.maximum(split_ref[s], 0) for s in range(2)]
    match, rank = ranks(got_ref[:, D:], posts)
    sent = jnp.zeros((NC, 128), F32)
    for s in range(2):
        q = posts[s]
        alive = jnp.where(split_ref[s] >= 0, 1.0, 0.0).astype(F32)
        x, filled = appended(match, rank, s, fill_ref[q], got_ref[:, :D], post_ref[q].astype(F32))
        prior = jnp.sum(jnp.where(iota(own.shape, 0) == q, own, 0.0), axis=0, keepdims=True)
        mask = jnp.where(line < filled, 1.0, 0.0).astype(F32)
        weights = jnp.sum(jnp.where(eye, members[s : s + 1], 0.0), axis=1, keepdims=True)

        def update(weights):
            w1, w2 = mask * weights, mask * (1.0 - weights)
            s1 = jnp.sum(w1 * x, axis=0, keepdims=True) + prior
            s2 = jnp.sum(w2 * x, axis=0, keepdims=True) + prior
            t1 = jnp.sum(w1, axis=0, keepdims=True) + 1.0
            t2 = jnp.sum(w2, axis=0, keepdims=True) + 1.0
            return s1 / t1, s2 / t2

        a1, a2 = update(weights)
        for _ in range(ITERS):
            far = jnp.sum(jnp.square(x - a2), axis=1, keepdims=True) - jnp.sum(
                jnp.square(x - a1), axis=1, keepdims=True
            )
            a1, a2 = update(jax.nn.sigmoid(0.125 * far))
        a1, a2 = a1 * alive, a2 * alive
        centers_ref[s, 0:1, :] = a1
        centers_ref[s, 1:2, :] = a2
        c1 = jnp.sum(head * a1, axis=1, keepdims=True)
        c2 = jnp.sum(head * a2, axis=1, keepdims=True)
        for t in range(2):
            where_to = one_hot((ndest == to) & (nplace == t) & (nsplit == s))
            table = dot_nt(where_to, picks).astype(BF)
            values = jnp.where(lane == 32 + 2 * t, c1, jnp.where(lane == 33 + 2 * t, c2, 0.0))
            sent = sent + dot(table, values.astype(BF))
    send_ref[...] = jnp.where(iota((NC, 128), 1) < V, best_ref[...], sent)


BLOCK = 1024


def scan_blocks(ref, part, best):
    for i in range(2048 // BLOCK):
        scores = dot_nt(ref[BLOCK * i : BLOCK * i + BLOCK, :], part)
        best = jnp.maximum(best, jnp.max(scores.reshape(BLOCK // 8, 8, NC * 4), axis=0))
    return best


def first_kernel(own_ref, mate_in, v_ref, v1_in, v2_in, acc_ref, near_ref, mate_ref, part_ref, sems):
    pairs = ((v1_in, part_ref.at[0]), (v2_in, part_ref.at[1]), (mate_in, mate_ref), (own_ref, near_ref))
    copies = [pltpu.make_async_copy(src, dst, sems.at[i]) for i, (src, dst) in enumerate(pairs)]
    for copy in copies:
        copy.start()
    blank = jnp.full((8, NC * 4), LOW, F32)
    acc_ref[0] = scan_blocks(own_ref, v_ref[...], blank)
    copies[0].wait()
    acc_ref[1] = scan_blocks(own_ref, part_ref[0], blank)
    copies[1].wait()
    acc_ref[2] = scan_blocks(own_ref, part_ref[1], blank)
    copies[2].wait()
    acc_ref[0] = scan_blocks(mate_ref, v_ref[...], acc_ref[0])
    acc_ref[1] = scan_blocks(mate_ref, part_ref[0], acc_ref[1])
    acc_ref[2] = scan_blocks(mate_ref, part_ref[1], acc_ref[2])
    copies[3].wait()


def best_kernel(
    place_ref, own_ref, mate_ref, v_in, acc_ref, post_ref, out_ref, prior_ref, part_ref, sems
):
    fetch([(v_in, part_ref)], sems)
    prior_ref[...] = own_ref[:16, :]
    best = scan_blocks(own_ref, part_ref[...], jnp.full((8, NC * 4), LOW, F32))
    accs = [acc_ref[0], acc_ref[1], scan_blocks(mate_ref, part_ref[...], best), acc_ref[2]]
    x, core = place_ref[0], place_ref[1]
    wide = (NC, NC * 4)
    mine = (iota(wide, 1) >> 2) == iota(wide, 0)
    lane = iota((NC, 128), 1)
    best = jnp.full((NC, 128), LOW, F32)
    for a in range(NX):
        top = jnp.max(accs[a], axis=0, keepdims=True)
        spread = jnp.where(mine, jnp.broadcast_to(top, wide), LOW)
        folded = jnp.maximum(spread[:, :128], spread[:, 128:])
        for shift in (64, 32, 16, 8, 4):
            folded = jnp.maximum(folded, pltpu.roll(folded, shift, 1))
        group = lax.rem(x + NX - a, NX) * NK + core
        best = jnp.where((lane >> 2) == group, folded, best)
    out_ref[...] = best


def final_kernel(in_ref, table_ref, best_ref, score_ref):
    got = in_ref[...]
    lane = iota((NC, 128), 1)
    src = iota((NC, 128), 0)
    n = NZ * NK
    pair = jnp.maximum(
        jnp.maximum(got[:n], got[n : 2 * n]), jnp.maximum(got[2 * n : 3 * n], got[3 * n :])
    )
    tops = jnp.concatenate(
        [
            jnp.broadcast_to(jnp.max(pair[NK * z : NK * z + NK], axis=0, keepdims=True), (16, 128))
            for z in range(NZ)
        ],
        axis=0,
    )
    p = iota((128, 128), 0)
    best = jnp.full((1, V), LOW, F32)
    for x in range(NX):
        slot = (x * NK + ((p >> 3) & 1)) * 4 + (p & 3)
        value = jnp.max(jnp.where(iota((128, 128), 1) == slot, tops, LOW), axis=1, keepdims=True)
        table = table_ref[128 * x : 128 * x + 128, :V].astype(F32)
        best = jnp.maximum(best, jnp.max(jnp.where(table > 0.5, value, LOW), axis=0, keepdims=True))
    best_ref[...] = best
    vals = jnp.where((lane >= 32) & (lane < 36), got, 0.0).astype(BF)
    total = jnp.zeros((8, 128), F32)
    pick = iota((8, 128), 0)
    at = iota((8, 128), 1)
    for t in range(2):
        chosen = one_hot(at == 32 + 2 * t + pick)
        rows = dot_nt(chosen, vals).astype(BF)
        total = total + dot(rows, one_hot(lane == src * 2 + t))
    score_ref[...] = total[:2].astype(BF)


def vm():
    return pl.BlockSpec(memory_space=pltpu.VMEM)


def sm():
    return pl.BlockSpec(memory_space=pltpu.SMEM)


def params(mib=28):
    return pltpu.CompilerParams(vmem_limit_bytes=mib * MIB)


def shards(
    vectors,
    centroids,
    postings,
    fill,
    assign,
    split_posts,
    split_members,
    neigh_post,
    neigh_row,
    neigh_split,
    neigh_dest,
):
    place = jnp.stack([lax.axis_index("x"), lax.axis_index("core")]).astype(I32)
    npost, nrow, nsplit, ndest = (
        a.reshape(1, NB) for a in (neigh_post, neigh_row, neigh_split, neigh_dest)
    )
    one = lambda *shape: pl.BlockSpec(shape, lambda i: (0,) * len(shape))
    hbm = pl.BlockSpec(memory_space=pl.ANY)
    packed, table = pl.pallas_call(
        pack_kernel,
        out_shape=(
            jax.ShapeDtypeStruct((NC * 8, P8), BF),
            jax.ShapeDtypeStruct((NC * 8, 128), BF),
        ),
        grid=(1,),
        in_specs=[one(V, D), one(POSTS, HEAD, D), one(1, V), one(1, NB), one(1, NB), one(1, NB)],
        out_specs=(one(NC * 8, P8), one(NC * 8, 128)),
        compiler_params=params(60),
        name="pack_rows",
    )(vectors, postings, assign.reshape(1, V), npost, nrow, ndest)
    held, packed = lax.optimization_barrier((centroids, packed))
    mate = lax.ppermute(held, "core", [(0, 1), (1, 0)])
    got = lax.all_to_all(packed.reshape(NC, 8, P8), CENT, 0, 0, tiled=True).reshape(NC * 8, P8)
    share = pl.pallas_call(
        share_kernel,
        out_shape=jax.ShapeDtypeStruct((NC * 4, D), BF),
        in_specs=[vm()],
        out_specs=vm(),
        compiler_params=params(),
        cost_estimate=pl.CostEstimate(flops=2 * 10**10, bytes_accessed=0, transcendentals=0),
        name="share_rows",
    )(got)
    parts = {a: lax.ppermute(share, "x", [(i, (i + a) % NX) for i in range(NX)]) for a in (2, 1, 3)}
    spread = pl.pallas_call(
        spread_kernel,
        out_shape=jax.ShapeDtypeStruct((NY, V, W), BF),
        in_specs=[vm(), vm()],
        out_specs=pl.BlockSpec(memory_space=pltpu.HBM),
        scratch_shapes=[pltpu.VMEM((V, W), BF), pltpu.SemaphoreType.DMA((NY,))],
        compiler_params=params(),
        cost_estimate=pl.CostEstimate(flops=2 * 10**10, bytes_accessed=0, transcendentals=0),
        name="spread_rows",
    )(got, share)
    gathered = lax.all_to_all(spread, "y", 0, 0, tiled=True).reshape(NY * V, W)
    moved_rows = pl.pallas_call(
        moved_kernel,
        out_shape=jax.ShapeDtypeStruct((NC * 2, D), BF),
        in_specs=[vm()],
        out_specs=vm(),
        compiler_params=params(),
        name="moved_rows",
    )(got)

    def cost(count):
        work = 2 * 4096 * 256 * D * count
        return pl.CostEstimate(flops=work, bytes_accessed=2 * 4096 * D, transcendentals=0)

    first, near, mate = pl.pallas_call(
        first_kernel,
        out_shape=(
            jax.ShapeDtypeStruct((NX - 1, 8, NC * 4), F32),
            jax.ShapeDtypeStruct((2048, D), BF),
            jax.ShapeDtypeStruct((2048, D), BF),
        ),
        in_specs=[vm(), hbm, vm(), hbm, hbm],
        out_specs=(vm(), vm(), vm()),
        scratch_shapes=[pltpu.VMEM((2, NC * 4, D), BF), pltpu.SemaphoreType.DMA((4,))],
        compiler_params=params(),
        cost_estimate=cost(3),
        name="best_of_three",
    )(centroids, mate, share, parts[1], parts[3])
    best, priors = pl.pallas_call(
        best_kernel,
        out_shape=(jax.ShapeDtypeStruct((NC, 128), F32), jax.ShapeDtypeStruct((16, D), BF)),
        in_specs=[sm(), vm(), vm(), hbm, vm(), vm()],
        out_specs=(vm(), vm()),
        scratch_shapes=[pltpu.VMEM((NC * 4, D), BF), pltpu.SemaphoreType.DMA((1,))],
        compiler_params=params(),
        cost_estimate=cost(1),
        name="best_scores",
    )(place, near, mate, parts[2], first, postings)
    split_centers, sending = pl.pallas_call(
        split_kernel,
        out_shape=(
            jax.ShapeDtypeStruct((2, 2, D), F32),
            jax.ShapeDtypeStruct((NC, 128), F32),
        ),
        in_specs=[sm(), sm()] + [vm()] * 9,
        out_specs=(vm(), vm()),
        compiler_params=params(),
        name="split_scores",
    )(
        fill, split_posts, gathered, split_members, npost, nrow, nsplit, ndest, postings, priors, best
    )
    postings_out, new_fill = pl.pallas_call(
        append_kernel,
        out_shape=(
            jax.ShapeDtypeStruct((POSTS, ROWS, D), BF),
            jax.ShapeDtypeStruct((POSTS,), I32),
        ),
        in_specs=[sm(), vm(), vm()],
        out_specs=(vm(), sm()),
        compiler_params=params(),
        name="append_rows",
    )(fill, gathered, postings)
    back = lax.all_to_all(sending.reshape(NC, 1, 128), CENT, 0, 0, tiled=True).reshape(NC, 128)
    best_score, moved_scores = pl.pallas_call(
        final_kernel,
        out_shape=(jax.ShapeDtypeStruct((1, V), F32), jax.ShapeDtypeStruct((2, 2 * NC), BF)),
        in_specs=[vm(), vm()],
        out_specs=(vm(), vm()),
        compiler_params=params(),
        name="last_step",
    )(back, table)
    return (
        best_score.reshape(V), postings_out, new_fill, split_centers, moved_rows, moved_scores
    )


def solution(mesh):
    fine = Mesh(mesh.devices.reshape(NY, NX, NZ, NK), ("y", "x", "z", "core"))
    both = ("y",) + CENT
    return jax.shard_map(
        shards,
        mesh=fine,
        in_specs=(
            P(both, None),
            P(CENT, None),
            P(CENT, None, None),
            P(CENT),
            P(both),
            P(CENT),
            P(CENT, None),
            P(both),
            P(both),
            P(both),
            P(both),
        ),
        out_specs=(
            P(both),
            P(CENT, None, None),
            P(CENT),
            P(CENT, None, None),
            P(both, None),
            P(None, both),
        ),
        check_vma=False,
    )
```

```python
import functools

import jax
import jax.numpy as jnp
from jax import lax
from jax.experimental import pallas as pl
from jax.experimental.pallas import tpu as pltpu
from jax.sharding import Mesh, PartitionSpec as P

D = 768
W = 896
ROWS = 128
HEAD = 32
ITERS = 2
NX, NY, NZ, NK = 4, 8, 8, 2
NC = NX * NZ * NK
V = 32
NB = 64
POSTS = 4
CENT = ("x", "z", "core")
LOW = -3.0e38
HALF = D // 2
P8 = HALF + 256
F32 = jnp.float32
BF = jnp.bfloat16
I32 = jnp.int32
MIB = 1024 * 1024


def iota(shape, dim):
    return lax.broadcasted_iota(I32, shape, dim)


def as_column(row):
    n = row.shape[1]
    eye = iota((n, n), 0) == iota((n, n), 1)
    return jnp.sum(jnp.where(eye, jnp.broadcast_to(row, (n, n)), 0), axis=1, keepdims=True)


def earlier_equal(row):
    n = row.shape[1]
    same = (as_column(row) == row) & (iota((n, n), 0) < iota((n, n), 1))
    return jnp.sum(same.astype(I32), axis=0, keepdims=True)


def one_hot(mask):
    return jnp.where(mask, 1.0, 0.0).astype(BF)


def dot(a, b):
    return jnp.dot(a, b, preferred_element_type=F32)


def dot_nt(a, b):
    return lax.dot_general(a, b, (((1,), (1,)), ((), ())), preferred_element_type=F32)


def fetch(pairs, sems):
    copies = [pltpu.make_async_copy(src, dst, sems.at[i]) for i, (src, dst) in enumerate(pairs)]
    for copy in copies:
        copy.start()
    for copy in copies:
        copy.wait()


def pack_kernel(vec_ref, head_ref, assign_ref, npost_ref, nrow_ref, ndest_ref, out_ref, table_ref):
    n = NC * 8
    assign = assign_ref[...]
    dest = assign >> 2
    zdest = (dest >> 1) & 7
    place = earlier_equal(dest)

    ones = jnp.ones((V, 128), BF)

    def routed(count, per):
        p = iota((count, V), 0)
        to, t = p >> (3 if per == 8 else 2), p & 3
        return (dest == to) & (place == t), (zdest != ((to >> 1) & 7))

    named, other = routed(n, 8)
    small, _ = routed(NC * 4, 4)
    free = (1.0 - dot(one_hot(small), ones)).astype(BF)
    p, c = iota((n, NC * 4), 0), iota((n, NC * 4), 1)
    pd, cd = p >> 3, c >> 2
    slot = ((pd >> 4) * NK + (pd & 1)) * 4 + (p & 3)
    cslot = ((cd >> 4) * NK + (cd & 1)) * 4 + (c & 3)
    before = one_hot((((pd >> 1) & 7) == ((cd >> 1) & 7)) & (cslot < slot))
    free_rank = dot(before, free)[:, :V]
    upper = one_hot(iota((V, V), 0) < iota((V, V), 1))
    rest_rank = dot(one_hot(other), upper)
    taken = dot(one_hot(named), ones)[:, :V]
    share = named | (other & (taken < 0.5) & (free_rank == rest_rank))
    low_half = (iota((n, V), 0) & 7) < 4
    table = one_hot(share & low_half)
    table_ref[:, :V] = table
    out_ref[:, :HALF] = (
        dot(table, vec_ref[:, :HALF]) + dot(one_hot(share & ~low_half), vec_ref[:, HALF:])
    ).astype(BF)

    ndest = ndest_ref[...]
    nplace = earlier_equal(ndest)
    picks = one_hot(npost_ref[...] * HEAD + nrow_ref[...] == iota((POSTS * HEAD, NB), 0))
    head = head_ref[...].reshape(POSTS * HEAD, D)
    p, c = iota((n, 6 * NC), 0), iota((n, 6 * NC), 1)
    spread = one_hot(((p >> 3) == (c & 63)) & ((p & 7) == (c >> 6)))
    post = (as_column(assign) & 3) + 1
    mark = jnp.where(iota((V, 128), 1) == as_column(place), post, 0).astype(F32).astype(BF)
    sixth = one_hot(((iota((n, V), 0) >> 3) == dest) & ((iota((n, V), 0) & 7) == 6))
    i = iota((2 * NC, NB), 0)
    chosen = one_hot((ndest == (i & (NC - 1))) & (nplace == (i >> 6)))
    rows = dot(dot_nt(chosen, picks).astype(BF), head).astype(BF)
    stacks = [
        jnp.concatenate([rows[NC * t : NC * t + NC, 128 * k : 128 * k + 128] for k in range(6)], axis=0)
        for t in range(2)
    ]
    tiles = dot(spread, jnp.concatenate(stacks, axis=1))
    out_ref[:, HALF : HALF + 128] = (tiles[:, :128] + dot(sixth, mark)).astype(BF)
    out_ref[:, HALF + 128 :] = tiles[:, 128:].astype(BF)


def share_kernel(in_ref, share_ref):
    n = NC * 8
    p, i = iota((NC * 4, n), 1), iota((NC * 4, n), 0)
    first = (i >> 2) * 8 + (i & 3)
    rows = in_ref[:, :HALF]
    share_ref[:, :HALF] = dot(one_hot(p == first), rows).astype(BF)
    share_ref[:, HALF:] = dot(one_hot(p == first + 4), rows).astype(BF)


def moved_kernel(in_ref, moved_ref):
    n = NC * 8
    tiles = in_ref[:, HALF:]
    p, i = iota((NC * 2, n), 1), iota((NC * 2, n), 0)
    odd = (iota((NC * 2, 128), 0) & 1) == 1
    for k in range(6):
        both = dot(one_hot(p == (i >> 1) * 8 + k), tiles)
        moved_ref[:, 128 * k : 128 * k + 128] = jnp.where(odd, both[:, 128:], both[:, :128]).astype(BF)


def spread_kernel(in_ref, share_ref, out_ref, buf_ref, sems):
    n = NC * 8
    p, d = iota((NC, n), 1), iota((NC, n), 0)
    marks = dot(one_hot(p == d * 8 + 6), in_ref[:, HALF : HALF + 128]).astype(BF)
    first = dot_nt(one_hot(iota((8, 128), 1) == 0), marks)
    upper = one_hot(iota((NC, NC), 0) < iota((NC, NC), 1))
    valid = one_hot(first > 0.5)
    rank = dot(valid, upper).astype(BF)
    m = NC * 4
    widen = one_hot(iota((NC, m), 0) == iota((NC, m), 1) >> 2)
    valid, rank = dot(valid, widen)[:1], dot(rank, widen)[:1].astype(I32)
    t = iota((V, m), 1) & 3
    hit = one_hot((valid > 0.5) & (t < 2) & (2 * rank + t == iota((V, m), 0)))
    tall = one_hot(iota((m, NC), 1) == iota((m, NC), 0) >> 2)
    lane = iota((m, 128), 1)
    mine = jnp.where(lane == (iota((m, 128), 0) & 3), dot(tall, marks), 0.0)
    post = jnp.sum(mine, axis=1, keepdims=True)
    buf_ref[:, :D] = dot(hit, share_ref[...]).astype(BF)
    buf_ref[:, D:] = dot(hit, jnp.where(lane == 0, post, 0.0).astype(BF)).astype(BF)
    copies = [pltpu.make_async_copy(buf_ref, out_ref.at[g], sems.at[g]) for g in range(NY)]
    for copy in copies:
        copy.start()
    for copy in copies:
        copy.wait()


def ranks(got, posts):
    n = NY * V
    mark = dot_nt(one_hot(iota((8, 128), 1) == 0), got).astype(I32)
    row = iota((8, n), 0)
    wanted = jnp.zeros((8, n), I32)
    for i, q in enumerate(posts):
        wanted = jnp.where(row == i, q + 1, wanted)
    match = mark == wanted
    upper = one_hot(iota((n, n), 0) < iota((n, n), 1))
    return match, dot(one_hot(match), upper).astype(I32)


def appended(match, rank, i, first, got, before):
    mine = match[i : i + 1]
    count = jnp.sum(mine.astype(I32))
    table = one_hot(mine & (iota((ROWS, NY * V), 0) == first + rank[i : i + 1]))
    line = iota((ROWS, 1), 0)
    hit = (line >= first) & (line < first + count)
    return jnp.where(hit, dot(table, got), before), first + count


def append_kernel(fill_ref, got_ref, post_ref, out_ref, count_ref):
    match, rank = ranks(got_ref[:, D:], range(POSTS))
    for q in range(POSTS):
        rows, count = appended(
            match, rank, q, fill_ref[q], got_ref[:, :D], post_ref[q].astype(F32)
        )
        out_ref[q] = rows.astype(BF)
        count_ref[q] = count


def split_kernel(
    fill_ref, split_ref, got_ref, member_ref, npost_ref, nrow_ref, nsplit_ref, ndest_ref, post_ref, own_ref,
    best_ref, centers_ref, send_ref,
):
    line = iota((ROWS, 1), 0)
    head = post_ref[:, :HEAD, :].reshape(POSTS * HEAD, D).astype(F32)
    members = member_ref[...].astype(F32)
    eye = iota((ROWS, ROWS), 0) == iota((ROWS, ROWS), 1)
    lane = iota((POSTS * HEAD, 128), 1)
    ndest = ndest_ref[...]
    nplace = earlier_equal(ndest)
    nsplit = nsplit_ref[...]
    picks = one_hot(npost_ref[...] * HEAD + nrow_ref[...] == iota((POSTS * HEAD, NB), 0))
    to = iota((NC, NB), 0)
    own = own_ref[:16, :].astype(F32)
    posts = [jnp.maximum(split_ref[s], 0) for s in range(2)]
    match, rank = ranks(got_ref[:, D:], posts)
    sent = jnp.zeros((NC, 128), F32)
    for s in range(2):
        q = posts[s]
        alive = jnp.where(split_ref[s] >= 0, 1.0, 0.0).astype(F32)
        x, filled = appended(match, rank, s, fill_ref[q], got_ref[:, :D], post_ref[q].astype(F32))
        prior = jnp.sum(jnp.where(iota(own.shape, 0) == q, own, 0.0), axis=0, keepdims=True)
        mask = jnp.where(line < filled, 1.0, 0.0).astype(F32)
        weights = jnp.sum(jnp.where(eye, members[s : s + 1], 0.0), axis=1, keepdims=True)

        def update(weights):
            w1, w2 = mask * weights, mask * (1.0 - weights)
            s1 = jnp.sum(w1 * x, axis=0, keepdims=True) + prior
            s2 = jnp.sum(w2 * x, axis=0, keepdims=True) + prior
            t1 = jnp.sum(w1, axis=0, keepdims=True) + 1.0
            t2 = jnp.sum(w2, axis=0, keepdims=True) + 1.0
            return s1 / t1, s2 / t2

        a1, a2 = update(weights)
        for _ in range(ITERS):
            far = jnp.sum(jnp.square(x - a2), axis=1, keepdims=True) - jnp.sum(
                jnp.square(x - a1), axis=1, keepdims=True
            )
            a1, a2 = update(jax.nn.sigmoid(0.125 * far))
        a1, a2 = a1 * alive, a2 * alive
        centers_ref[s, 0:1, :] = a1
        centers_ref[s, 1:2, :] = a2
        c1 = jnp.sum(head * a1, axis=1, keepdims=True)
        c2 = jnp.sum(head * a2, axis=1, keepdims=True)
        for t in range(2):
            where_to = one_hot((ndest == to) & (nplace == t) & (nsplit == s))
            table = dot_nt(where_to, picks).astype(BF)
            values = jnp.where(lane == 32 + 2 * t, c1, jnp.where(lane == 33 + 2 * t, c2, 0.0))
            sent = sent + dot(table, values.astype(BF))
    send_ref[...] = jnp.where(iota((NC, 128), 1) < V, best_ref[...], sent)


BLOCK = 1024


def scan_blocks(ref, part, best):
    for i in range(2048 // BLOCK):
        scores = dot_nt(ref[BLOCK * i : BLOCK * i + BLOCK, :], part)
        best = jnp.maximum(best, jnp.max(scores.reshape(BLOCK // 8, 8, NC * 4), axis=0))
    return best


def first_kernel(own_ref, mate_in, v_ref, v1_in, v2_in, acc_ref, near_ref, mate_ref, part_ref, sems):
    pairs = ((v1_in, part_ref.at[0]), (v2_in, part_ref.at[1]), (mate_in, mate_ref), (own_ref, near_ref))
    copies = [pltpu.make_async_copy(src, dst, sems.at[i]) for i, (src, dst) in enumerate(pairs)]
    for copy in copies:
        copy.start()
    blank = jnp.full((8, NC * 4), LOW, F32)
    acc_ref[0] = scan_blocks(own_ref, v_ref[...], blank)
    copies[0].wait()
    acc_ref[1] = scan_blocks(own_ref, part_ref[0], blank)
    copies[1].wait()
    acc_ref[2] = scan_blocks(own_ref, part_ref[1], blank)
    copies[2].wait()
    acc_ref[0] = scan_blocks(mate_ref, v_ref[...], acc_ref[0])
    acc_ref[1] = scan_blocks(mate_ref, part_ref[0], acc_ref[1])
    acc_ref[2] = scan_blocks(mate_ref, part_ref[1], acc_ref[2])
    copies[3].wait()


def best_kernel(
    place_ref, own_ref, mate_ref, v_in, acc_ref, post_ref, out_ref, prior_ref, part_ref, sems
):
    fetch([(v_in, part_ref)], sems)
    prior_ref[...] = own_ref[:16, :]
    best = scan_blocks(own_ref, part_ref[...], jnp.full((8, NC * 4), LOW, F32))
    accs = [acc_ref[0], acc_ref[1], scan_blocks(mate_ref, part_ref[...], best), acc_ref[2]]
    x, core = place_ref[0], place_ref[1]
    wide = (NC, NC * 4)
    mine = (iota(wide, 1) >> 2) == iota(wide, 0)
    lane = iota((NC, 128), 1)
    best = jnp.full((NC, 128), LOW, F32)
    for a in range(NX):
        top = jnp.max(accs[a], axis=0, keepdims=True)
        spread = jnp.where(mine, jnp.broadcast_to(top, wide), LOW)
        folded = jnp.maximum(spread[:, :128], spread[:, 128:])
        for shift in (64, 32, 16, 8, 4):
            folded = jnp.maximum(folded, pltpu.roll(folded, shift, 1))
        group = lax.rem(x + NX - a, NX) * NK + core
        best = jnp.where((lane >> 2) == group, folded, best)
    out_ref[...] = best


def final_kernel(in_ref, table_ref, best_ref, score_ref):
    got = in_ref[...]
    lane = iota((NC, 128), 1)
    src = iota((NC, 128), 0)
    n = NZ * NK
    pair = jnp.maximum(
        jnp.maximum(got[:n], got[n : 2 * n]), jnp.maximum(got[2 * n : 3 * n], got[3 * n :])
    )
    tops = jnp.concatenate(
        [
            jnp.broadcast_to(jnp.max(pair[NK * z : NK * z + NK], axis=0, keepdims=True), (16, 128))
            for z in range(NZ)
        ],
        axis=0,
    )
    p = iota((128, 128), 0)
    best = jnp.full((1, V), LOW, F32)
    for x in range(NX):
        slot = (x * NK + ((p >> 3) & 1)) * 4 + (p & 3)
        value = jnp.max(jnp.where(iota((128, 128), 1) == slot, tops, LOW), axis=1, keepdims=True)
        table = table_ref[128 * x : 128 * x + 128, :V].astype(F32)
        best = jnp.maximum(best, jnp.max(jnp.where(table > 0.5, value, LOW), axis=0, keepdims=True))
    best_ref[...] = best
    vals = jnp.where((lane >= 32) & (lane < 36), got, 0.0).astype(BF)
    total = jnp.zeros((8, 128), F32)
    pick = iota((8, 128), 0)
    at = iota((8, 128), 1)
    for t in range(2):
        chosen = one_hot(at == 32 + 2 * t + pick)
        rows = dot_nt(chosen, vals).astype(BF)
        total = total + dot(rows, one_hot(lane == src * 2 + t))
    score_ref[...] = total[:2].astype(BF)


def vm():
    return pl.BlockSpec(memory_space=pltpu.VMEM)


def sm():
    return pl.BlockSpec(memory_space=pltpu.SMEM)


def params(mib=28):
    return pltpu.CompilerParams(vmem_limit_bytes=mib * MIB)


def shards(
    vectors,
    centroids,
    postings,
    fill,
    assign,
    split_posts,
    split_members,
    neigh_post,
    neigh_row,
    neigh_split,
    neigh_dest,
):
    place = jnp.stack([lax.axis_index("x"), lax.axis_index("core")]).astype(I32)
    npost, nrow, nsplit, ndest = (
        a.reshape(1, NB) for a in (neigh_post, neigh_row, neigh_split, neigh_dest)
    )
    one = lambda *shape: pl.BlockSpec(shape, lambda i: (0,) * len(shape))
    hbm = pl.BlockSpec(memory_space=pl.ANY)
    packed, table = pl.pallas_call(
        pack_kernel,
        out_shape=(
            jax.ShapeDtypeStruct((NC * 8, P8), BF),
            jax.ShapeDtypeStruct((NC * 8, 128), BF),
        ),
        grid=(1,),
        in_specs=[one(V, D), one(POSTS, HEAD, D), one(1, V), one(1, NB), one(1, NB), one(1, NB)],
        out_specs=(one(NC * 8, P8), one(NC * 8, 128)),
        compiler_params=params(60),
        name="pack_rows",
    )(vectors, postings, assign.reshape(1, V), npost, nrow, ndest)
    held, packed = lax.optimization_barrier((centroids, packed))
    mate = lax.ppermute(held, "core", [(0, 1), (1, 0)])
    got = lax.all_to_all(packed.reshape(NC, 8, P8), CENT, 0, 0, tiled=True).reshape(NC * 8, P8)
    share = pl.pallas_call(
        share_kernel,
        out_shape=jax.ShapeDtypeStruct((NC * 4, D), BF),
        in_specs=[vm()],
        out_specs=vm(),
        compiler_params=params(),
        cost_estimate=pl.CostEstimate(flops=2 * 10**10, bytes_accessed=0, transcendentals=0),
        name="share_rows",
    )(got)
    parts = {a: lax.ppermute(share, "x", [(i, (i + a) % NX) for i in range(NX)]) for a in (2, 1, 3)}
    spread = pl.pallas_call(
        spread_kernel,
        out_shape=jax.ShapeDtypeStruct((NY, V, W), BF),
        in_specs=[vm(), vm()],
        out_specs=pl.BlockSpec(memory_space=pltpu.HBM),
        scratch_shapes=[pltpu.VMEM((V, W), BF), pltpu.SemaphoreType.DMA((NY,))],
        compiler_params=params(),
        cost_estimate=pl.CostEstimate(flops=2 * 10**10, bytes_accessed=0, transcendentals=0),
        name="spread_rows",
    )(got, share)
    gathered = lax.all_to_all(spread, "y", 0, 0, tiled=True).reshape(NY * V, W)
    moved_rows = pl.pallas_call(
        moved_kernel,
        out_shape=jax.ShapeDtypeStruct((NC * 2, D), BF),
        in_specs=[vm()],
        out_specs=vm(),
        compiler_params=params(),
        name="moved_rows",
    )(got)

    def cost(count):
        work = 2 * 4096 * 256 * D * count
        return pl.CostEstimate(flops=work, bytes_accessed=2 * 4096 * D, transcendentals=0)

    first, near, mate = pl.pallas_call(
        first_kernel,
        out_shape=(
            jax.ShapeDtypeStruct((NX - 1, 8, NC * 4), F32),
            jax.ShapeDtypeStruct((2048, D), BF),
            jax.ShapeDtypeStruct((2048, D), BF),
        ),
        in_specs=[vm(), hbm, vm(), hbm, hbm],
        out_specs=(vm(), vm(), vm()),
        scratch_shapes=[pltpu.VMEM((2, NC * 4, D), BF), pltpu.SemaphoreType.DMA((4,))],
        compiler_params=params(),
        cost_estimate=cost(3),
        name="best_of_three",
    )(centroids, mate, share, parts[1], parts[3])
    best, priors = pl.pallas_call(
        best_kernel,
        out_shape=(jax.ShapeDtypeStruct((NC, 128), F32), jax.ShapeDtypeStruct((16, D), BF)),
        in_specs=[sm(), vm(), vm(), hbm, vm(), vm()],
        out_specs=(vm(), vm()),
        scratch_shapes=[pltpu.VMEM((NC * 4, D), BF), pltpu.SemaphoreType.DMA((1,))],
        compiler_params=params(),
        cost_estimate=cost(1),
        name="best_scores",
    )(place, near, mate, parts[2], first, postings)
    split_centers, sending = pl.pallas_call(
        split_kernel,
        out_shape=(
            jax.ShapeDtypeStruct((2, 2, D), F32),
            jax.ShapeDtypeStruct((NC, 128), F32),
        ),
        in_specs=[sm(), sm()] + [vm()] * 9,
        out_specs=(vm(), vm()),
        compiler_params=params(),
        name="split_scores",
    )(
        fill, split_posts, gathered, split_members, npost, nrow, nsplit, ndest, postings, priors, best
    )
    postings_out, new_fill = pl.pallas_call(
        append_kernel,
        out_shape=(
            jax.ShapeDtypeStruct((POSTS, ROWS, D), BF),
            jax.ShapeDtypeStruct((POSTS,), I32),
        ),
        in_specs=[sm(), vm(), vm()],
        out_specs=(vm(), sm()),
        compiler_params=params(),
        name="append_rows",
    )(fill, gathered, postings)
    back = lax.all_to_all(sending.reshape(NC, 1, 128), CENT, 0, 0, tiled=True).reshape(NC, 128)
    best_score, moved_scores = pl.pallas_call(
        final_kernel,
        out_shape=(jax.ShapeDtypeStruct((1, V), F32), jax.ShapeDtypeStruct((2, 2 * NC), BF)),
        in_specs=[vm(), vm()],
        out_specs=(vm(), vm()),
        compiler_params=params(),
        name="last_step",
    )(back, table)
    return (
        best_score.reshape(V), postings_out, new_fill, split_centers, moved_rows, moved_scores
    )


def solution(mesh):
    fine = Mesh(mesh.devices.reshape(NY, NX, NZ, NK), ("y", "x", "z", "core"))
    both = ("y",) + CENT
    return jax.shard_map(
        shards,
        mesh=fine,
        in_specs=(
            P(both, None),
            P(CENT, None),
            P(CENT, None, None),
            P(CENT),
            P(both),
            P(CENT),
            P(CENT, None),
            P(both),
            P(both),
            P(both),
            P(both),
        ),
        out_specs=(
            P(both),
            P(CENT, None, None),
            P(CENT),
            P(CENT, None, None),
            P(both, None),
            P(None, both),
        ),
        check_vma=False,
    )
```
